32 devices in a mesh: dp: 4 (over z), node: 8 (over y, x, core).
Axes of the slice: x: 2, y: 2, z: 4, core: 2. Of those that a mesh axis runs over, the one named last changes fastest.
Arguments:
- node_state: bfloat16 [4, 4, 1024, 512], P('dp', None, 'node'), may hold values from -6 to 6
- edge_state: bfloat16 [4, 4, 6144, 512], P('dp', None, 'node'), may hold values from -6 to 6
- node_cotangent: bfloat16 [4, 4, 1024, 512], P('dp', None, 'node'), may hold values from -6 to 6
- edge_cotangent: bfloat16 [4, 4, 6144, 512], P('dp', None, 'node'), may hold values from -6 to 6
- send_rows: int32 [8, 64], P('node'), may hold values from 0 to 127
- edge_sender: int32 [6144], P('node'), may hold values from 0 to 191
- edge_receiver: int32 [6144], P('node'), may hold values from 0 to 127
- rollout_length: int32 [4], P('dp'), may hold values from 1 to 4, as said below
- slot_block: int32 [8], replicated, may hold values from 0 to 7, each once
- step_count: int32 [9], replicated, may hold values from 2 to 6
- weight_slots: float32 [8, 512, 512], P('dp', 'node'), may hold values from -0.1875 to 0.1875
- moment_first: float32 [8, 512, 512], P('dp', 'node'), may hold values from -6 to 6
- moment_second: float32 [8, 512, 512], P('dp', 'node'), may hold values from 0.5 to 3
- basis_left: float32 [8, 512, 512], P('dp', None, 'node'), may hold values from -1 to 1, as said below
- basis_right: float32 [8, 512, 512], P('dp'), may hold values from -1 to 1, as said below
- vector_params: float32 [8, 512], replicated
- vector_first: float32 [8, 512], replicated, may hold values from -6 to 6
- vector_second: float32 [8, 512], replicated, may hold values from 0.5 to 3
Outputs:
- node_output: bfloat16 [4, 4, 1024, 512], P('dp', None, 'node')
- edge_output: bfloat16 [4, 4, 6144, 512], P('dp', None, 'node')
- node_gradient: bfloat16 [4, 4, 1024, 512], P('dp', None, 'node')
- edge_gradient: bfloat16 [4, 4, 6144, 512], P('dp', None, 'node')
- new_first: float32 [8, 512, 512], P('dp', 'node')
- new_second: float32 [8, 512, 512], P('dp', 'node')
- new_weights: float32 [8, 512, 512], P('dp', 'node')
- weights_copy: bfloat16 [8, 512, 512], P('dp', 'node')
- vector_state: float32 [3, 8, 512], replicated
- global_norm: float32 [1], replicated
The draws below stay inside these ranges and needn't reach their ends.
Inputs may be any that keep to these rules, and one draw needn't show every extreme that they name: Slot s holds weight block slot_block[s] where that is below 7, and no block otherwise. `rollout_length`: some sample has all 4 steps. `basis_left`: each slot's matrix is orthogonal. `basis_right`: each slot's matrix is orthogonal.
All inputs are finite; a program needn't handle non-finite values.
Results may differ from the reference program's by a relative error of at most 0.0095.
Values may be sent and summed in bfloat16 or wider, within the bound.
A program may use at most 192 MiB of HBM per device.

```python
import math
import jax
import jax.numpy as jnp
from jax import lax

L = 512
NODE_DEV = 128
ROLL = 4
NBLOCK = 7
EDGE_DEV = 768
HALO_SLOT = 8
HALO = 64
NODES = 1024
EDGES = 6144
SAMPLES = 4
SLOTS = 8
N_NODE = 8


def orthogonal(key):
    order_keys = jax.random.split(jax.random.fold_in(key, 3), SLOTS)
    order = jax.vmap(lambda one_key: jax.random.permutation(one_key, L))(order_keys).astype(jnp.float32)
    row_signs = 2.0 * jax.random.randint(jax.random.fold_in(key, 4), (SLOTS, L, 1), 0, 2).astype(jnp.float32) - 1.0
    col_signs = 2.0 * jax.random.randint(jax.random.fold_in(key, 6), (SLOTS, 1, L), 0, 2).astype(jnp.float32) - 1.0
    freq = order[:, :, None]
    column_ids = jnp.arange(L, dtype=jnp.float32)[None, None, :]
    table = jnp.cos(math.pi * (2.0 * column_ids + 1.0) * freq / (2.0 * L))
    scales = jnp.where(freq == 0.0, math.sqrt(1.0 / L), math.sqrt(2.0 / L))
    return (table * scales * row_signs * col_signs).astype(jnp.float32)


def draw_basis_left(key, part):
    return orthogonal(jax.random.fold_in(key, 11))


def draw_basis_right(key, part):
    return orthogonal(jax.random.fold_in(key, 23))


def draw_vector_params(key, part):
    row_ids = jnp.arange(8, dtype=jnp.int32)[:, None]
    gain_rows = (row_ids == 2) | (row_ids == 6)
    noise_draw = jax.random.normal(jax.random.fold_in(key, 31), (8, L), jnp.float32)
    return jnp.where(gain_rows, 1.0 + 0.15 * noise_draw, 0.5 * noise_draw)


def draw_rollout_length(key, part):
    lengths = jax.random.randint(jax.random.fold_in(key, 5), (SAMPLES,), 1, ROLL + 1)
    longest = jax.random.randint(jax.random.fold_in(key, 7), (), 0, SAMPLES)
    return jnp.where(jnp.arange(SAMPLES) == longest, ROLL, lengths).astype(jnp.int32)


def touch_ends(drawn, key, low, high):
    index_at = [jax.random.randint(jax.random.fold_in(key, axis), (), 0, length) for axis, length in enumerate(drawn.shape)]
    widest = drawn.shape.index(max(drawn.shape))
    beside = index_at[:widest] + [(index_at[widest] + 1) % drawn.shape[widest]] + index_at[widest + 1:]
    return drawn.at[tuple(index_at)].set(low).at[tuple(beside)].set(high)


def levels(own_key, shape, cuts, least, top_value):
    loudness = 1.0
    for dim, shards_of in cuts:
        steps = jax.random.uniform(jax.random.fold_in(jax.random.fold_in(own_key, 6), dim), (shards_of,), jnp.float32, least / len(cuts), top_value / len(cuts))
        loudness = loudness * jnp.repeat(jnp.exp(steps), shape[dim] // shards_of).reshape((-1,) + (1,) * (len(shape) - 1 - dim))
    return loudness


def centred(key, shape, scale, most, pieces=(), kind=jnp.bfloat16):
    drawn = scale * jax.random.normal(key, shape, jnp.float32)
    if pieces:
        drawn = drawn * levels(key, shape, pieces, -0.22, 0.18)
    return jnp.clip(drawn, -most, most).astype(kind)


def setup_inputs(seed: int = 0) -> dict:
    key_list = jax.random.split(jax.random.key(seed), 19)
    node_state = centred(key_list[0], (SAMPLES, ROLL, NODES, L), 1.0, 6.0, ((0, 4), (2, 8)))
    edge_state = centred(key_list[1], (SAMPLES, ROLL, EDGES, L), 1.0, 6.0, ((0, 4), (2, 8)))
    node_cotangent = centred(key_list[2], (SAMPLES, ROLL, NODES, L), 1.0, 6.0, ((0, 4), (2, 8)))
    edge_cotangent = centred(key_list[3], (SAMPLES, ROLL, EDGES, L), 1.0, 6.0, ((0, 4), (2, 8)))
    send_rows = touch_ends(jax.random.randint(key_list[4], (N_NODE, HALO), 0, NODE_DEV), jax.random.fold_in(key_list[4], 1), 0, NODE_DEV - 1).astype(jnp.int32)
    edge_sender = touch_ends(jax.random.randint(key_list[5], (EDGES,), 0, NODE_DEV + HALO), jax.random.fold_in(key_list[5], 1), 0, (NODE_DEV + HALO) - 1).astype(jnp.int32)
    edge_receiver = touch_ends(jax.random.randint(key_list[6], (EDGES,), 0, NODE_DEV), jax.random.fold_in(key_list[6], 1), 0, NODE_DEV - 1).astype(jnp.int32)
    rollout_length = draw_rollout_length(jax.random.fold_in(key_list[18], 71), 0)
    slot_block = jax.random.permutation(key_list[8], SLOTS).astype(jnp.int32)
    step_count = touch_ends(jax.random.randint(key_list[9], (SLOTS + 1,), 2, 7), jax.random.fold_in(key_list[9], 1), 2, 6).astype(jnp.int32)
    weight_slots = centred(key_list[10], (SLOTS, L, L), (2 * L) ** -0.5, 0.1875, ((0, 4), (1, 8)), jnp.float32)
    moment_first = centred(key_list[11], (SLOTS, L, L), 1.0, 6.0, ((0, 4), (1, 8)), jnp.float32)
    moment_second = jnp.clip(jnp.exp(math.log(3.0) - 1.7917595 * jax.random.uniform(key_list[12], (SLOTS, L, L), jnp.float32) ** levels(key_list[12], (SLOTS, L, L), ((0, 4), (1, 8)), -0.2, 0.2)), 0.5, 3.0)
    basis_left = draw_basis_left(jax.random.fold_in(key_list[18], 71), 0)
    basis_right = draw_basis_right(jax.random.fold_in(key_list[18], 71), 0)
    vector_params = draw_vector_params(jax.random.fold_in(key_list[18], 71), 0)
    vector_first = centred(key_list[16], (8, L), 1.0, 6.0, (), jnp.float32)
    vector_second = jnp.clip(jnp.exp(jax.random.uniform(key_list[17], (8, L), jnp.float32, math.log(0.5), math.log(3.0))), 0.5, 3.0)
    return dict(node_state=node_state, edge_state=edge_state, node_cotangent=node_cotangent, edge_cotangent=edge_cotangent, send_rows=send_rows, edge_sender=edge_sender, edge_receiver=edge_receiver, rollout_length=rollout_length, slot_block=slot_block, step_count=step_count, weight_slots=weight_slots, moment_first=moment_first, moment_second=moment_second, basis_left=basis_left, basis_right=basis_right, vector_params=vector_params, vector_first=vector_first, vector_second=vector_second)


highest = lax.Precision.HIGHEST
norm_epsilon = 1e-05
adam_epsilon = 1e-08
beta_first = 0.5
beta_second = 0.5
rate_matrix = 0.03
rate_vector = 0.4
weight_decay = 0.01

@jax.custom_vjp
def low(v):
    return lax.optimization_barrier(v.astype(jnp.bfloat16)).astype(jnp.float32)

@jax.custom_vjp
def low_back(v):
    return v

def low_keep(v):
    return (low(v), None)

def low_pass(kept, grad):
    return (grad,)

def back_keep(v):
    return (v, None)

def back_low(kept, grad):
    return (low(grad),)
low.defvjp(low_keep, low_pass)
low_back.defvjp(back_keep, back_low)

def layer_norm(values, norm_gain, norm_shift):
    center = values - lax.optimization_barrier(jnp.mean(values, axis=-1, keepdims=True))
    spread = lax.optimization_barrier(jnp.mean(center * center, axis=-1, keepdims=True))
    return center * lax.rsqrt(spread + norm_epsilon) * norm_gain + norm_shift

def branch(inputs, w_in, w_out, vectors, offset):
    before = low_back(jnp.dot(inputs, w_in, precision=highest, preferred_element_type=jnp.float32) + vectors[offset])
    hidden = low(jax.nn.silu(before))
    branch_out = low_back(jnp.dot(hidden, w_out, precision=highest, preferred_element_type=jnp.float32) + vectors[offset + 1])
    return layer_norm(branch_out, vectors[offset + 2], vectors[offset + 3])

def adam_direction(moment_one, moment_two, fix_one, fix_two):
    return moment_one / fix_one / (jnp.sqrt(moment_two / fix_two) + adam_epsilon)

def reference(node_state, edge_state, node_cotangent, edge_cotangent, send_rows, edge_sender, edge_receiver, rollout_length, slot_block, step_count, weight_slots, moment_first, moment_second, basis_left, basis_right, vector_params, vector_first, vector_second):
    clip_limit = math.sqrt(7 * L * L + 8 * L)
    device = jnp.arange(EDGES, dtype=jnp.int32) // EDGE_DEV
    local_id = edge_sender.astype(jnp.int32)
    halo_id = jnp.maximum(local_id - NODE_DEV, 0)
    source = halo_id // HALO_SLOT
    column = device * HALO_SLOT + halo_id % HALO_SLOT
    remote = source * NODE_DEV + send_rows[source, column]
    sender = jnp.where(local_id < NODE_DEV, device * NODE_DEV + local_id, remote).astype(jnp.int32)
    receiver = (device * NODE_DEV + edge_receiver).astype(jnp.int32)
    live_steps = (jnp.arange(ROLL, dtype=jnp.int32)[None, :] < rollout_length[:, None]).astype(jnp.float32)
    block_slot = jnp.argmax(slot_block[None, :] == jnp.arange(NBLOCK, dtype=jnp.int32)[:, None], axis=1)

    def forward(node_values, edge_values, slot_values, vector_values):
        rounded = low(slot_values)
        blocks = rounded[block_slot]
        w_edge_in = blocks[0:3].reshape(3 * L, L)
        w_edge_out = blocks[3]
        w_node_in = blocks[4:6].reshape(2 * L, L)
        w_node_out = blocks[6]

        def one_graph(graph_item):
            node_in, edge_in, keep_mask = graph_item
            joined = jnp.concatenate([edge_in, node_in[sender], node_in[receiver]], axis=1)
            edge_new = edge_in + branch(joined, w_edge_in, w_edge_out, vector_values, 0)
            summed = jax.ops.segment_sum(edge_new, receiver, num_segments=NODES)
            node_join = jnp.concatenate([node_in, low(summed)], axis=1)
            node_new = node_in + branch(node_join, w_node_in, w_node_out, vector_values, 4)
            return (node_new * keep_mask, edge_new * keep_mask)
        outputs = lax.map(jax.checkpoint(one_graph), (node_values.reshape(SAMPLES * ROLL, NODES, L), edge_values.reshape(SAMPLES * ROLL, EDGES, L), live_steps.reshape(-1)))
        return (outputs[0].reshape(node_values.shape), outputs[1].reshape(edge_values.shape))
    primal, pullback = jax.vjp(forward, node_state.astype(jnp.float32), edge_state.astype(jnp.float32), weight_slots, vector_params)
    gradients = pullback((node_cotangent.astype(jnp.float32), edge_cotangent.astype(jnp.float32)))
    grad_slots = gradients[2]
    grad_vectors = gradients[3]
    square_sum = jnp.sum(grad_slots * grad_slots) + jnp.sum(grad_vectors * grad_vectors)
    grad_norm = jnp.sqrt(square_sum)
    clip_scale = jnp.minimum(1.0, clip_limit / grad_norm)
    grad_slots = grad_slots * clip_scale
    grad_vectors = grad_vectors * clip_scale
    slot_steps = step_count[:SLOTS].astype(jnp.float32)[:, None, None]
    fix_one = 1.0 - jnp.power(jnp.float32(beta_first), slot_steps)
    fix_two = 1.0 - jnp.power(jnp.float32(beta_second), slot_steps)
    rotated = jnp.einsum('sij,sik->sjk', basis_left, grad_slots, precision=highest)
    rotated = jnp.einsum('sjk,skl->sjl', rotated, basis_right, precision=highest)
    moment_one = beta_first * moment_first + (1.0 - beta_first) * rotated
    moment_two = beta_second * moment_second + (1.0 - beta_second) * rotated * rotated
    direction = adam_direction(moment_one, moment_two, fix_one, fix_two)
    turned = jnp.einsum('sjl,sml->sjm', direction, basis_right, precision=highest)
    reverted = jnp.einsum('sij,sjm->sim', basis_left, turned, precision=highest)
    new_weights = weight_slots - rate_matrix * (reverted + weight_decay * weight_slots)
    vec_step = step_count[SLOTS].astype(jnp.float32)
    vfix_one = 1.0 - jnp.power(jnp.float32(beta_first), vec_step)
    vfix_two = 1.0 - jnp.power(jnp.float32(beta_second), vec_step)
    vec_one = beta_first * vector_first + (1.0 - beta_first) * grad_vectors
    vec_two = beta_second * vector_second + (1.0 - beta_second) * grad_vectors * grad_vectors
    vec_new = vector_params - rate_vector * adam_direction(vec_one, vec_two, vfix_one, vfix_two)
    return (primal[0].astype(jnp.bfloat16), primal[1].astype(jnp.bfloat16), gradients[0].astype(jnp.bfloat16), gradients[1].astype(jnp.bfloat16), moment_one, moment_two, new_weights, new_weights.astype(jnp.bfloat16), jnp.stack([vec_new, vec_one, vec_two]), grad_norm.reshape(1))
```

```python
import functools
import math

import jax
import jax.numpy as jnp
from jax import lax
from jax.experimental import pallas as pl
from jax.experimental.pallas import tpu as pltpu
from jax.sharding import PartitionSpec as P

NBLOCK = 7
f32 = jnp.float32
bf16 = jnp.bfloat16
highest = lax.Precision.HIGHEST
norm_epsilon = 1e-05
adam_epsilon = 1e-08
beta_first = 0.5
beta_second = 0.5
rate_matrix = 0.03
rate_vector = 0.4
weight_decay = 0.01


def dot(a, b):
    return jnp.dot(a, b, preferred_element_type=f32)


def dot_tb(a, b):
    return lax.dot_general(a, b, (((1,), (1,)), ((), ())), preferred_element_type=f32)


def dot_ta(a, b):
    return lax.dot_general(a, b, (((0,), (0,)), ((), ())), preferred_element_type=f32)


def eights(x):
    return jnp.sum(x.reshape(x.shape[0] // 8, 8, x.shape[1]), axis=0)


def sigmoid(z):
    return 0.5 * jnp.tanh(0.5 * z) + 0.5


def branch_forward(z, w_out, bias_out):
    s = sigmoid(z)
    h = z * s
    slope = s + h * (1.0 - s)
    hidden = h.astype(bf16)
    after = dot(hidden, w_out) + bias_out
    center = after - jnp.mean(after, axis=1, keepdims=True)
    spread = jnp.mean(center * center, axis=1, keepdims=True)
    inverse = lax.rsqrt(spread + norm_epsilon)
    return hidden, slope, center * inverse, inverse


def norm_backward(upstream, normed, inverse, gain):
    u = upstream * gain
    first = jnp.mean(u, axis=1, keepdims=True)
    second = jnp.mean(u * normed, axis=1, keepdims=True)
    return (inverse * (u - first - normed * second)).astype(bf16)


def layer_kernel(
    rollout_ref,
    slot_block_ref,
    node_hbm,
    edge_hbm,
    ncot_hbm,
    ecot_hbm,
    sender_ref,
    receiver_ref,
    halo_ref,
    w_ref,
    vec_ref,
    nout_ref,
    eout_hbm,
    nbase_ref,
    egrad_hbm,
    grad_ref,
    gvec_ref,
    hback_ref,
    node_v,
    edge_v,
    ncot_v,
    ecot_v,
    eout_v,
    egrad_v,
    gather_t,
    gather,
    table,
    hidden_v,
    slope_v,
    normed_v,
    inv_v,
    dz_v,
    da_v,
    summed_v,
    dsum_v,
    sc_own,
    sc_recv,
    sc_halo,
    acc,
    sem_in,
    sem_out,
):
    roll, nodes, width = node_v.shape
    edges = edge_v.shape[1]
    peers, per_peer = sc_halo.shape[0], sc_halo.shape[2]
    halo = peers * per_peer
    known = nodes + halo
    padded = table.shape[1]
    chunk = 256
    pieces = edges // chunk

    copies = []
    for i, (src, dst) in enumerate(
        ((node_hbm, node_v), (edge_hbm, edge_v), (ncot_hbm, ncot_v), (ecot_hbm, ecot_v))
    ):
        copies.append(pltpu.make_async_copy(src.at[0], dst, sem_in.at[i]))
        copies[-1].start()

    slot_of = []
    for b in range(NBLOCK):
        found = jnp.int32(0)
        for s in range(slot_block_ref.shape[0]):
            found = jnp.where(slot_block_ref[s] == b, jnp.int32(s), found)
        slot_of.append(found)

    def weight(b):
        return w_ref[slot_of[b]]

    def live(t):
        return jnp.where(t < rollout_ref[0], 1.0, 0.0).astype(f32)

    ids = lax.broadcasted_iota(jnp.int32, (padded, edges), 0)
    onehot = (ids == sender_ref[...]) | (ids == receiver_ref[...] + known)
    onehot = jnp.where(onehot, 1.0, 0.0).astype(f32)
    gather_t[...] = onehot.astype(bf16)
    gather[...] = onehot.T.astype(bf16)
    table[...] = jnp.zeros_like(table)
    acc[...] = jnp.zeros_like(acc)

    copies[0].wait()
    flat_nodes = node_v[...].reshape(roll * nodes, width)
    own_sent = dot(flat_nodes, weight(1))
    own_recv = dot(flat_nodes, weight(2))
    halo_sent = dot(halo_ref[...], weight(1)).reshape(peers, roll, per_peer, width)
    for t in range(roll):
        table[t, :nodes] = own_sent[t * nodes : (t + 1) * nodes].astype(bf16)
        table[t, nodes:known] = halo_sent[:, t].reshape(halo, width).astype(bf16)
        table[t, known : known + nodes] = own_recv[t * nodes : (t + 1) * nodes].astype(bf16)
    copies[1].wait()

    def forward(t, carry):
        lv = live(t)
        total = jnp.zeros((nodes, width), f32)
        for c in range(pieces):
            rows = pl.ds(c * chunk, chunk)
            edge = edge_v[t, rows]
            z = dot(edge, weight(0)) + dot(gather[rows], table[t]) + vec_ref[0:1]
            hidden, slope, normed, inverse = branch_forward(z, weight(3), vec_ref[1:2])
            hidden_v[t, rows] = hidden
            slope_v[t, rows] = slope.astype(bf16)
            normed_v[t, rows] = normed.astype(bf16)
            inv_v[t, rows] = inverse
            new = edge.astype(f32) + (normed * vec_ref[2:3] + vec_ref[3:4])
            eout_v[t, rows] = (new * lv).astype(bf16)
            total += dot(gather_t[known : known + nodes, rows], new.astype(bf16))
        summed_v[pl.ds(t * nodes, nodes)] = total.astype(bf16)
        pltpu.make_async_copy(eout_v.at[t], eout_hbm.at[0, t], sem_out.at[t]).start()
        return carry

    lax.fori_loop(0, roll, forward, 0)

    flat_nodes = node_v[...].reshape(roll * nodes, width)
    summed = summed_v[...]
    z = dot(flat_nodes, weight(4)) + dot(summed, weight(5)) + vec_ref[4:5]
    hidden, slope, normed, inverse = branch_forward(z, weight(6), vec_ref[5:6])
    row_t = lax.broadcasted_iota(jnp.int32, (roll * nodes, 1), 0) // nodes
    row_live = jnp.where(row_t < rollout_ref[0], 1.0, 0.0).astype(f32)
    new = flat_nodes.astype(f32) + (normed * vec_ref[6:7] + vec_ref[7:8])
    nout_ref[0] = (new * row_live).astype(bf16).reshape(roll, nodes, width)
    copies[2].wait()
    d_new = ncot_v[...].reshape(roll * nodes, width).astype(f32) * row_live
    acc[6] += eights(d_new * normed)
    acc[7] += eights(d_new)
    d_after = norm_backward(d_new, normed, inverse, vec_ref[6:7])
    acc[5] += eights(d_after.astype(f32))
    grad_ref[6] = dot_ta(hidden, d_after)
    d_before = (dot_tb(d_after, weight(6)) * slope).astype(bf16)
    acc[4] += eights(d_before.astype(f32))
    grad_ref[4] = dot_ta(flat_nodes, d_before)
    grad_ref[5] = dot_ta(summed, d_before)
    dsum_v[...] = dot_tb(d_before, weight(5)).astype(bf16)
    nbase_ref[...] = d_new + dot_tb(d_before, weight(4))
    grad_ref[0] = jnp.zeros((width, width), f32)
    grad_ref[3] = jnp.zeros((width, width), f32)
    copies[3].wait()

    def backward(t, carry):
        lv = live(t)
        for c in range(pieces):
            rows = pl.ds(c * chunk, chunk)
            d_new = ecot_v[t, rows].astype(f32) * lv + dot(
                gather[rows, known : known + nodes], dsum_v[pl.ds(t * nodes, nodes)]
            )
            normed = normed_v[t, rows].astype(f32)
            acc[2] += eights(d_new * normed)
            acc[3] += eights(d_new)
            d_after = norm_backward(d_new, normed, inv_v[t, rows], vec_ref[2:3])
            acc[1] += eights(d_after.astype(f32))
            da_v[rows] = d_after
            d_before = (dot_tb(d_after, weight(3)) * slope_v[t, rows].astype(f32)).astype(bf16)
            acc[0] += eights(d_before.astype(f32))
            dz_v[rows] = d_before
            egrad_v[t, rows] = (d_new + dot_tb(d_before, weight(0))).astype(bf16)
        pltpu.make_async_copy(egrad_v.at[t], egrad_hbm.at[0, t], sem_out.at[roll + t]).start()
        grad_ref[3] += dot_ta(hidden_v[t], da_v[...])
        grad_ref[0] += dot_ta(edge_v[t], dz_v[...])
        scattered = dot(gather_t[...], dz_v[...])
        sc_own[pl.ds(t * nodes, nodes)] = scattered[:nodes].astype(bf16)
        sc_recv[pl.ds(t * nodes, nodes)] = scattered[known : known + nodes].astype(bf16)
        sc_halo[:, t] = scattered[nodes:known].reshape(peers, per_peer, width)
        return carry

    lax.fori_loop(0, roll, backward, 0)

    halo_sum = sc_halo[...].reshape(roll * halo, width).astype(bf16)
    grad_ref[1] = dot_ta(flat_nodes, sc_own[...]) + dot_ta(halo_ref[...], halo_sum)
    grad_ref[2] = dot_ta(flat_nodes, sc_recv[...])
    hback_ref[...] = dot_tb(halo_sum, weight(1)).astype(bf16)
    nbase_ref[...] += dot_tb(sc_own[...], weight(1)) + dot_tb(sc_recv[...], weight(2))
    gvec_ref[...] = jnp.sum(acc[...], axis=1)

    for t in range(roll):
        pltpu.make_async_copy(eout_v.at[t], eout_hbm.at[0, t], sem_out.at[t]).wait()
        pltpu.make_async_copy(egrad_v.at[t], egrad_hbm.at[0, t], sem_out.at[roll + t]).wait()


def layer(
    rollout_length,
    slot_block,
    node_state,
    edge_state,
    node_cotangent,
    edge_cotangent,
    edge_sender,
    edge_receiver,
    halo,
    slots,
    vector_params,
    per_peer,
):
    _, roll, nodes, width = node_state.shape
    edges = edge_state.shape[2]
    peers = halo.shape[0] // (roll * per_peer)
    known = nodes + peers * per_peer
    padded = -(-(known + nodes) // 128) * 128
    vmem = pl.BlockSpec(memory_space=pltpu.VMEM)
    smem = pl.BlockSpec(memory_space=pltpu.SMEM)
    hbm = pl.BlockSpec(memory_space=pl.ANY)
    shape = jax.ShapeDtypeStruct
    return pl.pallas_call(
        layer_kernel,
        out_shape=(
            shape(node_state.shape, bf16),
            shape(edge_state.shape, bf16),
            shape((roll * nodes, width), f32),
            shape(edge_state.shape, bf16),
            shape((NBLOCK, width, width), f32),
            shape((8, width), f32),
            shape(halo.shape, bf16),
        ),
        in_specs=[smem, smem, hbm, hbm, hbm, hbm, vmem, vmem, vmem, vmem, vmem],
        out_specs=(vmem, hbm, vmem, hbm, vmem, vmem, vmem),
        scratch_shapes=[
            pltpu.VMEM((roll, nodes, width), bf16),
            pltpu.VMEM((roll, edges, width), bf16),
            pltpu.VMEM((roll, nodes, width), bf16),
            pltpu.VMEM((roll, edges, width), bf16),
            pltpu.VMEM((roll, edges, width), bf16),
            pltpu.VMEM((roll, edges, width), bf16),
            pltpu.VMEM((padded, edges), bf16),
            pltpu.VMEM((edges, padded), bf16),
            pltpu.VMEM((roll, padded, width), bf16),
            pltpu.VMEM((roll, edges, width), bf16),
            pltpu.VMEM((roll, edges, width), bf16),
            pltpu.VMEM((roll, edges, width), bf16),
            pltpu.VMEM((roll, edges, 1), f32),
            pltpu.VMEM((edges, width), bf16),
            pltpu.VMEM((edges, width), bf16),
            pltpu.VMEM((roll * nodes, width), bf16),
            pltpu.VMEM((roll * nodes, width), bf16),
            pltpu.VMEM((roll * nodes, width), bf16),
            pltpu.VMEM((roll * nodes, width), bf16),
            pltpu.VMEM((peers, roll, per_peer, width), f32),
            pltpu.VMEM((8, 8, width), f32),
            pltpu.SemaphoreType.DMA((4,)),
            pltpu.SemaphoreType.DMA((2 * roll,)),
        ],
        compiler_params=pltpu.CompilerParams(vmem_limit_bytes=60 << 20),
        name="layer",
    )(
        rollout_length,
        slot_block,
        node_state,
        edge_state,
        node_cotangent,
        edge_cotangent,
        edge_sender.reshape(1, edges),
        edge_receiver.reshape(1, edges),
        halo,
        slots,
        vector_params,
    )


def adam_direction(moment_one, moment_two, fix_one, fix_two):
    return moment_one / fix_one / (jnp.sqrt(moment_two / fix_two) + adam_epsilon)


def local(
    node_state,
    edge_state,
    node_cotangent,
    edge_cotangent,
    send_rows,
    edge_sender,
    edge_receiver,
    rollout_length,
    slot_block,
    step_count,
    weight_slots,
    moment_first,
    moment_second,
    basis_left,
    basis_right,
    vector_params,
    vector_first,
    vector_second,
):
    width = node_state.shape[-1]
    roll, nodes = node_state.shape[1:3]
    clip_limit = math.sqrt(NBLOCK * width * width + 8 * width)
    slot_dev = weight_slots.shape[0]
    slot_total = slot_block.shape[0]
    halo_rows = send_rows.shape[1]
    peers = lax.axis_size("node")
    per_peer = halo_rows // peers
    copies = lax.all_gather(weight_slots.astype(bf16), "node", axis=1, tiled=True)
    slots = lax.all_gather(copies, "dp", axis=0, tiled=True)
    back_onehot = (send_rows[0][:, None] == jnp.arange(nodes, dtype=jnp.int32)[None, :]).astype(bf16)
    outgoing = jnp.einsum("hk,tkd->htd", back_onehot, node_state[0], preferred_element_type=f32)
    outgoing = outgoing.astype(bf16).reshape(peers, per_peer, roll, width).transpose(0, 2, 1, 3)
    outgoing = outgoing.reshape(peers * roll * per_peer, width)
    halo = lax.all_to_all(outgoing, "node", split_axis=0, concat_axis=0, tiled=True)

    node_output, edge_output, node_base, edge_gradient, grads, grad_vectors, halo_back = layer(
        rollout_length,
        slot_block,
        node_state,
        edge_state,
        node_cotangent,
        edge_cotangent,
        edge_sender,
        edge_receiver,
        halo,
        slots,
        vector_params,
        per_peer,
    )
    returned = lax.all_to_all(halo_back, "node", split_axis=0, concat_axis=0, tiled=True)
    returned = returned.reshape(peers, roll, per_peer, width).transpose(0, 2, 1, 3)
    d_back = jnp.einsum(
        "hk,htd->tkd",
        back_onehot,
        returned.reshape(halo_rows, roll, width),
        preferred_element_type=f32,
    )
    node_gradient = node_base.reshape(roll, nodes, width) + d_back
    node_gradient = node_gradient.astype(bf16).reshape(node_state.shape)

    block_of_slot = slot_block[None, :] == jnp.arange(NBLOCK, dtype=jnp.int32)[:, None]
    first = lax.axis_index("dp") * slot_dev
    summed, grad_vectors = lax.psum((grads, grad_vectors), ("dp", "node"))
    own_square = jnp.sum(summed * summed)
    mine = lax.dynamic_slice_in_dim(block_of_slot.astype(f32), first, slot_dev, 1)
    owned_grads = jnp.einsum("bs,bij->sij", mine, summed, precision=highest)
    square_sum = own_square + jnp.sum(grad_vectors * grad_vectors)
    grad_norm = jnp.sqrt(square_sum)
    clip_scale = jnp.minimum(1.0, clip_limit / grad_norm)
    owned_grads = owned_grads * clip_scale
    grad_vectors = grad_vectors * clip_scale
    own_steps = lax.dynamic_slice_in_dim(step_count, first, slot_dev, 0)
    slot_steps = own_steps.astype(f32)[:, None, None]
    fix_one = 1.0 - jnp.power(f32(beta_first), slot_steps)
    fix_two = 1.0 - jnp.power(f32(beta_second), slot_steps)
    rotated = jnp.einsum("sij,sik->sjk", basis_left, owned_grads, precision=highest, preferred_element_type=f32)
    rotated = jnp.einsum("sjk,skl->sjl", rotated, basis_right, precision=highest, preferred_element_type=f32)
    moment_one = beta_first * moment_first + (1.0 - beta_first) * rotated
    moment_two = beta_second * moment_second + (1.0 - beta_second) * rotated * rotated
    direction = adam_direction(moment_one, moment_two, fix_one, fix_two)
    turned = jnp.einsum("sjl,sml->sjm", direction, basis_right, precision=highest, preferred_element_type=f32)
    reverted = jnp.einsum("sij,sjm->ism", basis_left, turned, precision=highest, preferred_element_type=f32)
    reverted = lax.psum_scatter(reverted.astype(bf16), "node", scatter_dimension=0, tiled=True).astype(f32)
    reverted = jnp.transpose(reverted, (1, 0, 2))
    new_weights = weight_slots - rate_matrix * (reverted + weight_decay * weight_slots)
    vec_step = step_count[slot_total].astype(f32)
    vfix_one = 1.0 - jnp.power(f32(beta_first), vec_step)
    vfix_two = 1.0 - jnp.power(f32(beta_second), vec_step)
    vec_one = beta_first * vector_first + (1.0 - beta_first) * grad_vectors
    vec_two = beta_second * vector_second + (1.0 - beta_second) * grad_vectors * grad_vectors
    vec_new = vector_params - rate_vector * adam_direction(vec_one, vec_two, vfix_one, vfix_two)
    vector_state = jnp.stack([vec_new, vec_one, vec_two])
    return (
        node_output,
        edge_output,
        node_gradient,
        edge_gradient,
        moment_one,
        moment_two,
        new_weights,
        new_weights.astype(bf16),
        vector_state,
        grad_norm.reshape(1),
    )


def solution(mesh):
    in_specs = (
        P("dp", None, "node", None),
        P("dp", None, "node", None),
        P("dp", None, "node", None),
        P("dp", None, "node", None),
        P("node", None),
        P("node"),
        P("node"),
        P("dp"),
        P(),
        P(),
        P("dp", "node", None),
        P("dp", "node", None),
        P("dp", "node", None),
        P("dp", None, "node"),
        P("dp", None, None),
        P(),
        P(),
        P(),
    )
    out_specs = (
        P("dp", None, "node", None),
        P("dp", None, "node", None),
        P("dp", None, "node", None),
        P("dp", None, "node", None),
        P("dp", "node", None),
        P("dp", "node", None),
        P("dp", "node", None),
        P("dp", "node", None),
        P(),
        P(),
    )
    return jax.shard_map(local, mesh=mesh, in_specs=in_specs, out_specs=out_specs, check_vma=False)
```

```python
import functools
import math

import jax
import jax.numpy as jnp
from jax import lax
from jax.experimental import pallas as pl
from jax.experimental.pallas import tpu as pltpu
from jax.sharding import PartitionSpec as P

NBLOCK = 7
f32 = jnp.float32
bf16 = jnp.bfloat16
highest = lax.Precision.HIGHEST
norm_epsilon = 1e-05
adam_epsilon = 1e-08
beta_first = 0.5
beta_second = 0.5
rate_matrix = 0.03
rate_vector = 0.4
weight_decay = 0.01


def dot(a, b):
    return jnp.dot(a, b, preferred_element_type=f32)


def dot_tb(a, b):
    return lax.dot_general(a, b, (((1,), (1,)), ((), ())), preferred_element_type=f32)


def dot_ta(a, b):
    return lax.dot_general(a, b, (((0,), (0,)), ((), ())), preferred_element_type=f32)


def eights(x):
    return jnp.sum(x.reshape(x.shape[0] // 8, 8, x.shape[1]), axis=0)


def sigmoid(z):
    return 0.5 * jnp.tanh(0.5 * z) + 0.5


def branch_forward(z, w_out, bias_out):
    s = sigmoid(z)
    h = z * s
    slope = s + h * (1.0 - s)
    hidden = h.astype(bf16)
    after = dot(hidden, w_out) + bias_out
    center = after - jnp.mean(after, axis=1, keepdims=True)
    spread = jnp.mean(center * center, axis=1, keepdims=True)
    inverse = lax.rsqrt(spread + norm_epsilon)
    return hidden, slope, center * inverse, inverse


def norm_backward(upstream, normed, inverse, gain):
    u = upstream * gain
    first = jnp.mean(u, axis=1, keepdims=True)
    second = jnp.mean(u * normed, axis=1, keepdims=True)
    return (inverse * (u - first - normed * second)).astype(bf16)


def layer_kernel(
    rollout_ref,
    slot_block_ref,
    node_hbm,
    edge_hbm,
    ncot_hbm,
    ecot_hbm,
    sender_ref,
    receiver_ref,
    halo_ref,
    w_ref,
    vec_ref,
    nout_ref,
    eout_hbm,
    nbase_ref,
    egrad_hbm,
    grad_ref,
    gvec_ref,
    hback_ref,
    node_v,
    edge_v,
    ncot_v,
    ecot_v,
    eout_v,
    egrad_v,
    gather_t,
    gather,
    table,
    hidden_v,
    slope_v,
    normed_v,
    inv_v,
    dz_v,
    da_v,
    summed_v,
    dsum_v,
    sc_own,
    sc_recv,
    sc_halo,
    acc,
    sem_in,
    sem_out,
):
    roll, nodes, width = node_v.shape
    edges = edge_v.shape[1]
    peers, per_peer = sc_halo.shape[0], sc_halo.shape[2]
    halo = peers * per_peer
    known = nodes + halo
    padded = table.shape[1]
    chunk = 256
    pieces = edges // chunk

    copies = []
    for i, (src, dst) in enumerate(
        ((node_hbm, node_v), (edge_hbm, edge_v), (ncot_hbm, ncot_v), (ecot_hbm, ecot_v))
    ):
        copies.append(pltpu.make_async_copy(src.at[0], dst, sem_in.at[i]))
        copies[-1].start()

    slot_of = []
    for b in range(NBLOCK):
        found = jnp.int32(0)
        for s in range(slot_block_ref.shape[0]):
            found = jnp.where(slot_block_ref[s] == b, jnp.int32(s), found)
        slot_of.append(found)

    def weight(b):
        return w_ref[slot_of[b]]

    def live(t):
        return jnp.where(t < rollout_ref[0], 1.0, 0.0).astype(f32)

    ids = lax.broadcasted_iota(jnp.int32, (padded, edges), 0)
    onehot = (ids == sender_ref[...]) | (ids == receiver_ref[...] + known)
    onehot = jnp.where(onehot, 1.0, 0.0).astype(f32)
    gather_t[...] = onehot.astype(bf16)
    gather[...] = onehot.T.astype(bf16)
    table[...] = jnp.zeros_like(table)
    acc[...] = jnp.zeros_like(acc)

    copies[0].wait()
    flat_nodes = node_v[...].reshape(roll * nodes, width)
    own_sent = dot(flat_nodes, weight(1))
    own_recv = dot(flat_nodes, weight(2))
    halo_sent = dot(halo_ref[...], weight(1)).reshape(peers, roll, per_peer, width)
    for t in range(roll):
        table[t, :nodes] = own_sent[t * nodes : (t + 1) * nodes].astype(bf16)
        table[t, nodes:known] = halo_sent[:, t].reshape(halo, width).astype(bf16)
        table[t, known : known + nodes] = own_recv[t * nodes : (t + 1) * nodes].astype(bf16)
    copies[1].wait()

    def forward(t, carry):
        lv = live(t)
        total = jnp.zeros((nodes, width), f32)
        for c in range(pieces):
            rows = pl.ds(c * chunk, chunk)
            edge = edge_v[t, rows]
            z = dot(edge, weight(0)) + dot(gather[rows], table[t]) + vec_ref[0:1]
            hidden, slope, normed, inverse = branch_forward(z, weight(3), vec_ref[1:2])
            hidden_v[t, rows] = hidden
            slope_v[t, rows] = slope.astype(bf16)
            normed_v[t, rows] = normed.astype(bf16)
            inv_v[t, rows] = inverse
            new = edge.astype(f32) + (normed * vec_ref[2:3] + vec_ref[3:4])
            eout_v[t, rows] = (new * lv).astype(bf16)
            total += dot(gather_t[known : known + nodes, rows], new.astype(bf16))
        summed_v[pl.ds(t * nodes, nodes)] = total.astype(bf16)
        pltpu.make_async_copy(eout_v.at[t], eout_hbm.at[0, t], sem_out.at[t]).start()
        return carry

    lax.fori_loop(0, roll, forward, 0)

    flat_nodes = node_v[...].reshape(roll * nodes, width)
    summed = summed_v[...]
    z = dot(flat_nodes, weight(4)) + dot(summed, weight(5)) + vec_ref[4:5]
    hidden, slope, normed, inverse = branch_forward(z, weight(6), vec_ref[5:6])
    row_t = lax.broadcasted_iota(jnp.int32, (roll * nodes, 1), 0) // nodes
    row_live = jnp.where(row_t < rollout_ref[0], 1.0, 0.0).astype(f32)
    new = flat_nodes.astype(f32) + (normed * vec_ref[6:7] + vec_ref[7:8])
    nout_ref[0] = (new * row_live).astype(bf16).reshape(roll, nodes, width)
    copies[2].wait()
    d_new = ncot_v[...].reshape(roll * nodes, width).astype(f32) * row_live
    acc[6] += eights(d_new * normed)
    acc[7] += eights(d_new)
    d_after = norm_backward(d_new, normed, inverse, vec_ref[6:7])
    acc[5] += eights(d_after.astype(f32))
    grad_ref[6] = dot_ta(hidden, d_after)
    d_before = (dot_tb(d_after, weight(6)) * slope).astype(bf16)
    acc[4] += eights(d_before.astype(f32))
    grad_ref[4] = dot_ta(flat_nodes, d_before)
    grad_ref[5] = dot_ta(summed, d_before)
    dsum_v[...] = dot_tb(d_before, weight(5)).astype(bf16)
    nbase_ref[...] = d_new + dot_tb(d_before, weight(4))
    grad_ref[0] = jnp.zeros((width, width), f32)
    grad_ref[3] = jnp.zeros((width, width), f32)
    copies[3].wait()

    def backward(t, carry):
        lv = live(t)
        for c in range(pieces):
            rows = pl.ds(c * chunk, chunk)
            d_new = ecot_v[t, rows].astype(f32) * lv + dot(
                gather[rows, known : known + nodes], dsum_v[pl.ds(t * nodes, nodes)]
            )
            normed = normed_v[t, rows].astype(f32)
            acc[2] += eights(d_new * normed)
            acc[3] += eights(d_new)
            d_after = norm_backward(d_new, normed, inv_v[t, rows], vec_ref[2:3])
            acc[1] += eights(d_after.astype(f32))
            da_v[rows] = d_after
            d_before = (dot_tb(d_after, weight(3)) * slope_v[t, rows].astype(f32)).astype(bf16)
            acc[0] += eights(d_before.astype(f32))
            dz_v[rows] = d_before
            egrad_v[t, rows] = (d_new + dot_tb(d_before, weight(0))).astype(bf16)
        pltpu.make_async_copy(egrad_v.at[t], egrad_hbm.at[0, t], sem_out.at[roll + t]).start()
        grad_ref[3] += dot_ta(hidden_v[t], da_v[...])
        grad_ref[0] += dot_ta(edge_v[t], dz_v[...])
        scattered = dot(gather_t[...], dz_v[...])
        sc_own[pl.ds(t * nodes, nodes)] = scattered[:nodes].astype(bf16)
        sc_recv[pl.ds(t * nodes, nodes)] = scattered[known : known + nodes].astype(bf16)
        sc_halo[:, t] = scattered[nodes:known].reshape(peers, per_peer, width)
        return carry

    lax.fori_loop(0, roll, backward, 0)

    halo_sum = sc_halo[...].reshape(roll * halo, width).astype(bf16)
    grad_ref[1] = dot_ta(flat_nodes, sc_own[...]) + dot_ta(halo_ref[...], halo_sum)
    grad_ref[2] = dot_ta(flat_nodes, sc_recv[...])
    hback_ref[...] = dot_tb(halo_sum, weight(1)).astype(bf16)
    nbase_ref[...] += dot_tb(sc_own[...], weight(1)) + dot_tb(sc_recv[...], weight(2))
    gvec_ref[...] = jnp.sum(acc[...], axis=1)

    for t in range(roll):
        pltpu.make_async_copy(eout_v.at[t], eout_hbm.at[0, t], sem_out.at[t]).wait()
        pltpu.make_async_copy(egrad_v.at[t], egrad_hbm.at[0, t], sem_out.at[roll + t]).wait()


def layer(
    rollout_length,
    slot_block,
    node_state,
    edge_state,
    node_cotangent,
    edge_cotangent,
    edge_sender,
    edge_receiver,
    halo,
    slots,
    vector_params,
    per_peer,
):
    _, roll, nodes, width = node_state.shape
    edges = edge_state.shape[2]
    peers = halo.shape[0] // (roll * per_peer)
    known = nodes + peers * per_peer
    padded = -(-(known + nodes) // 128) * 128
    vmem = pl.BlockSpec(memory_space=pltpu.VMEM)
    smem = pl.BlockSpec(memory_space=pltpu.SMEM)
    hbm = pl.BlockSpec(memory_space=pl.ANY)
    shape = jax.ShapeDtypeStruct
    return pl.pallas_call(
        layer_kernel,
        out_shape=(
            shape(node_state.shape, bf16),
            shape(edge_state.shape, bf16),
            shape((roll * nodes, width), f32),
            shape(edge_state.shape, bf16),
            shape((NBLOCK, width, width), f32),
            shape((8, width), f32),
            shape(halo.shape, bf16),
        ),
        in_specs=[smem, smem, hbm, hbm, hbm, hbm, vmem, vmem, vmem, vmem, vmem],
        out_specs=(vmem, hbm, vmem, hbm, vmem, vmem, vmem),
        scratch_shapes=[
            pltpu.VMEM((roll, nodes, width), bf16),
            pltpu.VMEM((roll, edges, width), bf16),
            pltpu.VMEM((roll, nodes, width), bf16),
            pltpu.VMEM((roll, edges, width), bf16),
            pltpu.VMEM((roll, edges, width), bf16),
            pltpu.VMEM((roll, edges, width), bf16),
            pltpu.VMEM((padded, edges), bf16),
            pltpu.VMEM((edges, padded), bf16),
            pltpu.VMEM((roll, padded, width), bf16),
            pltpu.VMEM((roll, edges, width), bf16),
            pltpu.VMEM((roll, edges, width), bf16),
            pltpu.VMEM((roll, edges, width), bf16),
            pltpu.VMEM((roll, edges, 1), f32),
            pltpu.VMEM((edges, width), bf16),
            pltpu.VMEM((edges, width), bf16),
            pltpu.VMEM((roll * nodes, width), bf16),
            pltpu.VMEM((roll * nodes, width), bf16),
            pltpu.VMEM((roll * nodes, width), bf16),
            pltpu.VMEM((roll * nodes, width), bf16),
            pltpu.VMEM((peers, roll, per_peer, width), f32),
            pltpu.VMEM((8, 8, width), f32),
            pltpu.SemaphoreType.DMA((4,)),
            pltpu.SemaphoreType.DMA((2 * roll,)),
        ],
        compiler_params=pltpu.CompilerParams(vmem_limit_bytes=60 << 20),
        name="layer",
    )(
        rollout_length,
        slot_block,
        node_state,
        edge_state,
        node_cotangent,
        edge_cotangent,
        edge_sender.reshape(1, edges),
        edge_receiver.reshape(1, edges),
        halo,
        slots,
        vector_params,
    )


def adam_direction(moment_one, moment_two, fix_one, fix_two):
    return moment_one / fix_one / (jnp.sqrt(moment_two / fix_two) + adam_epsilon)


MESH = pl.DeviceIdType.MESH


class Place:
    def __init__(self):
        self.z = lax.axis_index("dp")
        self.n = lax.axis_index("node")
        self.c = lax.rem(self.n, 2)
        self.x = lax.rem(self.n // 2, 2)
        self.y = self.n // 4
        self.xn = self.n + 2 - 4 * self.x
        self.yn = self.n + 4 - 8 * self.y
        self.sib = self.n + 1 - 2 * self.c
        self.diag = self.xn + 4 - 8 * self.y


def remote(src, dst, send, recv, z, n):
    return pltpu.make_async_remote_copy(
        src_ref=src, dst_ref=dst, send_sem=send, recv_sem=recv, device_id=(z, n), device_id_type=MESH
    )


def greet(p, depth, peers):
    barrier = pltpu.get_barrier_semaphore()
    for k in range(1, peers):
        to = lax.rem(p.n + k, peers)
        pl.semaphore_signal(barrier, inc=1, device_id=(p.z, to), device_id_type=MESH)
    for k in range(1, depth):
        to = lax.rem(p.z + k, depth)
        pl.semaphore_signal(barrier, inc=1, device_id=(to, p.n), device_id_type=MESH)
    pl.semaphore_wait(barrier, peers + depth - 2)


ORDER = ((0, 1, 2, 3), (1, 0, 2, 3), (2, 3, 1, 0), (3, 2, 1, 0))


def gather_start(p, buf, k, sems):
    send, recv = sems
    own = buf(k, p.n)
    copies = []
    for i, to in ((0, p.xn), (1, p.yn), (3, p.sib)):
        copies.append(remote(own, own, send.at[i, k], recv.at[i, k], p.z, to))
        copies[-1].start()
    return copies


def gather_side(p, buf, k, sems):
    send, recv = sems
    copies = []
    for i, owner in ((0, p.xn), (1, p.yn)):
        got = buf(k, owner)
        remote(got, got, send.at[i, k], recv.at[i, k], p.z, owner).wait_recv()
        on = remote(got, got, send.at[4 + i, k], recv.at[4 + i, k], p.z, p.sib)
        on.start()
        copies.append(on)
        over = remote(got, got, send.at[2, k], recv.at[2, k], p.z, p.yn if i == 0 else p.xn)
        pl.when(p.c == i)(over.start)
    copies.append(over)
    return copies


def gather_far(p, buf, k, sems):
    send, recv = sems
    got = buf(k, p.diag)
    remote(got, got, send.at[2, k], recv.at[2, k], p.z, p.xn).wait_recv()
    on = remote(got, got, send.at[6, k], recv.at[6, k], p.z, p.sib)
    on.start()
    return [on]


def gather_end(p, buf, k, sems):
    send, recv = sems
    for i in (3, 4, 5, 6):
        got = buf(k, p.sib)
        remote(got, got, send.at[i, k], recv.at[i, k], p.z, p.sib).wait_recv()


def prepare_kernel(
    weight_ref,
    node_ref,
    send_rows_ref,
    left_ref,
    slots,
    halo,
    left_t,
    hout32,
    hout,
    left_b,
    ssem,
    rsem,
    zssem,
    zrsem,
    hssem,
    hrsem,
    lssem,
    lrsem,
):
    p = Place()
    depth, peers = 4, 8
    roll, nodes, width = node_ref.shape[1:]
    slot_dev, rows = weight_ref.shape[:2]
    per_peer = send_rows_ref.shape[1] // peers

    def buf(k, n):
        return slots.at[pl.ds(slot_dev * k, slot_dev), n]

    slots[pl.ds(slot_dev * p.z, slot_dev), p.n] = weight_ref[...].astype(bf16)
    greet(p, depth, peers)
    going = []
    order = []

    def arrive(j):
        k = jnp.int32(0)
        for z in range(depth):
            k = k + jnp.where(p.z == z, ORDER[z][j], 0)
        order.append(k)
        piece = buf(k, p.n)
        if j:
            remote(piece, piece, zssem.at[0, k], zrsem.at[k], p.z, p.n).wait_recv()
        for i, test, to in (
            (0, (k <= p.z) & (p.z < depth - 1), p.z + 1),
            (1, (k >= p.z) & (p.z > 0), p.z - 1),
        ):
            copy = remote(piece, piece, zssem.at[i, k], zrsem.at[k], to, p.n)
            pl.when(test)(copy.start)
            going.append((copy, test))
        going.extend((copy, None) for copy in gather_start(p, buf, k, (ssem, rsem)))

    def side(j):
        going.extend((copy, None) for copy in gather_side(p, buf, order[j], (ssem, rsem)))

    def far(j):
        going.extend((copy, None) for copy in gather_far(p, buf, order[j], (ssem, rsem)))

    arrive(0)
    ids = lax.broadcasted_iota(jnp.int32, (nodes, per_peer * peers), 0)
    pick_t = jnp.where(ids == send_rows_ref[...], 1.0, 0.0).astype(bf16)
    for t in range(roll):
        hout32[:, t] = dot_ta(pick_t, node_ref[0, t]).reshape(peers, per_peer, width)
    hout[...] = hout32[...].reshape(peers, roll * per_peer, width).astype(bf16)
    halo[p.n] = hout[p.n]
    for s in range(slot_dev):
        for m in range(peers):
            left_b[s, m] = left_ref[s, m * rows : (m + 1) * rows].T.astype(bf16)
    left_t[:, p.n] = left_b[:, p.n]
    for k in range(1, peers):
        to = lax.rem(p.n + k, peers)
        for copy in (
            remote(hout.at[to], halo.at[p.n], hssem.at[k], hrsem.at[k], p.z, to),
            remote(left_b.at[:, to], left_t.at[:, p.n], lssem.at[k], lrsem.at[k], p.z, to),
        ):
            copy.start()
            going.append((copy, None))

    arrive(1)
    side(0)
    arrive(2)
    side(1)
    far(0)
    arrive(3)
    side(2)
    far(1)
    side(3)
    far(2)
    far(3)
    for j in range(depth):
        gather_end(p, buf, order[j], (ssem, rsem))
    for k in range(1, peers):
        remote(hout.at[0], halo.at[0], hssem.at[k], hrsem.at[k], p.z, p.sib).wait_recv()
        remote(left_b.at[:, 0], left_t.at[:, 0], lssem.at[k], lrsem.at[k], p.z, p.sib).wait_recv()
    for copy, test in going:
        if test is None:
            copy.wait_send()
        else:
            pl.when(test)(copy.wait_send)


def prepare(weight_slots, node_state, send_rows, basis_left):
    depth, peers = 4, 8
    _, roll, nodes, width = node_state.shape
    slot_dev, rows = weight_slots.shape[:2]
    per_peer = send_rows.shape[1] // peers
    vmem = pl.BlockSpec(memory_space=pltpu.VMEM)
    shape = jax.ShapeDtypeStruct
    dma = pltpu.SemaphoreType.DMA
    slots, halo, left_t = pl.pallas_call(
        prepare_kernel,
        out_shape=(
            shape((slot_dev * depth, peers, rows, width), bf16),
            shape((peers, roll * per_peer, width), bf16),
            shape((slot_dev, peers, rows, rows), bf16),
        ),
        in_specs=[vmem] * 4,
        out_specs=(vmem, vmem, vmem),
        scratch_shapes=[
            pltpu.VMEM((peers, roll, per_peer, width), f32),
            pltpu.VMEM((peers, roll * per_peer, width), bf16),
            pltpu.VMEM((slot_dev, peers, rows, rows), bf16),
            dma((7, depth)),
            dma((7, depth)),
            dma((2, depth)),
            dma((depth,)),
            dma((peers,)),
            dma((peers,)),
            dma((peers,)),
            dma((peers,)),
        ],
        compiler_params=pltpu.CompilerParams(
            vmem_limit_bytes=40 << 20, collective_id=0, has_side_effects=True
        ),
        name="prepare",
    )(weight_slots, node_state, send_rows, basis_left)
    return (
        slots.reshape(slot_dev * depth, width, width),
        halo.reshape(peers * roll * per_peer, width),
        left_t.reshape(slot_dev, width, rows),
    )


def update_kernel(
    slot_block_ref,
    step_ref,
    grad_ref,
    gvec_ref,
    hback_ref,
    nbase_ref,
    send_rows_ref,
    weight_ref,
    first_ref,
    second_ref,
    left_ref,
    right_ref,
    left_t_ref,
    vec_ref,
    vfirst_ref,
    vsecond_ref,
    ngrad_ref,
    mone_ref,
    mtwo_ref,
    wnew_ref,
    wcopy_ref,
    vstate_ref,
    norm_ref,
    cast,
    got_core,
    put_one,
    keep_one,
    got_one,
    put_two,
    keep_two,
    got_two,
    plane,
    put_up,
    put_down,
    got_up,
    got_down,
    full,
    turned,
    hret,
    vput,
    vgot,
    vz,
    sput,
    sgot,
    szput,
    sz,
    ssem,
    rsem,
    gssem,
    grsem,
    tssem,
    trsem,
    zssem,
    zrsem,
    hssem,
    hrsem,
    vssem,
    vrsem,
    nssem,
    nrsem,
):
    p = Place()
    depth, peers = 4, 8
    slot_dev, rows, width = weight_ref.shape
    roll = ngrad_ref.shape[1]
    nodes = ngrad_ref.shape[2]
    per_peer = hback_ref.shape[1] // roll
    on_f = jnp.where(p.c == 0, p.x, p.y)
    on_g = jnp.where(p.c == 0, p.y, p.x)
    to_f = jnp.where(p.c == 0, p.xn, p.yn)
    to_g = jnp.where(p.c == 0, p.yn, p.xn)
    going = []

    def launch(src, dst, send, recv, z, n):
        copy = remote(src, dst, send, recv, z, n)
        copy.start()
        going.append((copy, None))

    def landed(dst, recv):
        remote(dst, dst, recv, recv, p.z, p.sib).wait_recv()

    greet(p, depth, peers)

    def to_core(b):
        cast[b] = grad_ref[b].reshape(peers // 2, 2, rows, width).astype(bf16)
        launch(cast.at[b, :, 1 - p.c], got_core.at[b], ssem.at[0, b], rsem.at[0, b], p.z, p.sib)

    def to_first(b):
        landed(got_core.at[b], rsem.at[0, b])
        for f in range(2):
            for g in range(2):
                at = jnp.where(p.c == 0, g * 2 + f, f * 2 + g)
                own = grad_ref[b, at * 2 + p.c]
                total = own + got_core[b, at].astype(f32)
                put_one[b, f, g] = total.astype(bf16)

                @pl.when(on_f == f)
                def _():
                    keep_one[b, g] = total

        launch(put_one.at[b, 1 - on_f], got_one.at[b], ssem.at[1, b], rsem.at[1, b], p.z, to_f)

    def to_second(b):
        landed(got_one.at[b], rsem.at[1, b])
        put_two[b] = (keep_one[b, 1 - on_g] + got_one[b, 1 - on_g].astype(f32)).astype(bf16)
        launch(put_two.at[b], got_two.at[b], ssem.at[2, b], rsem.at[2, b], p.z, to_g)
        keep_two[b] = keep_one[b, on_g] + got_one[b, on_g].astype(f32)

    def settle(b):
        landed(got_two.at[b], rsem.at[2, b])
        plane[b] = keep_two[b] + got_two[b].astype(f32)

    for k in range(1, peers):
        to = lax.rem(p.n + k, peers)
        launch(hback_ref.at[to], hret.at[p.n], hssem.at[k], hrsem.at[k], p.z, to)
    hret[p.n] = hback_ref[p.n]
    vput[0] = gvec_ref[...]
    launch(vput.at[0], vgot.at[0], vssem.at[0], vrsem.at[0], p.z, p.sib)
    plane[NBLOCK] = jnp.zeros((rows, width), f32)
    blocks = (6, 4, 5, 3, 0, 1, 2)
    for i in range(NBLOCK + 3):
        if i < NBLOCK:
            to_core(blocks[i])
        if 0 <= i - 1 < NBLOCK:
            to_first(blocks[i - 1])
        if 0 <= i - 2 < NBLOCK:
            to_second(blocks[i - 2])
        if 0 <= i - 3 < NBLOCK:
            settle(blocks[i - 3])
        if i == 1:
            landed(vgot.at[0], vrsem.at[0])
            vput[1] = vput[0] + vgot[0]
            launch(vput.at[1], vgot.at[1], vssem.at[1], vrsem.at[1], p.z, p.xn)
        if i == 3:
            landed(vgot.at[1], vrsem.at[1])
            vput[2] = vput[1] + vgot[1]
            launch(vput.at[2], vgot.at[2], vssem.at[2], vrsem.at[2], p.z, p.yn)
        if i == 5:
            landed(vgot.at[2], vrsem.at[2])
            vz[p.z] = vput[2] + vgot[2]
            vput[3] = vput[2] + vgot[2]
            for k in range(1, depth):
                to = lax.rem(p.z + k, depth)
                launch(vput.at[3], vz.at[p.z], vssem.at[2 + k], vrsem.at[2 + k], to, p.n)

    def slot_sum(s):
        return plane[jnp.minimum(slot_block_ref[s], NBLOCK)]

    def part(target, s):
        return slot_sum(target * slot_dev + s)

    def pass_on(way):
        put, got = (put_up, got_up) if way == 0 else (put_down, got_down)
        source = p.z > 0 if way == 0 else p.z < depth - 1
        for i in range(depth - 1):
            target = depth - 1 - i if way == 0 else i
            test = p.z < target if way == 0 else p.z > target
            at = p.z + 1 if way == 0 else p.z - 1

            @pl.when(test)
            def _():
                for s in range(slot_dev):

                    @pl.when(source)
                    def _():
                        landed(got.at[target, s], zrsem.at[way, target, s])
                        total = part(target, s) + got[target, s].astype(f32)
                        put[target, s] = total.astype(bf16)

                    @pl.when(jnp.logical_not(source))
                    def _():
                        put[target, s] = part(target, s).astype(bf16)

                    remote(
                        put.at[target, s],
                        got.at[target, s],
                        zssem.at[way, target, s],
                        zrsem.at[way, target, s],
                        at,
                        p.n,
                    ).start()

    @pl.when(p.z < depth // 2)
    def _():
        pass_on(0)
        pass_on(1)

    @pl.when(p.z >= depth // 2)
    def _():
        pass_on(1)
        pass_on(0)

    for k in range(1, peers):
        landed(hret.at[0], hrsem.at[k])
    ids = lax.broadcasted_iota(jnp.int32, (nodes, per_peer * peers), 0)
    pick_t = jnp.where(ids == send_rows_ref[...], 1.0, 0.0).astype(bf16)
    back = hret[...].astype(f32).reshape(peers, roll, per_peer, width)
    for t in range(roll):
        rows_t = back[:, t].reshape(peers * per_peer, width).astype(bf16)
        ngrad_ref[0, t] = (nbase_ref[t * nodes : (t + 1) * nodes] + dot(pick_t, rows_t)).astype(bf16)

    own = []
    square = jnp.zeros((8, width), f32)
    for s in range(slot_dev):
        mine = slot_sum(p.z * slot_dev + s)

        @pl.when(p.z > 0)
        def _():
            landed(got_up.at[p.z, s], zrsem.at[0, p.z, s])

        @pl.when(p.z < depth - 1)
        def _():
            landed(got_down.at[p.z, s], zrsem.at[1, p.z, s])

        mine = mine + jnp.where(p.z > 0, got_up[p.z, s].astype(f32), 0.0)
        mine = mine + jnp.where(p.z < depth - 1, got_down[p.z, s].astype(f32), 0.0)
        full[s, p.n] = mine.astype(bf16)
        for copy in gather_start(p, lambda k, n: full.at[k, n], s, (gssem, grsem)):
            going.append((copy, None))
        square = square + eights(mine * mine)
    square = square[:, :128] + square[:, 128:256] + square[:, 256:384] + square[:, 384:]
    sput[...] = square
    sgot[p.n] = square
    for k in range(1, peers):
        to = lax.rem(p.n + k, peers)
        launch(sput, sgot.at[p.n], nssem.at[k], nrsem.at[k], p.z, to)

    def collect(buf, sems, finish):
        for s in range(slot_dev):
            going.extend((copy, None) for copy in gather_side(p, buf, s, sems))
        for s in range(slot_dev):
            going.extend((copy, None) for copy in gather_far(p, buf, s, sems))
        for s in range(slot_dev):
            gather_end(p, buf, s, sems)
            finish(s)

    for k in range(1, peers):
        landed(sgot.at[0], nrsem.at[k])
    szput[...] = jnp.sum(sgot[...], axis=0)
    sz[p.z] = szput[...]
    for k in range(1, depth):
        to = lax.rem(p.z + k, depth)
        launch(szput, sz.at[p.z], nssem.at[peers - 1 + k], nrsem.at[peers - 1 + k], to, p.n)

    rotated = [None] * slot_dev

    def rotate(s):
        part_left = dot_ta(left_ref[s].astype(bf16), full[s].reshape(width, width))
        rotated[s] = dot(part_left.astype(bf16), right_ref[s].astype(bf16))

    collect(lambda k, n: full.at[k, n], (gssem, grsem), rotate)
    for k in range(1, depth):
        landed(vz.at[0], vrsem.at[2 + k])
        landed(sz.at[0], nrsem.at[peers - 1 + k])
    grad_vectors = vz[0] + vz[1] + vz[2] + vz[3]
    square_sum = jnp.sum(sz[0] + sz[1] + sz[2] + sz[3], keepdims=True).reshape(1, 1)
    square_sum = square_sum + jnp.sum(grad_vectors * grad_vectors, keepdims=True).reshape(1, 1)
    grad_norm = jnp.sqrt(square_sum)
    norm_ref[...] = jnp.broadcast_to(grad_norm, norm_ref.shape)
    limit = math.sqrt(NBLOCK * width * width + 8 * width)
    clip = jnp.minimum(1.0, limit / grad_norm)

    def fix(beta, step):
        return 1.0 - jnp.exp2(math.log2(beta) * jnp.full((1, 1), step, jnp.int32).astype(f32))

    tbuf = lambda k, n: turned.at[k, n]
    for s in range(slot_dev):
        step = step_ref[p.z * slot_dev + s]
        spun = rotated[s] * clip
        one = beta_first * first_ref[s] + (1.0 - beta_first) * spun
        two = beta_second * second_ref[s] + (1.0 - beta_second) * spun * spun
        mone_ref[s] = one
        mtwo_ref[s] = two
        direction = adam_direction(one, two, fix(beta_first, step), fix(beta_second, step))
        turned[s, p.n] = dot_tb(direction.astype(bf16), right_ref[s].astype(bf16)).astype(bf16)
        for copy in gather_start(p, tbuf, s, (tssem, trsem)):
            going.append((copy, None))

    step = step_ref[depth * slot_dev]
    spun = grad_vectors * clip
    one = beta_first * vfirst_ref[...] + (1.0 - beta_first) * spun
    two = beta_second * vsecond_ref[...] + (1.0 - beta_second) * spun * spun
    vstate_ref[0] = vec_ref[...] - rate_vector * adam_direction(
        one, two, fix(beta_first, step), fix(beta_second, step)
    )
    vstate_ref[1] = one
    vstate_ref[2] = two

    def finish(s):
        reverted = dot_ta(left_t_ref[s], turned[s].reshape(width, width))
        new = weight_ref[s] - rate_matrix * (reverted + weight_decay * weight_ref[s])
        wnew_ref[s] = new
        wcopy_ref[s] = new.astype(bf16)

    collect(tbuf, (tssem, trsem), finish)

    for copy, _ in going:
        copy.wait_send()
    for i in range(depth - 1):
        for s in range(slot_dev):
            for test, target, way, put in (
                (p.z < depth - 1 - i, depth - 1 - i, 0, put_up),
                (p.z > i, i, 1, put_down),
            ):
                sent = remote(
                    put.at[target, s],
                    put.at[target, s],
                    zssem.at[way, target, s],
                    zrsem.at[way, target, s],
                    p.z,
                    p.sib,
                )
                pl.when(test)(sent.wait_send)


def update(
    slot_block,
    step_count,
    grads,
    grad_vectors,
    halo_back,
    node_base,
    send_rows,
    weight_slots,
    moment_first,
    moment_second,
    basis_left,
    basis_right,
    left_t,
    vector_params,
    vector_first,
    vector_second,
    node_shape,
):
    depth, peers = 4, 8
    slot_dev, rows, width = weight_slots.shape
    vmem = pl.BlockSpec(memory_space=pltpu.VMEM)
    smem = pl.BlockSpec(memory_space=pltpu.SMEM)
    shape = jax.ShapeDtypeStruct
    dma = pltpu.SemaphoreType.DMA
    own = (slot_dev, rows, width)
    tile = (8, 128)
    *results, norm = pl.pallas_call(
        update_kernel,
        out_shape=(
            shape(node_shape, bf16),
            shape(own, f32),
            shape(own, f32),
            shape(own, f32),
            shape(own, bf16),
            shape((3, 8, width), f32),
            shape(tile, f32),
        ),
        in_specs=[smem] * 2 + [vmem] * 14,
        out_specs=(vmem,) * 7,
        scratch_shapes=[
            pltpu.VMEM((NBLOCK, peers // 2, 2, rows, width), bf16),
            pltpu.VMEM((NBLOCK, peers // 2, rows, width), bf16),
            pltpu.VMEM((NBLOCK, 2, 2, rows, width), bf16),
            pltpu.VMEM((NBLOCK, 2, rows, width), f32),
            pltpu.VMEM((NBLOCK, 2, rows, width), bf16),
            pltpu.VMEM((NBLOCK, rows, width), bf16),
            pltpu.VMEM((NBLOCK, rows, width), f32),
            pltpu.VMEM((NBLOCK, rows, width), bf16),
            pltpu.VMEM((NBLOCK + 1, rows, width), f32),
            pltpu.VMEM((depth, *own), bf16),
            pltpu.VMEM((depth, *own), bf16),
            pltpu.VMEM((depth, *own), bf16),
            pltpu.VMEM((depth, *own), bf16),
            pltpu.VMEM((slot_dev, peers, rows, width), bf16),
            pltpu.VMEM((slot_dev, peers, rows, width), bf16),
            pltpu.VMEM((peers, halo_back.shape[0] // peers, width), bf16),
            pltpu.VMEM((4, 8, width), f32),
            pltpu.VMEM((3, 8, width), f32),
            pltpu.VMEM((depth, 8, width), f32),
            pltpu.VMEM(tile, f32),
            pltpu.VMEM((peers, *tile), f32),
            pltpu.VMEM(tile, f32),
            pltpu.VMEM((depth, *tile), f32),
            dma((3, NBLOCK)),
            dma((3, NBLOCK)),
            dma((7, slot_dev)),
            dma((7, slot_dev)),
            dma((7, slot_dev)),
            dma((7, slot_dev)),
            dma((2, depth, slot_dev)),
            dma((2, depth, slot_dev)),
            dma((peers,)),
            dma((peers,)),
            dma((6,)),
            dma((6,)),
            dma((peers + depth - 1,)),
            dma((peers + depth - 1,)),
        ],
        compiler_params=pltpu.CompilerParams(
            vmem_limit_bytes=50 << 20, collective_id=1, has_side_effects=True
        ),
        name="update",
    )(
        slot_block,
        step_count,
        grads.reshape(NBLOCK, peers, rows, width),
        grad_vectors,
        halo_back.reshape(peers, -1, width),
        node_base,
        send_rows,
        weight_slots,
        moment_first,
        moment_second,
        basis_left,
        basis_right,
        left_t,
        vector_params,
        vector_first,
        vector_second,
    )
    return *results, norm[0, :1]


def local(
    node_state,
    edge_state,
    node_cotangent,
    edge_cotangent,
    send_rows,
    edge_sender,
    edge_receiver,
    rollout_length,
    slot_block,
    step_count,
    weight_slots,
    moment_first,
    moment_second,
    basis_left,
    basis_right,
    vector_params,
    vector_first,
    vector_second,
):
    width = node_state.shape[-1]
    roll, nodes = node_state.shape[1:3]
    clip_limit = math.sqrt(NBLOCK * width * width + 8 * width)
    slot_dev = weight_slots.shape[0]
    slot_total = slot_block.shape[0]
    halo_rows = send_rows.shape[1]
    peers = lax.axis_size("node")
    per_peer = halo_rows // peers
    if (lax.axis_size("dp"), peers) == (4, 8):
        slots, halo, left_t = prepare(weight_slots, node_state, send_rows, basis_left)
        node_output, edge_output, node_base, edge_gradient, grads, grad_vectors, halo_back = layer(
            rollout_length,
            slot_block,
            node_state,
            edge_state,
            node_cotangent,
            edge_cotangent,
            edge_sender,
            edge_receiver,
            halo,
            slots,
            vector_params,
            per_peer,
        )
        node_gradient, *results = update(
            slot_block,
            step_count,
            grads,
            grad_vectors,
            halo_back,
            node_base,
            send_rows,
            weight_slots,
            moment_first,
            moment_second,
            basis_left,
            basis_right,
            left_t,
            vector_params,
            vector_first,
            vector_second,
            node_state.shape,
        )
        return node_output, edge_output, node_gradient, edge_gradient, *results
    copies = lax.all_gather(weight_slots.astype(bf16), "node", axis=1, tiled=True)
    slots = lax.all_gather(copies, "dp", axis=0, tiled=True)
    back_onehot = (send_rows[0][:, None] == jnp.arange(nodes, dtype=jnp.int32)[None, :]).astype(bf16)
    outgoing = jnp.einsum("hk,tkd->htd", back_onehot, node_state[0], preferred_element_type=f32)
    outgoing = outgoing.astype(bf16).reshape(peers, per_peer, roll, width).transpose(0, 2, 1, 3)
    outgoing = outgoing.reshape(peers * roll * per_peer, width)
    halo = lax.all_to_all(outgoing, "node", split_axis=0, concat_axis=0, tiled=True)

    node_output, edge_output, node_base, edge_gradient, grads, grad_vectors, halo_back = layer(
        rollout_length,
        slot_block,
        node_state,
        edge_state,
        node_cotangent,
        edge_cotangent,
        edge_sender,
        edge_receiver,
        halo,
        slots,
        vector_params,
        per_peer,
    )
    returned = lax.all_to_all(halo_back, "node", split_axis=0, concat_axis=0, tiled=True)
    returned = returned.reshape(peers, roll, per_peer, width).transpose(0, 2, 1, 3)
    d_back = jnp.einsum(
        "hk,htd->tkd",
        back_onehot,
        returned.reshape(halo_rows, roll, width),
        preferred_element_type=f32,
    )
    node_gradient = node_base.reshape(roll, nodes, width) + d_back
    node_gradient = node_gradient.astype(bf16).reshape(node_state.shape)

    block_of_slot = slot_block[None, :] == jnp.arange(NBLOCK, dtype=jnp.int32)[:, None]
    first = lax.axis_index("dp") * slot_dev
    summed, grad_vectors = lax.psum((grads, grad_vectors), ("dp", "node"))
    own_square = jnp.sum(summed * summed)
    mine = lax.dynamic_slice_in_dim(block_of_slot.astype(f32), first, slot_dev, 1)
    owned_grads = jnp.einsum("bs,bij->sij", mine, summed, precision=highest)
    square_sum = own_square + jnp.sum(grad_vectors * grad_vectors)
    grad_norm = jnp.sqrt(square_sum)
    clip_scale = jnp.minimum(1.0, clip_limit / grad_norm)
    owned_grads = owned_grads * clip_scale
    grad_vectors = grad_vectors * clip_scale
    own_steps = lax.dynamic_slice_in_dim(step_count, first, slot_dev, 0)
    slot_steps = own_steps.astype(f32)[:, None, None]
    fix_one = 1.0 - jnp.power(f32(beta_first), slot_steps)
    fix_two = 1.0 - jnp.power(f32(beta_second), slot_steps)
    rotated = jnp.einsum("sij,sik->sjk", basis_left, owned_grads, precision=highest, preferred_element_type=f32)
    rotated = jnp.einsum("sjk,skl->sjl", rotated, basis_right, precision=highest, preferred_element_type=f32)
    moment_one = beta_first * moment_first + (1.0 - beta_first) * rotated
    moment_two = beta_second * moment_second + (1.0 - beta_second) * rotated * rotated
    direction = adam_direction(moment_one, moment_two, fix_one, fix_two)
    turned = jnp.einsum("sjl,sml->sjm", direction, basis_right, precision=highest, preferred_element_type=f32)
    reverted = jnp.einsum("sij,sjm->ism", basis_left, turned, precision=highest, preferred_element_type=f32)
    reverted = lax.psum_scatter(reverted.astype(bf16), "node", scatter_dimension=0, tiled=True).astype(f32)
    reverted = jnp.transpose(reverted, (1, 0, 2))
    new_weights = weight_slots - rate_matrix * (reverted + weight_decay * weight_slots)
    vec_step = step_count[slot_total].astype(f32)
    vfix_one = 1.0 - jnp.power(f32(beta_first), vec_step)
    vfix_two = 1.0 - jnp.power(f32(beta_second), vec_step)
    vec_one = beta_first * vector_first + (1.0 - beta_first) * grad_vectors
    vec_two = beta_second * vector_second + (1.0 - beta_second) * grad_vectors * grad_vectors
    vec_new = vector_params - rate_vector * adam_direction(vec_one, vec_two, vfix_one, vfix_two)
    vector_state = jnp.stack([vec_new, vec_one, vec_two])
    return (
        node_output,
        edge_output,
        node_gradient,
        edge_gradient,
        moment_one,
        moment_two,
        new_weights,
        new_weights.astype(bf16),
        vector_state,
        grad_norm.reshape(1),
    )


def solution(mesh):
    in_specs = (
        P("dp", None, "node", None),
        P("dp", None, "node", None),
        P("dp", None, "node", None),
        P("dp", None, "node", None),
        P("node", None),
        P("node"),
        P("node"),
        P("dp"),
        P(),
        P(),
        P("dp", "node", None),
        P("dp", "node", None),
        P("dp", "node", None),
        P("dp", None, "node"),
        P("dp", None, None),
        P(),
        P(),
        P(),
    )
    out_specs = (
        P("dp", None, "node", None),
        P("dp", None, "node", None),
        P("dp", None, "node", None),
        P("dp", None, "node", None),
        P("dp", "node", None),
        P("dp", "node", None),
        P("dp", "node", None),
        P("dp", "node", None),
        P(),
        P(),
    )
    return jax.shard_map(local, mesh=mesh, in_specs=in_specs, out_specs=out_specs, check_vma=False)
```

```python
import functools
import math

import jax
import jax.numpy as jnp
from jax import lax
from jax.experimental import pallas as pl
from jax.experimental.pallas import tpu as pltpu
from jax.sharding import PartitionSpec as P

NBLOCK = 7
f32 = jnp.float32
bf16 = jnp.bfloat16
highest = lax.Precision.HIGHEST
norm_epsilon = 1e-05
adam_epsilon = 1e-08
beta_first = 0.5
beta_second = 0.5
rate_matrix = 0.03
rate_vector = 0.4
weight_decay = 0.01


def dot(a, b):
    return jnp.dot(a, b, preferred_element_type=f32)


def dot_tb(a, b):
    return lax.dot_general(a, b, (((1,), (1,)), ((), ())), preferred_element_type=f32)


def dot_ta(a, b):
    return lax.dot_general(a, b, (((0,), (0,)), ((), ())), preferred_element_type=f32)


def eights(x):
    return jnp.sum(x.reshape(x.shape[0] // 8, 8, x.shape[1]), axis=0)


def sigmoid(z):
    return 0.5 * jnp.tanh(0.5 * z) + 0.5


def branch_forward(z, w_out, bias_out):
    s = sigmoid(z)
    h = z * s
    slope = s + h * (1.0 - s)
    hidden = h.astype(bf16)
    after = dot(hidden, w_out) + bias_out
    center = after - jnp.mean(after, axis=1, keepdims=True)
    spread = jnp.mean(center * center, axis=1, keepdims=True)
    inverse = lax.rsqrt(spread + norm_epsilon)
    return hidden, slope, center * inverse, inverse


def norm_backward(upstream, normed, inverse, gain):
    u = upstream * gain
    first = jnp.mean(u, axis=1, keepdims=True)
    second = jnp.mean(u * normed, axis=1, keepdims=True)
    return (inverse * (u - first - normed * second)).astype(bf16)


def layer_kernel(
    rollout_ref,
    slot_block_ref,
    node_hbm,
    edge_hbm,
    ncot_hbm,
    ecot_hbm,
    sender_ref,
    receiver_ref,
    halo_ref,
    w_ref,
    vec_ref,
    nout_ref,
    eout_hbm,
    nbase_ref,
    egrad_hbm,
    grad_ref,
    gvec_ref,
    hback_ref,
    node_v,
    edge_v,
    ncot_v,
    ecot_v,
    eout_v,
    egrad_v,
    gather_t,
    gather,
    table,
    hidden_v,
    slope_v,
    normed_v,
    inv_v,
    dz_v,
    da_v,
    summed_v,
    dsum_v,
    sc_own,
    sc_recv,
    sc_halo,
    acc,
    sem_in,
    sem_out,
):
    roll, nodes, width = node_v.shape
    edges = edge_v.shape[1]
    peers, per_peer = sc_halo.shape[0], sc_halo.shape[2]
    halo = peers * per_peer
    known = nodes + halo
    padded = table.shape[1]
    chunk = 256
    pieces = edges // chunk

    copies = []
    for i, (src, dst) in enumerate(
        ((node_hbm, node_v), (edge_hbm, edge_v), (ncot_hbm, ncot_v), (ecot_hbm, ecot_v))
    ):
        copies.append(pltpu.make_async_copy(src.at[0], dst, sem_in.at[i]))
        copies[-1].start()

    slot_of = []
    for b in range(NBLOCK):
        found = jnp.int32(0)
        for s in range(slot_block_ref.shape[0]):
            found = jnp.where(slot_block_ref[s] == b, jnp.int32(s), found)
        slot_of.append(found)

    def weight(b):
        return w_ref[slot_of[b]]

    def live(t):
        return jnp.where(t < rollout_ref[0], 1.0, 0.0).astype(f32)

    ids = lax.broadcasted_iota(jnp.int32, (padded, edges), 0)
    onehot = (ids == sender_ref[...]) | (ids == receiver_ref[...] + known)
    onehot = jnp.where(onehot, 1.0, 0.0).astype(f32)
    gather_t[...] = onehot.astype(bf16)
    gather[...] = onehot.T.astype(bf16)
    table[...] = jnp.zeros_like(table)
    acc[...] = jnp.zeros_like(acc)

    copies[0].wait()
    flat_nodes = node_v[...].reshape(roll * nodes, width)
    own_sent = dot(flat_nodes, weight(1))
    own_recv = dot(flat_nodes, weight(2))
    halo_sent = dot(halo_ref[...], weight(1)).reshape(peers, roll, per_peer, width)
    for t in range(roll):
        table[t, :nodes] = own_sent[t * nodes : (t + 1) * nodes].astype(bf16)
        table[t, nodes:known] = halo_sent[:, t].reshape(halo, width).astype(bf16)
        table[t, known : known + nodes] = own_recv[t * nodes : (t + 1) * nodes].astype(bf16)
    copies[1].wait()

    def forward(t, carry):
        lv = live(t)
        total = jnp.zeros((nodes, width), f32)
        for c in range(pieces):
            rows = pl.ds(c * chunk, chunk)
            edge = edge_v[t, rows]
            z = dot(edge, weight(0)) + dot(gather[rows], table[t]) + vec_ref[0:1]
            hidden, slope, normed, inverse = branch_forward(z, weight(3), vec_ref[1:2])
            hidden_v[t, rows] = hidden
            slope_v[t, rows] = slope.astype(bf16)
            normed_v[t, rows] = normed.astype(bf16)
            inv_v[t, rows] = inverse
            new = edge.astype(f32) + (normed * vec_ref[2:3] + vec_ref[3:4])
            eout_v[t, rows] = (new * lv).astype(bf16)
            total += dot(gather_t[known : known + nodes, rows], new.astype(bf16))
        summed_v[pl.ds(t * nodes, nodes)] = total.astype(bf16)
        pltpu.make_async_copy(eout_v.at[t], eout_hbm.at[0, t], sem_out.at[t]).start()
        return carry

    lax.fori_loop(0, roll, forward, 0)

    flat_nodes = node_v[...].reshape(roll * nodes, width)
    summed = summed_v[...]
    z = dot(flat_nodes, weight(4)) + dot(summed, weight(5)) + vec_ref[4:5]
    hidden, slope, normed, inverse = branch_forward(z, weight(6), vec_ref[5:6])
    row_t = lax.broadcasted_iota(jnp.int32, (roll * nodes, 1), 0) // nodes
    row_live = jnp.where(row_t < rollout_ref[0], 1.0, 0.0).astype(f32)
    new = flat_nodes.astype(f32) + (normed * vec_ref[6:7] + vec_ref[7:8])
    nout_ref[0] = (new * row_live).astype(bf16).reshape(roll, nodes, width)
    copies[2].wait()
    d_new = ncot_v[...].reshape(roll * nodes, width).astype(f32) * row_live
    acc[6] += eights(d_new * normed)
    acc[7] += eights(d_new)
    d_after = norm_backward(d_new, normed, inverse, vec_ref[6:7])
    acc[5] += eights(d_after.astype(f32))
    grad_ref[6] = dot_ta(hidden, d_after)
    d_before = (dot_tb(d_after, weight(6)) * slope).astype(bf16)
    acc[4] += eights(d_before.astype(f32))
    grad_ref[4] = dot_ta(flat_nodes, d_before)
    grad_ref[5] = dot_ta(summed, d_before)
    dsum_v[...] = dot_tb(d_before, weight(5)).astype(bf16)
    nbase_ref[...] = d_new + dot_tb(d_before, weight(4))
    grad_ref[0] = jnp.zeros((width, width), f32)
    grad_ref[3] = jnp.zeros((width, width), f32)
    copies[3].wait()

    def backward(t, carry):
        lv = live(t)
        for c in range(pieces):
            rows = pl.ds(c * chunk, chunk)
            d_new = ecot_v[t, rows].astype(f32) * lv + dot(
                gather[rows, known : known + nodes], dsum_v[pl.ds(t * nodes, nodes)]
            )
            normed = normed_v[t, rows].astype(f32)
            acc[2] += eights(d_new * normed)
            acc[3] += eights(d_new)
            d_after = norm_backward(d_new, normed, inv_v[t, rows], vec_ref[2:3])
            acc[1] += eights(d_after.astype(f32))
            da_v[rows] = d_after
            d_before = (dot_tb(d_after, weight(3)) * slope_v[t, rows].astype(f32)).astype(bf16)
            acc[0] += eights(d_before.astype(f32))
            dz_v[rows] = d_before
            egrad_v[t, rows] = (d_new + dot_tb(d_before, weight(0))).astype(bf16)
        pltpu.make_async_copy(egrad_v.at[t], egrad_hbm.at[0, t], sem_out.at[roll + t]).start()
        grad_ref[3] += dot_ta(hidden_v[t], da_v[...])
        grad_ref[0] += dot_ta(edge_v[t], dz_v[...])
        scattered = dot(gather_t[...], dz_v[...])
        sc_own[pl.ds(t * nodes, nodes)] = scattered[:nodes].astype(bf16)
        sc_recv[pl.ds(t * nodes, nodes)] = scattered[known : known + nodes].astype(bf16)
        sc_halo[:, t] = scattered[nodes:known].reshape(peers, per_peer, width)
        return carry

    lax.fori_loop(0, roll, backward, 0)

    halo_sum = sc_halo[...].reshape(roll * halo, width).astype(bf16)
    grad_ref[1] = dot_ta(flat_nodes, sc_own[...]) + dot_ta(halo_ref[...], halo_sum)
    grad_ref[2] = dot_ta(flat_nodes, sc_recv[...])
    hback_ref[...] = dot_tb(halo_sum, weight(1)).astype(bf16)
    nbase_ref[...] += dot_tb(sc_own[...], weight(1)) + dot_tb(sc_recv[...], weight(2))
    gvec_ref[...] = jnp.sum(acc[...], axis=1)

    for t in range(roll):
        pltpu.make_async_copy(eout_v.at[t], eout_hbm.at[0, t], sem_out.at[t]).wait()
        pltpu.make_async_copy(egrad_v.at[t], egrad_hbm.at[0, t], sem_out.at[roll + t]).wait()


def layer(
    rollout_length,
    slot_block,
    node_state,
    edge_state,
    node_cotangent,
    edge_cotangent,
    edge_sender,
    edge_receiver,
    halo,
    slots,
    vector_params,
    per_peer,
):
    _, roll, nodes, width = node_state.shape
    edges = edge_state.shape[2]
    peers = halo.shape[0] // (roll * per_peer)
    known = nodes + peers * per_peer
    padded = -(-(known + nodes) // 128) * 128
    vmem = pl.BlockSpec(memory_space=pltpu.VMEM)
    smem = pl.BlockSpec(memory_space=pltpu.SMEM)
    hbm = pl.BlockSpec(memory_space=pl.ANY)
    shape = jax.ShapeDtypeStruct
    return pl.pallas_call(
        layer_kernel,
        out_shape=(
            shape(node_state.shape, bf16),
            shape(edge_state.shape, bf16),
            shape((roll * nodes, width), f32),
            shape(edge_state.shape, bf16),
            shape((NBLOCK, width, width), f32),
            shape((8, width), f32),
            shape(halo.shape, bf16),
        ),
        in_specs=[smem, smem, hbm, hbm, hbm, hbm, vmem, vmem, vmem, vmem, vmem],
        out_specs=(vmem, hbm, vmem, hbm, vmem, vmem, vmem),
        scratch_shapes=[
            pltpu.VMEM((roll, nodes, width), bf16),
            pltpu.VMEM((roll, edges, width), bf16),
            pltpu.VMEM((roll, nodes, width), bf16),
            pltpu.VMEM((roll, edges, width), bf16),
            pltpu.VMEM((roll, edges, width), bf16),
            pltpu.VMEM((roll, edges, width), bf16),
            pltpu.VMEM((padded, edges), bf16),
            pltpu.VMEM((edges, padded), bf16),
            pltpu.VMEM((roll, padded, width), bf16),
            pltpu.VMEM((roll, edges, width), bf16),
            pltpu.VMEM((roll, edges, width), bf16),
            pltpu.VMEM((roll, edges, width), bf16),
            pltpu.VMEM((roll, edges, 1), f32),
            pltpu.VMEM((edges, width), bf16),
            pltpu.VMEM((edges, width), bf16),
            pltpu.VMEM((roll * nodes, width), bf16),
            pltpu.VMEM((roll * nodes, width), bf16),
            pltpu.VMEM((roll * nodes, width), bf16),
            pltpu.VMEM((roll * nodes, width), bf16),
            pltpu.VMEM((peers, roll, per_peer, width), f32),
            pltpu.VMEM((8, 8, width), f32),
            pltpu.SemaphoreType.DMA((4,)),
            pltpu.SemaphoreType.DMA((2 * roll,)),
        ],
        compiler_params=pltpu.CompilerParams(vmem_limit_bytes=60 << 20),
        name="layer",
    )(
        rollout_length,
        slot_block,
        node_state,
        edge_state,
        node_cotangent,
        edge_cotangent,
        edge_sender.reshape(1, edges),
        edge_receiver.reshape(1, edges),
        halo,
        slots,
        vector_params,
    )


def adam_direction(moment_one, moment_two, fix_one, fix_two):
    return moment_one / fix_one / (jnp.sqrt(moment_two / fix_two) + adam_epsilon)


MESH = pl.DeviceIdType.MESH


class Place:
    def __init__(self):
        self.z = lax.axis_index("dp")
        self.n = lax.axis_index("node")
        self.c = lax.rem(self.n, 2)
        self.x = lax.rem(self.n // 2, 2)
        self.y = self.n // 4
        self.xn = self.n + 2 - 4 * self.x
        self.yn = self.n + 4 - 8 * self.y
        self.sib = self.n + 1 - 2 * self.c
        self.diag = self.xn + 4 - 8 * self.y


def remote(src, dst, send, recv, z, n):
    return pltpu.make_async_remote_copy(
        src_ref=src, dst_ref=dst, send_sem=send, recv_sem=recv, device_id=(z, n), device_id_type=MESH
    )


def greet_start(p, depth, peers):
    barrier = pltpu.get_barrier_semaphore()
    for k in range(1, peers):
        to = lax.rem(p.n + k, peers)
        pl.semaphore_signal(barrier, inc=1, device_id=(p.z, to), device_id_type=MESH)
    for k in range(1, depth):
        to = lax.rem(p.z + k, depth)
        pl.semaphore_signal(barrier, inc=1, device_id=(to, p.n), device_id_type=MESH)


def greet_end(depth, peers):
    pl.semaphore_wait(pltpu.get_barrier_semaphore(), peers + depth - 2)


ORDER = ((0, 1, 2, 3), (1, 0, 2, 3), (2, 3, 1, 0), (3, 2, 1, 0))


def gather_start(p, buf, k, sems):
    send, recv = sems
    own = buf(k, p.n)
    copies = []
    for i, to in ((0, p.xn), (1, p.yn), (3, p.sib)):
        copies.append(remote(own, own, send.at[i, k], recv.at[i, k], p.z, to))
        copies[-1].start()
    return copies


def gather_side(p, buf, k, sems):
    send, recv = sems
    copies = []
    for i, owner in ((0, p.xn), (1, p.yn)):
        got = buf(k, owner)
        remote(got, got, send.at[i, k], recv.at[i, k], p.z, owner).wait_recv()
        on = remote(got, got, send.at[4 + i, k], recv.at[4 + i, k], p.z, p.sib)
        on.start()
        copies.append(on)
        over = remote(got, got, send.at[2, k], recv.at[2, k], p.z, p.yn if i == 0 else p.xn)
        pl.when(p.c == i)(over.start)
    copies.append(over)
    return copies


def gather_far(p, buf, k, sems):
    send, recv = sems
    got = buf(k, p.diag)
    remote(got, got, send.at[2, k], recv.at[2, k], p.z, p.xn).wait_recv()
    on = remote(got, got, send.at[6, k], recv.at[6, k], p.z, p.sib)
    on.start()
    return [on]


def gather_end(p, buf, k, sems):
    send, recv = sems
    for i in (3, 4, 5, 6):
        got = buf(k, p.sib)
        remote(got, got, send.at[i, k], recv.at[i, k], p.z, p.sib).wait_recv()


class Step:
    def __init__(self, **refs):
        self.__dict__.update(refs)


def step_kernel(names, *refs):
    k = Step(**dict(zip(names, refs, strict=True)))
    p = Place()
    depth, peers = 4, 8
    roll, nodes, width = k.node_v.shape
    edges = k.edge_v.shape[1]
    slot_dev, rows = k.weight_v.shape[:2]
    per_peer = k.halo.shape[1] // roll
    halo = peers * per_peer
    known = nodes + halo
    padded = k.table.shape[1]
    chunk = 384
    pieces = edges // chunk
    going = []
    leaving = []

    def launch(src, dst, send, recv, z, n):
        copy = remote(src, dst, send, recv, z, n)
        copy.start()
        going.append((copy, None))

    def landed(dst, recv):
        remote(dst, dst, recv, recv, p.z, p.sib).wait_recv()

    def leave(src, dst, i):
        copy = pltpu.make_async_copy(src, dst, k.out_sem.at[i])
        copy.start()
        leaving.append(copy)

    loads = []
    for i, (src, dst) in enumerate(
        (
            (k.weight_hbm, k.weight_v),
            (k.node_hbm.at[0], k.node_v),
            (k.left_hbm, k.grad.at[2, :slot_dev]),
            (k.right_hbm, k.grad.at[:slot_dev]),
            (k.edge_hbm.at[0], k.edge_v),
            (k.ncot_hbm.at[0], k.ncot_v),
            (k.ecot_hbm.at[0], k.ecot_v),
            (k.first_hbm, k.first_v),
            (k.second_hbm, k.second_v),
        )
    ):
        loads.append(pltpu.make_async_copy(src, dst, k.in_sem.at[i]))
        loads[-1].start()
    greet_start(p, depth, peers)

    def buf(z, n):
        return k.slots.at[pl.ds(slot_dev * z, slot_dev), n]

    wsems = (k.w_send, k.w_recv)
    order = []

    def arrive(j):
        z_of = 0
        for z in range(depth):
            z_of = z_of + jnp.where(p.z == z, ORDER[z][j], 0)
        order.append(z_of)
        piece = buf(z_of, p.n)
        if j:
            remote(piece, piece, k.wz_send.at[0, z_of], k.wz_recv.at[z_of], p.z, p.n).wait_recv()
        for i, test, to in (
            (0, (z_of <= p.z) & (p.z < depth - 1), p.z + 1),
            (1, (z_of >= p.z) & (p.z > 0), p.z - 1),
        ):
            copy = remote(piece, piece, k.wz_send.at[i, z_of], k.wz_recv.at[z_of], to, p.n)
            pl.when(test)(copy.start)
            going.append((copy, test))
        going.extend((copy, None) for copy in gather_start(p, buf, z_of, wsems))

    def side(j):
        going.extend((copy, None) for copy in gather_side(p, buf, order[j], wsems))

    def far(j):
        going.extend((copy, None) for copy in gather_far(p, buf, order[j], wsems))

    loads[0].wait()
    k.slots[pl.ds(slot_dev * p.z, slot_dev), p.n] = k.weight_v[...].astype(bf16)
    greet_end(depth, peers)
    arrive(0)
    loads[1].wait()
    node_ids = lax.broadcasted_iota(jnp.int32, (nodes, halo), 0)
    pick_t = jnp.where(node_ids == k.rows_ref[...], 1.0, 0.0).astype(bf16)
    for t in range(roll):
        k.spread[:, t] = dot(pick_t.T, k.node_v[t]).reshape(peers, per_peer, width)
    k.hput[...] = k.spread[...].reshape(peers, roll * per_peer, width).astype(bf16)
    k.halo[p.n] = k.hput[p.n]
    hsent = []
    for i in range(1, peers):
        to = lax.rem(p.n + i, peers)
        hsent.append(remote(k.hput.at[to], k.halo.at[p.n], k.h_send.at[0, i], k.h_recv.at[0, i], p.z, to))
        hsent[-1].start()
    arrive(1)
    side(0)
    loads[2].wait()
    for s in range(slot_dev):
        k.left_b[s] = k.grad[2, s].astype(bf16)
        for m in range(peers):
            k.lput[s, m] = k.grad[2, s, :, m * rows : (m + 1) * rows].astype(bf16)
    k.lgot[:, p.n] = k.lput[:, p.n]
    for i in range(1, peers):
        to = lax.rem(p.n + i, peers)
        launch(k.lput.at[:, to], k.lgot.at[:, p.n], k.l_send.at[i], k.l_recv.at[i], p.z, to)
    arrive(2)
    side(1)
    far(0)
    ids = lax.broadcasted_iota(jnp.int32, (padded, edges), 0)
    onehot = (ids == k.sender_ref[...].reshape(1, edges)) | (
        ids == k.receiver_ref[...].reshape(1, edges) + known
    )
    onehot = jnp.where(onehot, 1.0, 0.0).astype(f32)
    k.gather_t[...] = onehot.astype(bf16)
    arrive(3)
    side(2)
    far(1)
    k.gather[...] = onehot.T.astype(bf16)
    k.table[:, known + nodes :] = jnp.zeros((roll, padded - known - nodes, width), bf16)
    k.acc[...] = jnp.zeros_like(k.acc)
    side(3)
    far(2)
    loads[3].wait()
    for s in range(slot_dev):
        k.right_b[s] = k.grad[s].reshape(width, width).astype(bf16)
    far(3)
    for copy in hsent:
        copy.wait_send()
    for i in range(1, peers):
        landed(k.halo.at[0], k.h_recv.at[0, i])
        landed(k.lgot.at[:, 0], k.l_recv.at[i])
    for j in range(depth):
        gather_end(p, buf, order[j], wsems)

    slot_of = []
    for b in range(NBLOCK):
        found = 0
        for s in range(depth * slot_dev):
            found = jnp.where(k.slot_block_ref[s] == b, s, found)
        slot_of.append(found)

    def weight(b):
        return k.slots[slot_of[b]].reshape(width, width)

    rollout = k.rollout_ref[0]
    vec = k.vec_ref

    def live(t):
        return jnp.where(t < rollout, 1.0, 0.0).astype(f32)

    def flat_nodes():
        return k.node_v[...].reshape(roll * nodes, width)

    own_sent = dot(flat_nodes(), weight(1))
    own_recv = dot(flat_nodes(), weight(2))
    halo_flat = k.halo[...].reshape(roll * halo, width)
    halo_sent = dot(halo_flat, weight(1)).reshape(peers, roll, per_peer, width)
    for t in range(roll):
        k.table[t, :nodes] = own_sent[t * nodes : (t + 1) * nodes].astype(bf16)
        k.table[t, nodes:known] = halo_sent[:, t].reshape(halo, width).astype(bf16)
        k.table[t, known : known + nodes] = own_recv[t * nodes : (t + 1) * nodes].astype(bf16)
    loads[4].wait()

    def edge_out(t):
        return pltpu.make_async_copy(k.eout_v.at[t % 2], k.eout_hbm.at[0, t], k.e_sem.at[t])

    def forward(t, carry):
        lv = live(t)
        slot = t % 2

        @pl.when(t >= 2)
        def _():
            edge_out(t - 2).wait()

        total = jnp.zeros((nodes, width), f32)
        for c in range(pieces):
            at = pl.ds(c * chunk, chunk)
            edge = k.edge_v[t, at]
            z = dot(edge, weight(0)) + dot(k.gather[at], k.table[t]) + vec[0:1]
            hidden, slope, normed, inverse = branch_forward(z, weight(3), vec[1:2])
            k.hidden_v[t, at] = hidden
            k.slope_v[t, at] = slope.astype(bf16)
            k.normed_v[t, at] = normed.astype(bf16)
            k.inv_v[t, at] = inverse
            new = edge.astype(f32) + (normed * vec[2:3] + vec[3:4])
            k.eout_v[slot, at] = (new * lv).astype(bf16)
            total += dot(k.gather_t[known : known + nodes, at], new.astype(bf16))
        k.summed_v[pl.ds(t * nodes, nodes)] = total.astype(bf16)
        edge_out(t).start()
        return carry

    lax.fori_loop(0, roll, forward, 0)

    on_f = jnp.where(p.c == 0, p.x, p.y)
    on_g = jnp.where(p.c == 0, p.y, p.x)
    to_f = jnp.where(p.c == 0, p.xn, p.yn)
    to_g = jnp.where(p.c == 0, p.yn, p.xn)

    def spot(f, g):
        return jnp.where(p.c == 0, g * 2 + f, f * 2 + g)

    def hop(stage, b):
        put, got, to = (
            (k.cast, k.got_core, p.sib),
            (k.put_one, k.got_one, to_f),
            (k.put_two, k.got_two, to_g),
        )[stage]
        at = stage * NBLOCK + b
        return remote(put.at[b], got.at[b], k.r_send.at[at], k.r_recv.at[at], p.z, to)

    def to_core(b):
        for i in range(peers // 2):
            k.cast[b, i] = k.grad[b, 2 * i + 1 - p.c].astype(bf16)
        hop(0, b).start()

    def to_first(b):
        hop(0, b).wait_recv()
        for g in range(2):
            at = spot(1 - on_f, g)
            k.put_one[b, g] = (k.grad[b, 2 * at + p.c] + k.got_core[b, at].astype(f32)).astype(bf16)
        hop(1, b).start()
        for g in range(2):
            at = spot(on_f, g)
            k.grad[b, 2 * at + p.c] = k.grad[b, 2 * at + p.c] + k.got_core[b, at].astype(f32)

    def to_second(b):
        hop(1, b).wait_recv()
        at = spot(on_f, 1 - on_g)
        total = k.grad[b, 2 * at + p.c] + k.got_one[b, 1 - on_g].astype(f32)
        k.put_two[b] = total.astype(bf16)
        hop(2, b).start()
        k.grad[b, p.n] = k.grad[b, p.n] + k.got_one[b, on_g].astype(f32)

    def settle(b):
        hop(2, b).wait_recv()
        k.grad[b, p.n] = k.grad[b, p.n] + k.got_two[b].astype(f32)

    def put_grad(b, value):
        k.grad[b] = value.reshape(peers, rows, width)

    summed = k.summed_v[...]
    z = dot(flat_nodes(), weight(4)) + dot(summed, weight(5)) + vec[4:5]
    hidden, slope, normed, inverse = branch_forward(z, weight(6), vec[5:6])
    row_t = lax.broadcasted_iota(jnp.int32, (roll * nodes, 1), 0) // nodes
    row_live = jnp.where(row_t < rollout, 1.0, 0.0).astype(f32)
    new = flat_nodes().astype(f32) + (normed * vec[6:7] + vec[7:8])
    k.nout_v[...] = (new * row_live).astype(bf16).reshape(roll, nodes, width)
    leave(k.nout_v, k.nout_hbm.at[0], 0)
    loads[5].wait()
    d_new = k.ncot_v[...].reshape(roll * nodes, width).astype(f32) * row_live
    k.acc[6] = eights(d_new * normed)
    k.acc[7] = eights(d_new)
    d_after = norm_backward(d_new, normed, inverse, vec[6:7])
    k.acc[5] = eights(d_after.astype(f32))
    put_grad(6, dot_ta(hidden, d_after))
    to_core(6)
    d_before = (dot_tb(d_after, weight(6)) * slope).astype(bf16)
    k.acc[4] = eights(d_before.astype(f32))
    put_grad(4, dot_ta(flat_nodes(), d_before))
    to_core(4)
    put_grad(5, dot_ta(summed, d_before))
    to_core(5)
    k.summed_v[...] = dot_tb(d_before, weight(5)).astype(bf16)
    k.nbase_v[...] = d_new + dot_tb(d_before, weight(4))
    k.grad[0] = jnp.zeros((peers, rows, width), f32)
    k.grad[3] = jnp.zeros((peers, rows, width), f32)
    loads[6].wait()

    def backward(t, carry):
        lv = live(t)
        for c in range(pieces):
            at = pl.ds(c * chunk, chunk)
            d_new = k.ecot_v[t, at].astype(f32) * lv + dot(
                k.gather[at, known : known + nodes], k.summed_v[pl.ds(t * nodes, nodes)]
            )
            k.ecot_v[t, at] = d_new.astype(bf16)
            normed = k.normed_v[t, at].astype(f32)
            k.acc[2] += eights(d_new * normed)
            k.acc[3] += eights(d_new)
            d_after = norm_backward(d_new, normed, k.inv_v[t, at], vec[2:3])
            k.acc[1] += eights(d_after.astype(f32))
            k.normed_v[t, at] = d_after
            d_before = (dot_tb(d_after, weight(3)) * k.slope_v[t, at].astype(f32)).astype(bf16)
            k.acc[0] += eights(d_before.astype(f32))
            k.slope_v[t, at] = d_before
        k.grad[3] += dot_ta(k.hidden_v[t], k.normed_v[t]).reshape(peers, rows, width)
        k.grad[0] += dot_ta(k.edge_v[t], k.slope_v[t]).reshape(peers, rows, width)
        scattered = dot(k.gather_t[...], k.slope_v[t])
        k.sc_own[pl.ds(t * nodes, nodes)] = scattered[:nodes].astype(bf16)
        k.sc_recv[pl.ds(t * nodes, nodes)] = scattered[known : known + nodes].astype(bf16)
        k.spread[:, t] = scattered[nodes:known].reshape(peers, per_peer, width)
        for step, work in enumerate((to_first, to_second, settle)):

            @pl.when(t == step)
            def _():
                def one(b, carry):
                    work(b)
                    return carry

                lax.fori_loop(4, NBLOCK, one, 0)

        return carry

    lax.fori_loop(0, roll, backward, 0)

    to_core(3)
    to_core(0)
    k.hput[...] = k.spread[...].reshape(peers, roll * per_peer, width).astype(bf16)
    put_grad(1, dot_ta(flat_nodes(), k.sc_own[...]) + dot_ta(halo_flat, k.hput[...].reshape(roll * halo, width)))
    to_core(1)
    put_grad(2, dot_ta(flat_nodes(), k.sc_recv[...]))
    to_core(2)
    k.vput[0] = jnp.sum(k.acc[...], axis=1)
    launch(k.vput.at[0], k.vgot.at[0], k.v_send.at[0], k.v_recv.at[0], p.z, p.sib)
    for i in range(1, peers):
        to = lax.rem(p.n + i, peers)
        launch(k.hput.at[to], k.hret.at[p.n], k.h_send.at[1, i], k.h_recv.at[1, i], p.z, to)
    k.hret[p.n] = k.hput[p.n]
    to_first(3)
    to_first(0)

    def edge_gradient(t):
        for c in range(pieces):
            at = pl.ds(c * chunk, chunk)
            grown = k.ecot_v[t, at].astype(f32) + dot_tb(k.slope_v[t, at], weight(0))
            k.ecot_v[t, at] = grown.astype(bf16)
        leave(k.ecot_v.at[t], k.egrad_hbm.at[0, t], 2 + t)

    edge_gradient(0)
    to_first(1)
    to_first(2)
    to_second(3)
    to_second(0)
    landed(k.vgot.at[0], k.v_recv.at[0])
    k.vput[1] = k.vput[0] + k.vgot[0]
    launch(k.vput.at[1], k.vgot.at[1], k.v_send.at[1], k.v_recv.at[1], p.z, p.xn)
    edge_gradient(1)
    to_second(1)
    to_second(2)
    settle(3)
    settle(0)
    landed(k.vgot.at[1], k.v_recv.at[1])
    k.vput[2] = k.vput[1] + k.vgot[1]
    launch(k.vput.at[2], k.vgot.at[2], k.v_send.at[2], k.v_recv.at[2], p.z, p.yn)
    edge_gradient(2)
    settle(1)
    settle(2)

    def part(target, s):
        b = k.slot_block_ref[target * slot_dev + s]
        held = k.grad[jnp.minimum(b, NBLOCK - 1), p.n]
        return jnp.where(b < NBLOCK, held, 0.0)

    def pass_on(way):
        put, got = (k.put_up, k.got_up) if way == 0 else (k.put_down, k.got_down)
        source = p.z > 0 if way == 0 else p.z < depth - 1
        for i in range(depth - 1):
            target = depth - 1 - i if way == 0 else i
            test = p.z < target if way == 0 else p.z > target
            at = p.z + 1 if way == 0 else p.z - 1

            @pl.when(test)
            def _():
                for s in range(slot_dev):

                    @pl.when(source)
                    def _():
                        landed(got.at[target, s], k.z_recv.at[way, target, s])
                        total = part(target, s) + got[target, s].astype(f32)
                        put[target, s] = total.astype(bf16)

                    @pl.when(jnp.logical_not(source))
                    def _():
                        put[target, s] = part(target, s).astype(bf16)

                    remote(
                        put.at[target, s],
                        got.at[target, s],
                        k.z_send.at[way, target, s],
                        k.z_recv.at[way, target, s],
                        at,
                        p.n,
                    ).start()

    @pl.when(p.z < depth // 2)
    def _():
        pass_on(0)
        pass_on(1)

    @pl.when(p.z >= depth // 2)
    def _():
        pass_on(1)
        pass_on(0)

    landed(k.vgot.at[2], k.v_recv.at[2])
    k.vput[3] = k.vput[2] + k.vgot[2]
    k.vz[p.z] = k.vput[3]
    for i in range(1, depth):
        to = lax.rem(p.z + i, depth)
        launch(k.vput.at[3], k.vz.at[p.z], k.v_send.at[2 + i], k.v_recv.at[2 + i], to, p.n)
    edge_gradient(3)
    for i in range(1, peers):
        landed(k.hret.at[0], k.h_recv.at[1, i])
    back = k.hret[...].astype(f32).reshape(peers, roll, per_peer, width)
    for t in range(roll):
        at = pl.ds(t * nodes, nodes)
        rows_t = back[:, t].reshape(halo, width).astype(bf16)
        k.sc_own[at] = (k.sc_own[at].astype(f32) + dot(pick_t, rows_t)).astype(bf16)
    grown = k.nbase_v[...] + dot_tb(k.sc_own[...], weight(1)) + dot_tb(k.sc_recv[...], weight(2))
    k.ngrad_v[...] = grown.astype(bf16).reshape(roll, nodes, width)
    leave(k.ngrad_v, k.ngrad_hbm.at[0], 1)

    square = jnp.zeros((8, width), f32)
    gsems = (k.g_send, k.g_recv)
    gbuf = lambda s, n: k.full.at[s, n]
    for s in range(slot_dev):

        @pl.when(p.z > 0)
        def _():
            landed(k.got_up.at[p.z, s], k.z_recv.at[0, p.z, s])

        @pl.when(p.z < depth - 1)
        def _():
            landed(k.got_down.at[p.z, s], k.z_recv.at[1, p.z, s])

        mine = part(p.z, s) + jnp.where(p.z > 0, k.got_up[p.z, s].astype(f32), 0.0)
        mine = mine + jnp.where(p.z < depth - 1, k.got_down[p.z, s].astype(f32), 0.0)
        k.full[s, p.n] = mine.astype(bf16)
        for copy in gather_start(p, gbuf, s, gsems):
            going.append((copy, None))
        square = square + eights(mine * mine)
    square = square[:, :128] + square[:, 128:256] + square[:, 256:384] + square[:, 384:]
    k.sput[...] = square
    k.sgot[p.n] = square
    for i in range(1, peers):
        to = lax.rem(p.n + i, peers)
        launch(k.sput, k.sgot.at[p.n], k.n_send.at[i], k.n_recv.at[i], p.z, to)

    def collect(buffer, sems, finish):
        for s in range(slot_dev):
            going.extend((copy, None) for copy in gather_side(p, buffer, s, sems))
        for s in range(slot_dev):
            going.extend((copy, None) for copy in gather_far(p, buffer, s, sems))
        for s in range(slot_dev):
            gather_end(p, buffer, s, sems)
            finish(s)

    for i in range(1, peers):
        landed(k.sgot.at[0], k.n_recv.at[i])
    k.szput[...] = jnp.sum(k.sgot[...], axis=0)
    k.sz[p.z] = k.szput[...]
    for i in range(1, depth):
        to = lax.rem(p.z + i, depth)
        launch(k.szput, k.sz.at[p.z], k.n_send.at[peers - 1 + i], k.n_recv.at[peers - 1 + i], to, p.n)

    rotated = [None] * slot_dev

    def rotate(s):
        part_left = dot(k.left_b[s], k.full[s].reshape(width, width))
        rotated[s] = dot(part_left.astype(bf16), k.right_b[s])

    collect(gbuf, gsems, rotate)
    for i in range(1, depth):
        landed(k.vz.at[0], k.v_recv.at[2 + i])
        landed(k.sz.at[0], k.n_recv.at[peers - 1 + i])
    grad_vectors = k.vz[0] + k.vz[1] + k.vz[2] + k.vz[3]
    square_sum = jnp.sum(k.sz[0] + k.sz[1] + k.sz[2] + k.sz[3], keepdims=True).reshape(1, 1)
    square_sum = square_sum + jnp.sum(grad_vectors * grad_vectors, keepdims=True).reshape(1, 1)
    grad_norm = jnp.sqrt(square_sum)
    k.norm_v[...] = jnp.broadcast_to(grad_norm, k.norm_v.shape)
    leave(k.norm_v, k.norm_hbm, 2 + roll)
    limit = math.sqrt(NBLOCK * width * width + 8 * width)
    clip = jnp.minimum(1.0, limit / grad_norm)

    def fix(beta, step):
        return 1.0 - jnp.exp2(math.log2(beta) * jnp.full((1, 1), step, jnp.int32).astype(f32))

    tsems = (k.t_send, k.t_recv)
    tbuf = lambda s, n: k.turned.at[s, n]
    loads[7].wait()
    loads[8].wait()
    for s in range(slot_dev):
        step = k.step_ref[p.z * slot_dev + s]
        spun = rotated[s] * clip
        one = beta_first * k.first_v[s] + (1.0 - beta_first) * spun
        two = beta_second * k.second_v[s] + (1.0 - beta_second) * spun * spun
        k.first_v[s] = one
        k.second_v[s] = two
        direction = adam_direction(one, two, fix(beta_first, step), fix(beta_second, step))
        k.turned[s, p.n] = dot_tb(direction.astype(bf16), k.right_b[s]).astype(bf16)
        for copy in gather_start(p, tbuf, s, tsems):
            going.append((copy, None))
    leave(k.first_v, k.first_out, 3 + roll)
    leave(k.second_v, k.second_out, 4 + roll)

    step = k.step_ref[depth * slot_dev]
    spun = grad_vectors * clip
    one = beta_first * k.vfirst_ref[...] + (1.0 - beta_first) * spun
    two = beta_second * k.vsecond_ref[...] + (1.0 - beta_second) * spun * spun
    k.vstate_v[0] = vec[...] - rate_vector * adam_direction(
        one, two, fix(beta_first, step), fix(beta_second, step)
    )
    k.vstate_v[1] = one
    k.vstate_v[2] = two
    leave(k.vstate_v, k.vstate_hbm, 5 + roll)

    def finish(s):
        left_back = k.lgot[s].reshape(width, rows)
        reverted = dot_ta(left_back, k.turned[s].reshape(width, width))
        new = k.weight_v[s] - rate_matrix * (reverted + weight_decay * k.weight_v[s])
        k.wnew_v[s] = new
        k.wcopy_v[s] = new.astype(bf16)
        leave(k.wnew_v.at[s], k.wnew_hbm.at[s], 6 + roll + s)
        leave(k.wcopy_v.at[s], k.wcopy_hbm.at[s], 6 + roll + slot_dev + s)

    collect(tbuf, tsems, finish)

    for copy, test in going:
        if test is None:
            copy.wait_send()
        else:
            pl.when(test)(copy.wait_send)
    for b in range(NBLOCK):
        for stage in range(3):
            hop(stage, b).wait_send()
    for i in range(depth - 1):
        for s in range(slot_dev):
            for test, target, way, put in (
                (p.z < depth - 1 - i, depth - 1 - i, 0, k.put_up),
                (p.z > i, i, 1, k.put_down),
            ):
                sent = remote(
                    put.at[target, s],
                    put.at[target, s],
                    k.z_send.at[way, target, s],
                    k.z_recv.at[way, target, s],
                    p.z,
                    p.sib,
                )
                pl.when(test)(sent.wait_send)
    for t in (roll - 2, roll - 1):
        edge_out(t).wait()
    for copy in leaving:
        copy.wait()


def copy_kernel(*refs):
    count = 9
    sources, norm, targets, norm_out = refs[:count], refs[count], refs[count + 1 : -count - 3], refs[-count - 3]
    stage, in_sem, out_sem = refs[-count - 2 : -2], refs[-2], refs[-1]
    first, second = [], []
    for i in range(count):
        first.append(pltpu.make_async_copy(sources[i], stage[i], in_sem.at[i]))
        second.append(pltpu.make_async_copy(stage[i], targets[i], out_sem.at[i]))
        first[-1].start()
    norm_out[0] = norm[0, 0]
    for i in range(count):
        first[i].wait()
        second[i].start()
    for copy in second:
        copy.wait()


def whole_step(
    node_state,
    edge_state,
    node_cotangent,
    edge_cotangent,
    send_rows,
    edge_sender,
    edge_receiver,
    rollout_length,
    slot_block,
    step_count,
    weight_slots,
    moment_first,
    moment_second,
    basis_left,
    basis_right,
    vector_params,
    vector_first,
    vector_second,
):
    depth, peers = 4, 8
    _, roll, nodes, width = node_state.shape
    edges = edge_state.shape[2]
    slot_dev, rows = weight_slots.shape[:2]
    halo = send_rows.shape[1]
    per_peer = halo // peers
    padded = -(-(2 * nodes + halo) // 128) * 128
    own = (slot_dev, rows, width)
    tile = (8, 128)
    hbm = pl.BlockSpec(memory_space=pl.ANY)
    vmem = pl.BlockSpec(memory_space=pltpu.VMEM)
    smem = pl.BlockSpec(memory_space=pltpu.SMEM)
    shape = jax.ShapeDtypeStruct
    dma = pltpu.SemaphoreType.DMA
    ins = dict(
        rollout_ref=(rollout_length, smem),
        slot_block_ref=(slot_block, smem),
        step_ref=(step_count, smem),
        node_hbm=(node_state, hbm),
        edge_hbm=(edge_state, hbm),
        ncot_hbm=(node_cotangent, hbm),
        ecot_hbm=(edge_cotangent, hbm),
        rows_ref=(send_rows, vmem),
        sender_ref=(edge_sender, vmem),
        receiver_ref=(edge_receiver, vmem),
        weight_hbm=(weight_slots, hbm),
        first_hbm=(moment_first, hbm),
        second_hbm=(moment_second, hbm),
        left_hbm=(jnp.swapaxes(basis_left, 1, 2), hbm),
        right_hbm=(basis_right.reshape(slot_dev, peers, rows, width), hbm),
        vec_ref=(vector_params, vmem),
        vfirst_ref=(vector_first, vmem),
        vsecond_ref=(vector_second, vmem),
    )
    outs = dict(
        nout_hbm=shape(node_state.shape, bf16),
        eout_hbm=shape(edge_state.shape, bf16),
        ngrad_hbm=shape(node_state.shape, bf16),
        egrad_hbm=shape(edge_state.shape, bf16),
        first_out=shape(own, f32),
        second_out=shape(own, f32),
        wnew_hbm=shape(own, f32),
        wcopy_hbm=shape(own, bf16),
        vstate_hbm=shape((3, 8, width), f32),
        norm_hbm=shape(tile, f32),
    )
    v = pltpu.VMEM
    scratch = dict(
        weight_v=v(own, f32),
        node_v=v((roll, nodes, width), bf16),
        edge_v=v((roll, edges, width), bf16),
        ncot_v=v((roll, nodes, width), bf16),
        ecot_v=v((roll, edges, width), bf16),
        first_v=v(own, f32),
        second_v=v(own, f32),
        slots=v((slot_dev * depth, peers, rows, width), bf16),
        halo=v((peers, roll * per_peer, width), bf16),
        spread=v((peers, roll, per_peer, width), f32),
        hput=v((peers, roll * per_peer, width), bf16),
        hret=v((peers, roll * per_peer, width), bf16),
        left_b=v((slot_dev, rows, width), bf16),
        lput=v((slot_dev, peers, rows, rows), bf16),
        lgot=v((slot_dev, peers, rows, rows), bf16),
        right_b=v((slot_dev, width, width), bf16),
        gather_t=v((padded, edges), bf16),
        gather=v((edges, padded), bf16),
        table=v((roll, padded, width), bf16),
        eout_v=v((2, edges, width), bf16),
        hidden_v=v((roll, edges, width), bf16),
        slope_v=v((roll, edges, width), bf16),
        normed_v=v((roll, edges, width), bf16),
        inv_v=v((roll, edges, 1), f32),
        summed_v=v((roll * nodes, width), bf16),
        sc_own=v((roll * nodes, width), bf16),
        sc_recv=v((roll * nodes, width), bf16),
        nbase_v=v((roll * nodes, width), f32),
        nout_v=v((roll, nodes, width), bf16),
        ngrad_v=v((roll, nodes, width), bf16),
        acc=v((8, 8, width), f32),
        grad=v((NBLOCK, peers, rows, width), f32),
        cast=v((NBLOCK, peers // 2, rows, width), bf16),
        got_core=v((NBLOCK, peers // 2, rows, width), bf16),
        put_one=v((NBLOCK, 2, rows, width), bf16),
        got_one=v((NBLOCK, 2, rows, width), bf16),
        put_two=v((NBLOCK, rows, width), bf16),
        got_two=v((NBLOCK, rows, width), bf16),
        put_up=v((depth, *own), bf16),
        put_down=v((depth, *own), bf16),
        got_up=v((depth, *own), bf16),
        got_down=v((depth, *own), bf16),
        full=v((slot_dev, peers, rows, width), bf16),
        turned=v((slot_dev, peers, rows, width), bf16),
        wnew_v=v(own, f32),
        wcopy_v=v(own, bf16),
        vstate_v=v((3, 8, width), f32),
        norm_v=v(tile, f32),
        vput=v((4, 8, width), f32),
        vgot=v((3, 8, width), f32),
        vz=v((depth, 8, width), f32),
        sput=v(tile, f32),
        sgot=v((peers, *tile), f32),
        szput=v(tile, f32),
        sz=v((depth, *tile), f32),
        in_sem=dma((9,)),
        out_sem=dma((6 + roll + 2 * slot_dev,)),
        e_sem=dma((roll,)),
        w_send=dma((7, depth)),
        w_recv=dma((7, depth)),
        wz_send=dma((2, depth)),
        wz_recv=dma((depth,)),
        h_send=dma((2, peers)),
        h_recv=dma((2, peers)),
        l_send=dma((peers,)),
        l_recv=dma((peers,)),
        r_send=dma((3 * NBLOCK,)),
        r_recv=dma((3 * NBLOCK,)),
        z_send=dma((2, depth, slot_dev)),
        z_recv=dma((2, depth, slot_dev)),
        g_send=dma((7, slot_dev)),
        g_recv=dma((7, slot_dev)),
        t_send=dma((7, slot_dev)),
        t_recv=dma((7, slot_dev)),
        v_send=dma((6,)),
        v_recv=dma((6,)),
        n_send=dma((peers + depth - 1,)),
        n_recv=dma((peers + depth - 1,)),
    )
    names = (*ins, *outs, *scratch)
    results = pl.pallas_call(
        functools.partial(step_kernel, names),
        out_shape=tuple(outs.values()),
        in_specs=[spec for _, spec in ins.values()],
        out_specs=(hbm,) * len(outs),
        scratch_shapes=list(scratch.values()),
        compiler_params=pltpu.CompilerParams(
            vmem_limit_bytes=61 << 20, collective_id=0, has_side_effects=True
        ),
        name="step",
    )(*(value for value, _ in ins.values()))
    final = [*outs.values()][:-1]
    return pl.pallas_call(
        copy_kernel,
        out_shape=(*final, shape((1,), f32)),
        in_specs=[hbm] * len(final) + [vmem],
        out_specs=(*([hbm] * len(final)), smem),
        scratch_shapes=[v(out.shape, out.dtype) for out in final] + [dma((len(final),))] * 2,
        compiler_params=pltpu.CompilerParams(vmem_limit_bytes=60 << 20),
        name="results",
    )(*results)


def local(
    node_state,
    edge_state,
    node_cotangent,
    edge_cotangent,
    send_rows,
    edge_sender,
    edge_receiver,
    rollout_length,
    slot_block,
    step_count,
    weight_slots,
    moment_first,
    moment_second,
    basis_left,
    basis_right,
    vector_params,
    vector_first,
    vector_second,
):
    width = node_state.shape[-1]
    roll, nodes = node_state.shape[1:3]
    clip_limit = math.sqrt(NBLOCK * width * width + 8 * width)
    slot_dev = weight_slots.shape[0]
    slot_total = slot_block.shape[0]
    halo_rows = send_rows.shape[1]
    peers = lax.axis_size("node")
    per_peer = halo_rows // peers
    if (lax.axis_size("dp"), peers) == (4, 8):
        return whole_step(
            node_state,
            edge_state,
            node_cotangent,
            edge_cotangent,
            send_rows,
            edge_sender,
            edge_receiver,
            rollout_length,
            slot_block,
            step_count,
            weight_slots,
            moment_first,
            moment_second,
            basis_left,
            basis_right,
            vector_params,
            vector_first,
            vector_second,
        )
    copies = lax.all_gather(weight_slots.astype(bf16), "node", axis=1, tiled=True)
    slots = lax.all_gather(copies, "dp", axis=0, tiled=True)
    back_onehot = (send_rows[0][:, None] == jnp.arange(nodes, dtype=jnp.int32)[None, :]).astype(bf16)
    outgoing = jnp.einsum("hk,tkd->htd", back_onehot, node_state[0], preferred_element_type=f32)
    outgoing = outgoing.astype(bf16).reshape(peers, per_peer, roll, width).transpose(0, 2, 1, 3)
    outgoing = outgoing.reshape(peers * roll * per_peer, width)
    halo = lax.all_to_all(outgoing, "node", split_axis=0, concat_axis=0, tiled=True)

    node_output, edge_output, node_base, edge_gradient, grads, grad_vectors, halo_back = layer(
        rollout_length,
        slot_block,
        node_state,
        edge_state,
        node_cotangent,
        edge_cotangent,
        edge_sender,
        edge_receiver,
        halo,
        slots,
        vector_params,
        per_peer,
    )
    returned = lax.all_to_all(halo_back, "node", split_axis=0, concat_axis=0, tiled=True)
    returned = returned.reshape(peers, roll, per_peer, width).transpose(0, 2, 1, 3)
    d_back = jnp.einsum(
        "hk,htd->tkd",
        back_onehot,
        returned.reshape(halo_rows, roll, width),
        preferred_element_type=f32,
    )
    node_gradient = node_base.reshape(roll, nodes, width) + d_back
    node_gradient = node_gradient.astype(bf16).reshape(node_state.shape)

    block_of_slot = slot_block[None, :] == jnp.arange(NBLOCK, dtype=jnp.int32)[:, None]
    first = lax.axis_index("dp") * slot_dev
    summed, grad_vectors = lax.psum((grads, grad_vectors), ("dp", "node"))
    own_square = jnp.sum(summed * summed)
    mine = lax.dynamic_slice_in_dim(block_of_slot.astype(f32), first, slot_dev, 1)
    owned_grads = jnp.einsum("bs,bij->sij", mine, summed, precision=highest)
    square_sum = own_square + jnp.sum(grad_vectors * grad_vectors)
    grad_norm = jnp.sqrt(square_sum)
    clip_scale = jnp.minimum(1.0, clip_limit / grad_norm)
    owned_grads = owned_grads * clip_scale
    grad_vectors = grad_vectors * clip_scale
    own_steps = lax.dynamic_slice_in_dim(step_count, first, slot_dev, 0)
    slot_steps = own_steps.astype(f32)[:, None, None]
    fix_one = 1.0 - jnp.power(f32(beta_first), slot_steps)
    fix_two = 1.0 - jnp.power(f32(beta_second), slot_steps)
    rotated = jnp.einsum("sij,sik->sjk", basis_left, owned_grads, precision=highest, preferred_element_type=f32)
    rotated = jnp.einsum("sjk,skl->sjl", rotated, basis_right, precision=highest, preferred_element_type=f32)
    moment_one = beta_first * moment_first + (1.0 - beta_first) * rotated
    moment_two = beta_second * moment_second + (1.0 - beta_second) * rotated * rotated
    direction = adam_direction(moment_one, moment_two, fix_one, fix_two)
    turned = jnp.einsum("sjl,sml->sjm", direction, basis_right, precision=highest, preferred_element_type=f32)
    reverted = jnp.einsum("sij,sjm->ism", basis_left, turned, precision=highest, preferred_element_type=f32)
    reverted = lax.psum_scatter(reverted.astype(bf16), "node", scatter_dimension=0, tiled=True).astype(f32)
    reverted = jnp.transpose(reverted, (1, 0, 2))
    new_weights = weight_slots - rate_matrix * (reverted + weight_decay * weight_slots)
    vec_step = step_count[slot_total].astype(f32)
    vfix_one = 1.0 - jnp.power(f32(beta_first), vec_step)
    vfix_two = 1.0 - jnp.power(f32(beta_second), vec_step)
    vec_one = beta_first * vector_first + (1.0 - beta_first) * grad_vectors
    vec_two = beta_second * vector_second + (1.0 - beta_second) * grad_vectors * grad_vectors
    vec_new = vector_params - rate_vector * adam_direction(vec_one, vec_two, vfix_one, vfix_two)
    vector_state = jnp.stack([vec_new, vec_one, vec_two])
    return (
        node_output,
        edge_output,
        node_gradient,
        edge_gradient,
        moment_one,
        moment_two,
        new_weights,
        new_weights.astype(bf16),
        vector_state,
        grad_norm.reshape(1),
    )


def solution(mesh):
    in_specs = (
        P("dp", None, "node", None),
        P("dp", None, "node", None),
        P("dp", None, "node", None),
        P("dp", None, "node", None),
        P("node", None),
        P("node"),
        P("node"),
        P("dp"),
        P(),
        P(),
        P("dp", "node", None),
        P("dp", "node", None),
        P("dp", "node", None),
        P("dp", None, "node"),
        P("dp", None, None),
        P(),
        P(),
        P(),
    )
    out_specs = (
        P("dp", None, "node", None),
        P("dp", None, "node", None),
        P("dp", None, "node", None),
        P("dp", None, "node", None),
        P("dp", "node", None),
        P("dp", "node", None),
        P("dp", "node", None),
        P("dp", "node", None),
        P(),
        P(),
    )
    return jax.shard_map(local, mesh=mesh, in_specs=in_specs, out_specs=out_specs, check_vma=False)
```

```python
import functools
import math

import jax
import jax.numpy as jnp
from jax import lax
from jax.experimental import pallas as pl
from jax.experimental.pallas import tpu as pltpu
from jax.sharding import PartitionSpec as P

NBLOCK = 7
f32 = jnp.float32
bf16 = jnp.bfloat16
highest = lax.Precision.HIGHEST
norm_epsilon = 1e-05
adam_epsilon = 1e-08
beta_first = 0.5
beta_second = 0.5
rate_matrix = 0.03
rate_vector = 0.4
weight_decay = 0.01


def dot(a, b):
    return jnp.dot(a, b, preferred_element_type=f32)


def dot_tb(a, b):
    return lax.dot_general(a, b, (((1,), (1,)), ((), ())), preferred_element_type=f32)


def dot_ta(a, b):
    return lax.dot_general(a, b, (((0,), (0,)), ((), ())), preferred_element_type=f32)


def eights(x):
    return jnp.sum(x.reshape(x.shape[0] // 8, 8, x.shape[1]), axis=0)


def sigmoid(z):
    return 0.5 * jnp.tanh(0.5 * z) + 0.5


def branch_forward(z, w_out, bias_out):
    s = sigmoid(z)
    h = z * s
    slope = s + h * (1.0 - s)
    hidden = h.astype(bf16)
    after = dot(hidden, w_out) + bias_out
    center = after - jnp.mean(after, axis=1, keepdims=True)
    spread = jnp.mean(center * center, axis=1, keepdims=True)
    inverse = lax.rsqrt(spread + norm_epsilon)
    return hidden, slope, center * inverse, inverse


def norm_backward(upstream, normed, inverse, gain):
    u = upstream * gain
    first = jnp.mean(u, axis=1, keepdims=True)
    second = jnp.mean(u * normed, axis=1, keepdims=True)
    return (inverse * (u - first - normed * second)).astype(bf16)


def layer_kernel(
    rollout_ref,
    slot_block_ref,
    node_hbm,
    edge_hbm,
    ncot_hbm,
    ecot_hbm,
    sender_ref,
    receiver_ref,
    halo_ref,
    w_ref,
    vec_ref,
    nout_ref,
    eout_hbm,
    nbase_ref,
    egrad_hbm,
    grad_ref,
    gvec_ref,
    hback_ref,
    node_v,
    edge_v,
    ncot_v,
    ecot_v,
    eout_v,
    egrad_v,
    gather_t,
    gather,
    table,
    hidden_v,
    slope_v,
    normed_v,
    inv_v,
    dz_v,
    da_v,
    summed_v,
    dsum_v,
    sc_own,
    sc_recv,
    sc_halo,
    acc,
    sem_in,
    sem_out,
):
    roll, nodes, width = node_v.shape
    edges = edge_v.shape[1]
    peers, per_peer = sc_halo.shape[0], sc_halo.shape[2]
    halo = peers * per_peer
    known = nodes + halo
    padded = table.shape[1]
    chunk = 256
    pieces = edges // chunk

    copies = []
    for i, (src, dst) in enumerate(
        ((node_hbm, node_v), (edge_hbm, edge_v), (ncot_hbm, ncot_v), (ecot_hbm, ecot_v))
    ):
        copies.append(pltpu.make_async_copy(src.at[0], dst, sem_in.at[i]))
        copies[-1].start()

    slot_of = []
    for b in range(NBLOCK):
        found = jnp.int32(0)
        for s in range(slot_block_ref.shape[0]):
            found = jnp.where(slot_block_ref[s] == b, jnp.int32(s), found)
        slot_of.append(found)

    def weight(b):
        return w_ref[slot_of[b]]

    def live(t):
        return jnp.where(t < rollout_ref[0], 1.0, 0.0).astype(f32)

    ids = lax.broadcasted_iota(jnp.int32, (padded, edges), 0)
    onehot = (ids == sender_ref[...]) | (ids == receiver_ref[...] + known)
    onehot = jnp.where(onehot, 1.0, 0.0).astype(f32)
    gather_t[...] = onehot.astype(bf16)
    gather[...] = onehot.T.astype(bf16)
    table[...] = jnp.zeros_like(table)
    acc[...] = jnp.zeros_like(acc)

    copies[0].wait()
    flat_nodes = node_v[...].reshape(roll * nodes, width)
    own_sent = dot(flat_nodes, weight(1))
    own_recv = dot(flat_nodes, weight(2))
    halo_sent = dot(halo_ref[...], weight(1)).reshape(peers, roll, per_peer, width)
    for t in range(roll):
        table[t, :nodes] = own_sent[t * nodes : (t + 1) * nodes].astype(bf16)
        table[t, nodes:known] = halo_sent[:, t].reshape(halo, width).astype(bf16)
        table[t, known : known + nodes] = own_recv[t * nodes : (t + 1) * nodes].astype(bf16)
    copies[1].wait()

    def forward(t, carry):
        lv = live(t)
        total = jnp.zeros((nodes, width), f32)
        for c in range(pieces):
            rows = pl.ds(c * chunk, chunk)
            edge = edge_v[t, rows]
            z = dot(edge, weight(0)) + dot(gather[rows], table[t]) + vec_ref[0:1]
            hidden, slope, normed, inverse = branch_forward(z, weight(3), vec_ref[1:2])
            hidden_v[t, rows] = hidden
            slope_v[t, rows] = slope.astype(bf16)
            normed_v[t, rows] = normed.astype(bf16)
            inv_v[t, rows] = inverse
            new = edge.astype(f32) + (normed * vec_ref[2:3] + vec_ref[3:4])
            eout_v[t, rows] = (new * lv).astype(bf16)
            total += dot(gather_t[known : known + nodes, rows], new.astype(bf16))
        summed_v[pl.ds(t * nodes, nodes)] = total.astype(bf16)
        pltpu.make_async_copy(eout_v.at[t], eout_hbm.at[0, t], sem_out.at[t]).start()
        return carry

    lax.fori_loop(0, roll, forward, 0)

    flat_nodes = node_v[...].reshape(roll * nodes, width)
    summed = summed_v[...]
    z = dot(flat_nodes, weight(4)) + dot(summed, weight(5)) + vec_ref[4:5]
    hidden, slope, normed, inverse = branch_forward(z, weight(6), vec_ref[5:6])
    row_t = lax.broadcasted_iota(jnp.int32, (roll * nodes, 1), 0) // nodes
    row_live = jnp.where(row_t < rollout_ref[0], 1.0, 0.0).astype(f32)
    new = flat_nodes.astype(f32) + (normed * vec_ref[6:7] + vec_ref[7:8])
    nout_ref[0] = (new * row_live).astype(bf16).reshape(roll, nodes, width)
    copies[2].wait()
    d_new = ncot_v[...].reshape(roll * nodes, width).astype(f32) * row_live
    acc[6] += eights(d_new * normed)
    acc[7] += eights(d_new)
    d_after = norm_backward(d_new, normed, inverse, vec_ref[6:7])
    acc[5] += eights(d_after.astype(f32))
    grad_ref[6] = dot_ta(hidden, d_after)
    d_before = (dot_tb(d_after, weight(6)) * slope).astype(bf16)
    acc[4] += eights(d_before.astype(f32))
    grad_ref[4] = dot_ta(flat_nodes, d_before)
    grad_ref[5] = dot_ta(summed, d_before)
    dsum_v[...] = dot_tb(d_before, weight(5)).astype(bf16)
    nbase_ref[...] = d_new + dot_tb(d_before, weight(4))
    grad_ref[0] = jnp.zeros((width, width), f32)
    grad_ref[3] = jnp.zeros((width, width), f32)
    copies[3].wait()

    def backward(t, carry):
        lv = live(t)
        for c in range(pieces):
            rows = pl.ds(c * chunk, chunk)
            d_new = ecot_v[t, rows].astype(f32) * lv + dot(
                gather[rows, known : known + nodes], dsum_v[pl.ds(t * nodes, nodes)]
            )
            normed = normed_v[t, rows].astype(f32)
            acc[2] += eights(d_new * normed)
            acc[3] += eights(d_new)
            d_after = norm_backward(d_new, normed, inv_v[t, rows], vec_ref[2:3])
            acc[1] += eights(d_after.astype(f32))
            da_v[rows] = d_after
            d_before = (dot_tb(d_after, weight(3)) * slope_v[t, rows].astype(f32)).astype(bf16)
            acc[0] += eights(d_before.astype(f32))
            dz_v[rows] = d_before
            egrad_v[t, rows] = (d_new + dot_tb(d_before, weight(0))).astype(bf16)
        pltpu.make_async_copy(egrad_v.at[t], egrad_hbm.at[0, t], sem_out.at[roll + t]).start()
        grad_ref[3] += dot_ta(hidden_v[t], da_v[...])
        grad_ref[0] += dot_ta(edge_v[t], dz_v[...])
        scattered = dot(gather_t[...], dz_v[...])
        sc_own[pl.ds(t * nodes, nodes)] = scattered[:nodes].astype(bf16)
        sc_recv[pl.ds(t * nodes, nodes)] = scattered[known : known + nodes].astype(bf16)
        sc_halo[:, t] = scattered[nodes:known].reshape(peers, per_peer, width)
        return carry

    lax.fori_loop(0, roll, backward, 0)

    halo_sum = sc_halo[...].reshape(roll * halo, width).astype(bf16)
    grad_ref[1] = dot_ta(flat_nodes, sc_own[...]) + dot_ta(halo_ref[...], halo_sum)
    grad_ref[2] = dot_ta(flat_nodes, sc_recv[...])
    hback_ref[...] = dot_tb(halo_sum, weight(1)).astype(bf16)
    nbase_ref[...] += dot_tb(sc_own[...], weight(1)) + dot_tb(sc_recv[...], weight(2))
    gvec_ref[...] = jnp.sum(acc[...], axis=1)

    for t in range(roll):
        pltpu.make_async_copy(eout_v.at[t], eout_hbm.at[0, t], sem_out.at[t]).wait()
        pltpu.make_async_copy(egrad_v.at[t], egrad_hbm.at[0, t], sem_out.at[roll + t]).wait()


def layer(
    rollout_length,
    slot_block,
    node_state,
    edge_state,
    node_cotangent,
    edge_cotangent,
    edge_sender,
    edge_receiver,
    halo,
    slots,
    vector_params,
    per_peer,
):
    _, roll, nodes, width = node_state.shape
    edges = edge_state.shape[2]
    peers = halo.shape[0] // (roll * per_peer)
    known = nodes + peers * per_peer
    padded = -(-(known + nodes) // 128) * 128
    vmem = pl.BlockSpec(memory_space=pltpu.VMEM)
    smem = pl.BlockSpec(memory_space=pltpu.SMEM)
    hbm = pl.BlockSpec(memory_space=pl.ANY)
    shape = jax.ShapeDtypeStruct
    return pl.pallas_call(
        layer_kernel,
        out_shape=(
            shape(node_state.shape, bf16),
            shape(edge_state.shape, bf16),
            shape((roll * nodes, width), f32),
            shape(edge_state.shape, bf16),
            shape((NBLOCK, width, width), f32),
            shape((8, width), f32),
            shape(halo.shape, bf16),
        ),
        in_specs=[smem, smem, hbm, hbm, hbm, hbm, vmem, vmem, vmem, vmem, vmem],
        out_specs=(vmem, hbm, vmem, hbm, vmem, vmem, vmem),
        scratch_shapes=[
            pltpu.VMEM((roll, nodes, width), bf16),
            pltpu.VMEM((roll, edges, width), bf16),
            pltpu.VMEM((roll, nodes, width), bf16),
            pltpu.VMEM((roll, edges, width), bf16),
            pltpu.VMEM((roll, edges, width), bf16),
            pltpu.VMEM((roll, edges, width), bf16),
            pltpu.VMEM((padded, edges), bf16),
            pltpu.VMEM((edges, padded), bf16),
            pltpu.VMEM((roll, padded, width), bf16),
            pltpu.VMEM((roll, edges, width), bf16),
            pltpu.VMEM((roll, edges, width), bf16),
            pltpu.VMEM((roll, edges, width), bf16),
            pltpu.VMEM((roll, edges, 1), f32),
            pltpu.VMEM((edges, width), bf16),
            pltpu.VMEM((edges, width), bf16),
            pltpu.VMEM((roll * nodes, width), bf16),
            pltpu.VMEM((roll * nodes, width), bf16),
            pltpu.VMEM((roll * nodes, width), bf16),
            pltpu.VMEM((roll * nodes, width), bf16),
            pltpu.VMEM((peers, roll, per_peer, width), f32),
            pltpu.VMEM((8, 8, width), f32),
            pltpu.SemaphoreType.DMA((4,)),
            pltpu.SemaphoreType.DMA((2 * roll,)),
        ],
        compiler_params=pltpu.CompilerParams(vmem_limit_bytes=60 << 20),
        name="layer",
    )(
        rollout_length,
        slot_block,
        node_state,
        edge_state,
        node_cotangent,
        edge_cotangent,
        edge_sender.reshape(1, edges),
        edge_receiver.reshape(1, edges),
        halo,
        slots,
        vector_params,
    )


def adam_direction(moment_one, moment_two, fix_one, fix_two):
    return moment_one / fix_one / (jnp.sqrt(moment_two / fix_two) + adam_epsilon)


MESH = pl.DeviceIdType.MESH


class Place:
    def __init__(self):
        self.z = lax.axis_index("dp")
        self.n = lax.axis_index("node")
        self.c = lax.rem(self.n, 2)
        self.x = lax.rem(self.n // 2, 2)
        self.y = self.n // 4
        self.xn = self.n + 2 - 4 * self.x
        self.yn = self.n + 4 - 8 * self.y
        self.sib = self.n + 1 - 2 * self.c
        self.diag = self.xn + 4 - 8 * self.y


def remote(src, dst, send, recv, z, n):
    return pltpu.make_async_remote_copy(
        src_ref=src, dst_ref=dst, send_sem=send, recv_sem=recv, device_id=(z, n), device_id_type=MESH
    )


def greet_start(p, depth, peers):
    barrier = pltpu.get_barrier_semaphore()
    for k in range(1, peers):
        to = lax.rem(p.n + k, peers)
        pl.semaphore_signal(barrier, inc=1, device_id=(p.z, to), device_id_type=MESH)
    for k in range(1, depth):
        to = lax.rem(p.z + k, depth)
        pl.semaphore_signal(barrier, inc=1, device_id=(to, p.n), device_id_type=MESH)


def greet_end(depth, peers):
    pl.semaphore_wait(pltpu.get_barrier_semaphore(), peers + depth - 2)


ORDER = ((0, 1, 2, 3), (1, 0, 2, 3), (2, 3, 1, 0), (3, 2, 1, 0))


def gather_start(p, buf, k, sems):
    send, recv = sems
    own = buf(k, p.n)
    copies = []
    for i, to in ((0, p.xn), (1, p.yn), (3, p.sib)):
        copies.append(remote(own, own, send.at[i, k], recv.at[i, k], p.z, to))
        copies[-1].start()
    return copies


def gather_side(p, buf, k, sems):
    send, recv = sems
    copies = []
    for i, owner in ((0, p.xn), (1, p.yn)):
        got = buf(k, owner)
        remote(got, got, send.at[i, k], recv.at[i, k], p.z, owner).wait_recv()
        on = remote(got, got, send.at[4 + i, k], recv.at[4 + i, k], p.z, p.sib)
        on.start()
        copies.append(on)
        over = remote(got, got, send.at[2, k], recv.at[2, k], p.z, p.yn if i == 0 else p.xn)
        pl.when(p.c == i)(over.start)
    copies.append(over)
    return copies


def gather_far(p, buf, k, sems):
    send, recv = sems
    got = buf(k, p.diag)
    remote(got, got, send.at[2, k], recv.at[2, k], p.z, p.xn).wait_recv()
    on = remote(got, got, send.at[6, k], recv.at[6, k], p.z, p.sib)
    on.start()
    return [on]


def gather_end(p, buf, k, sems):
    send, recv = sems
    for i in (3, 4, 5, 6):
        got = buf(k, p.sib)
        remote(got, got, send.at[i, k], recv.at[i, k], p.z, p.sib).wait_recv()


class Step:
    def __init__(self, **refs):
        self.__dict__.update(refs)


def step_kernel(names, *refs):
    k = Step(**dict(zip(names, refs, strict=True)))
    p = Place()
    depth, peers = 4, 8
    roll, nodes, width = k.node_v.shape
    edges = k.edge_v.shape[1]
    slot_dev, rows = k.weight_v.shape[:2]
    per_peer = k.halo.shape[1] // roll
    halo = peers * per_peer
    known = nodes + halo
    padded = k.table.shape[1]
    chunk = edges
    pieces = edges // chunk
    going = []

    def launch(src, dst, send, recv, z, n):
        copy = remote(src, dst, send, recv, z, n)
        copy.start()
        going.append((copy, None))

    def landed(dst, recv):
        remote(dst, dst, recv, recv, p.z, p.sib).wait_recv()

    loads = []
    for i, (src, dst) in enumerate(
        (
            (k.weight_hbm, k.weight_v),
            (k.node_hbm.at[0], k.node_v),
            (k.left_hbm, k.grad.at[2, :slot_dev]),
            (k.right_hbm, k.grad.at[:slot_dev]),
            (k.edge_hbm.at[0], k.edge_v),
            (k.ncot_hbm.at[0], k.ncot_v),
            (k.ecot_hbm.at[0], k.egrad_v.at[0]),
            (k.first_hbm, k.first_v),
            (k.second_hbm, k.second_v),
        )
    ):
        loads.append(pltpu.make_async_copy(src, dst, k.in_sem.at[i]))
        loads[-1].start()
    greet_start(p, depth, peers)

    def buf(slot, n):
        return k.slots.at[slot, n]

    wsems = (k.w_send, k.w_recv)
    order = []

    def arrive(j):
        z_of = 0
        for z in range(depth):
            z_of = z_of + jnp.where(p.z == z, ORDER[z][j // slot_dev], 0)
        slot = z_of * slot_dev + j % slot_dev
        order.append(slot)
        piece = buf(slot, p.n)
        if j >= slot_dev:
            remote(piece, piece, k.wz_send.at[0, slot], k.wz_recv.at[slot], p.z, p.n).wait_recv()
        for i, test, to in (
            (0, (z_of <= p.z) & (p.z < depth - 1), p.z + 1),
            (1, (z_of >= p.z) & (p.z > 0), p.z - 1),
        ):
            copy = remote(piece, piece, k.wz_send.at[i, slot], k.wz_recv.at[slot], to, p.n)
            pl.when(test)(copy.start)
            going.append((copy, test))
        going.extend((copy, None) for copy in gather_start(p, buf, slot, wsems))

    def side(j):
        going.extend((copy, None) for copy in gather_side(p, buf, order[j], wsems))

    def far(j):
        going.extend((copy, None) for copy in gather_far(p, buf, order[j], wsems))

    loads[0].wait()
    k.slots[pl.ds(slot_dev * p.z, slot_dev), p.n] = k.weight_v[...].astype(bf16)
    greet_end(depth, peers)

    def rounds(*names):
        for name in names:
            {"a": arrive, "s": side, "f": far}[name[0]](int(name[1:]))

    rounds("a0", "a1")
    loads[1].wait()
    node_ids = lax.broadcasted_iota(jnp.int32, (nodes, halo), 0)
    pick_t = jnp.where(node_ids == k.rows_ref[...], 1.0, 0.0).astype(bf16)
    for t in range(roll):
        k.spread[:, t] = dot_ta(pick_t, k.node_v[t]).reshape(peers, per_peer, width)
    k.hput[...] = k.spread[...].reshape(peers, roll * per_peer, width).astype(bf16)
    k.halo[p.n] = k.hput[p.n]
    rounds("a2", "a3", "s0", "s1")
    hsent = []
    for i in range(1, peers):
        to = lax.rem(p.n + i, peers)
        hsent.append(remote(k.hput.at[to], k.halo.at[p.n], k.h_send.at[0, i], k.h_recv.at[0, i], p.z, to))
        hsent[-1].start()
    loads[2].wait()
    for s in range(slot_dev):
        k.pre[2 * slot_dev + s, p.n] = k.grad[2, s].astype(bf16)
        for m in range(peers):
            k.lput[s, m] = k.grad[2, s, :, m * rows : (m + 1) * rows].astype(bf16)
    k.lgot[:, p.n] = k.lput[:, p.n]
    rounds("a4", "a5", "s2", "s3", "f0", "f1")
    ids = lax.broadcasted_iota(jnp.int32, (padded, edges), 0)
    onehot = (ids == k.sender_ref[...].reshape(1, edges)) | (
        ids == k.receiver_ref[...].reshape(1, edges) + known
    )
    onehot = jnp.where(onehot, 1.0, 0.0).astype(f32)
    k.gather_t[...] = onehot.astype(bf16)
    rounds("a6", "a7", "s4", "s5", "f2", "f3")
    k.gather[...] = onehot.T.astype(bf16)
    k.table[:, known + nodes :] = jnp.zeros((roll, padded - known - nodes, width), bf16)
    k.acc[...] = jnp.zeros_like(k.acc)
    rounds("s6", "s7", "f4", "f5")
    loads[3].wait()
    for s in range(slot_dev):
        k.right_b[s] = k.grad[s].reshape(width, width).astype(bf16)
    rounds("f6", "f7")
    for copy in hsent:
        copy.wait_send()
    for i in range(1, peers):
        landed(k.halo.at[0], k.h_recv.at[0, i])
    for slot in order:
        gather_end(p, buf, slot, wsems)

    slot_of = []
    for b in range(NBLOCK):
        found = 0
        for s in range(depth * slot_dev):
            found = jnp.where(k.slot_block_ref[s] == b, s, found)
        slot_of.append(found)

    def weight(b):
        return k.slots[slot_of[b]].reshape(width, width)

    rollout = k.rollout_ref[0]
    vec = k.vec_ref

    def live(t):
        return jnp.where(t < rollout, 1.0, 0.0).astype(f32)

    def flat_nodes():
        return k.node_v[...].reshape(roll * nodes, width)

    own_sent = dot(flat_nodes(), weight(1))
    own_recv = dot(flat_nodes(), weight(2))
    halo_flat = k.halo[...].reshape(roll * halo, width)
    halo_sent = dot(halo_flat, weight(1)).reshape(peers, roll, per_peer, width)
    for t in range(roll):
        k.table[t, :nodes] = own_sent[t * nodes : (t + 1) * nodes].astype(bf16)
        k.table[t, nodes:known] = halo_sent[:, t].reshape(halo, width).astype(bf16)
        k.table[t, known : known + nodes] = own_recv[t * nodes : (t + 1) * nodes].astype(bf16)
    loads[4].wait()

    for i in range(1, peers):
        to = lax.rem(p.n + i, peers)
        launch(k.lput.at[:, to], k.lgot.at[:, p.n], k.l_send.at[i], k.l_recv.at[i], p.z, to)
    loads[7].wait()
    loads[8].wait()
    psems = (k.p_send, k.p_recv)
    early = range(3 * slot_dev)
    pbuf = lambda i, n: k.pre.at[i, n]
    for s in range(slot_dev):
        k.pre[s, p.n] = k.first_v[s].astype(bf16)
        k.pre[slot_dev + s, p.n] = k.second_v[s].astype(bf16)
    for i in early:
        going.extend((copy, None) for copy in gather_start(p, pbuf, i, psems))

    def forward(t, carry):
        lv = live(t)
        total = jnp.zeros((nodes, width), f32)
        for c in range(pieces):
            at = pl.ds(c * chunk, chunk)
            edge = k.edge_v[t, at]
            z = dot(edge, weight(0)) + dot(k.gather[at], k.table[t]) + vec[0:1]
            hidden, slope, normed, inverse = branch_forward(z, weight(3), vec[1:2])
            k.hidden_v[t, at] = hidden
            k.slope_v[t, at] = slope.astype(bf16)
            k.normed_v[t, at] = normed.astype(bf16)
            k.inv_v[t, at] = inverse
            new = edge.astype(f32) + (normed * vec[2:3] + vec[3:4])
            k.eout_v[0, t, at] = (new * lv).astype(bf16)
            total += dot(k.gather_t[known : known + nodes, at], new.astype(bf16))
        k.summed_v[pl.ds(t * nodes, nodes)] = total.astype(bf16)
        return carry

    lax.fori_loop(0, roll, forward, 0)

    on_f = jnp.where(p.c == 0, p.x, p.y)
    on_g = jnp.where(p.c == 0, p.y, p.x)
    to_f = jnp.where(p.c == 0, p.xn, p.yn)
    to_g = jnp.where(p.c == 0, p.yn, p.xn)

    def spot(f, g):
        return jnp.where(p.c == 0, g * 2 + f, f * 2 + g)

    def hop(stage, b):
        put, got, to = (
            (k.cast, k.got_core, p.sib),
            (k.put_one, k.got_one, to_f),
            (k.put_two, k.got_two, to_g),
        )[stage]
        at = stage * NBLOCK + b
        return remote(put.at[b], got.at[b], k.r_send.at[at], k.r_recv.at[at], p.z, to)

    def to_core(b):
        for i in range(peers // 2):
            k.cast[b, i] = k.grad[b, 2 * i + 1 - p.c].astype(bf16)
        hop(0, b).start()

    def to_first(b):
        hop(0, b).wait_recv()
        for g in range(2):
            at = spot(1 - on_f, g)
            k.put_one[b, g] = (k.grad[b, 2 * at + p.c] + k.got_core[b, at].astype(f32)).astype(bf16)
        hop(1, b).start()
        for g in range(2):
            at = spot(on_f, g)
            k.grad[b, 2 * at + p.c] = k.grad[b, 2 * at + p.c] + k.got_core[b, at].astype(f32)

    def to_second(b):
        hop(1, b).wait_recv()
        at = spot(on_f, 1 - on_g)
        total = k.grad[b, 2 * at + p.c] + k.got_one[b, 1 - on_g].astype(f32)
        k.put_two[b] = total.astype(bf16)
        hop(2, b).start()
        k.grad[b, p.n] = k.grad[b, p.n] + k.got_one[b, on_g].astype(f32)

    def settle(b):
        hop(2, b).wait_recv()
        k.grad[b, p.n] = k.grad[b, p.n] + k.got_two[b].astype(f32)

    def put_grad(b, value):
        k.grad[b] = value.reshape(peers, rows, width)

    summed = k.summed_v[...]
    z = dot(flat_nodes(), weight(4)) + dot(summed, weight(5)) + vec[4:5]
    hidden, slope, normed, inverse = branch_forward(z, weight(6), vec[5:6])
    row_t = lax.broadcasted_iota(jnp.int32, (roll * nodes, 1), 0) // nodes
    row_live = jnp.where(row_t < rollout, 1.0, 0.0).astype(f32)
    new = flat_nodes().astype(f32) + (normed * vec[6:7] + vec[7:8])
    k.nout_v[0] = (new * row_live).astype(bf16).reshape(roll, nodes, width)
    loads[5].wait()
    d_new = k.ncot_v[...].reshape(roll * nodes, width).astype(f32) * row_live
    k.acc[6] = eights(d_new * normed)
    k.acc[7] = eights(d_new)
    d_after = norm_backward(d_new, normed, inverse, vec[6:7])
    k.acc[5] = eights(d_after.astype(f32))
    put_grad(6, dot_ta(hidden, d_after))
    to_core(6)
    d_before = (dot_tb(d_after, weight(6)) * slope).astype(bf16)
    k.acc[4] = eights(d_before.astype(f32))
    put_grad(4, dot_ta(flat_nodes(), d_before))
    to_core(4)
    put_grad(5, dot_ta(summed, d_before))
    to_core(5)
    k.summed_v[...] = dot_tb(d_before, weight(5)).astype(bf16)
    k.table[:, 2 * nodes : 3 * nodes] = d_before.reshape(roll, nodes, width)
    for i in early:
        going.extend((copy, None) for copy in gather_side(p, pbuf, i, psems))
    k.grad[0] = jnp.zeros((peers, rows, width), f32)
    k.grad[3] = jnp.zeros((peers, rows, width), f32)
    loads[6].wait()

    def backward(t, carry):
        lv = live(t)
        for c in range(pieces):
            at = pl.ds(c * chunk, chunk)
            d_new = k.egrad_v[0, t, at].astype(f32) * lv + dot(
                k.gather[at, known : known + nodes], k.summed_v[pl.ds(t * nodes, nodes)]
            )
            k.egrad_v[0, t, at] = d_new.astype(bf16)
            normed = k.normed_v[t, at].astype(f32)
            k.acc[2] += eights(d_new * normed)
            k.acc[3] += eights(d_new)
            d_after = norm_backward(d_new, normed, k.inv_v[t, at], vec[2:3])
            k.acc[1] += eights(d_after.astype(f32))
            k.normed_v[t, at] = d_after
            d_before = (dot_tb(d_after, weight(3)) * k.slope_v[t, at].astype(f32)).astype(bf16)
            k.acc[0] += eights(d_before.astype(f32))
            k.slope_v[t, at] = d_before
        k.grad[3] += dot_ta(k.hidden_v[t], k.normed_v[t]).reshape(peers, rows, width)
        k.grad[0] += dot_ta(k.edge_v[t], k.slope_v[t]).reshape(peers, rows, width)
        scattered = dot(k.gather_t[...], k.slope_v[t])
        k.table[t, :nodes] = scattered[:nodes].astype(bf16)
        k.table[t, nodes : 2 * nodes] = scattered[known : known + nodes].astype(bf16)
        k.spread[:, t] = scattered[nodes:known].reshape(peers, per_peer, width)
        for step, work in enumerate((to_first, to_second, settle)):

            @pl.when(t == step)
            def _():
                def one(b, carry):
                    work(b)
                    return carry

                lax.fori_loop(4, NBLOCK, one, 0)

        return carry

    lax.fori_loop(0, roll, backward, 0)

    to_core(3)
    to_core(0)
    k.hput[...] = k.spread[...].reshape(peers, roll * per_peer, width).astype(bf16)
    def kept(i):
        return k.table[:, i * nodes : (i + 1) * nodes].reshape(roll * nodes, width)

    put_grad(1, dot_ta(flat_nodes(), kept(0)) + dot_ta(halo_flat, k.hput[...].reshape(roll * halo, width)))
    to_core(1)
    to_first(3)
    put_grad(2, dot_ta(flat_nodes(), kept(1)))
    to_core(2)
    to_first(0)
    k.vput[0] = jnp.sum(k.acc[...], axis=1)
    launch(k.vput.at[0], k.vgot.at[0], k.v_send.at[0], k.v_recv.at[0], p.z, p.sib)
    to_first(1)
    to_second(3)
    to_first(2)
    landed(k.vgot.at[0], k.v_recv.at[0])
    k.vput[1] = k.vput[0] + k.vgot[0]
    launch(k.vput.at[1], k.vgot.at[1], k.v_send.at[1], k.v_recv.at[1], p.z, p.xn)
    to_second(0)
    for i in early:
        going.extend((copy, None) for copy in gather_far(p, pbuf, i, psems))

    def edge_gradient(t):
        for c in range(pieces):
            at = pl.ds(c * chunk, chunk)
            grown = k.egrad_v[0, t, at].astype(f32) + dot_tb(k.slope_v[t, at], weight(0))
            k.egrad_v[0, t, at] = grown.astype(bf16)

    to_second(1)
    settle(3)
    to_second(2)
    settle(0)
    landed(k.vgot.at[1], k.v_recv.at[1])
    k.vput[2] = k.vput[1] + k.vgot[1]
    launch(k.vput.at[2], k.vgot.at[2], k.v_send.at[2], k.v_recv.at[2], p.z, p.yn)
    for i in range(1, peers):
        to = lax.rem(p.n + i, peers)
        launch(k.hput.at[to], k.hret.at[p.n], k.h_send.at[1, i], k.h_recv.at[1, i], p.z, to)
    k.hret[p.n] = k.hput[p.n]
    settle(1)
    settle(2)

    def part(target, s):
        b = k.slot_block_ref[target * slot_dev + s]
        held = k.grad[jnp.minimum(b, NBLOCK - 1), p.n]
        return jnp.where(b < NBLOCK, held, 0.0)

    def pass_on(way):
        put, got = (k.put_up, k.got_up) if way == 0 else (k.put_down, k.got_down)
        source = p.z > 0 if way == 0 else p.z < depth - 1
        for i in range(depth - 1):
            target = depth - 1 - i if way == 0 else i
            test = p.z < target if way == 0 else p.z > target
            at = p.z + 1 if way == 0 else p.z - 1

            @pl.when(test)
            def _():
                for s in range(slot_dev):

                    @pl.when(source)
                    def _():
                        landed(got.at[target, s], k.z_recv.at[way, target, s])
                        total = part(target, s) + got[target, s].astype(f32)
                        put[target, s] = total.astype(bf16)

                    @pl.when(jnp.logical_not(source))
                    def _():
                        put[target, s] = part(target, s).astype(bf16)

                    remote(
                        put.at[target, s],
                        got.at[target, s],
                        k.z_send.at[way, target, s],
                        k.z_recv.at[way, target, s],
                        at,
                        p.n,
                    ).start()

    @pl.when(p.z == 0)
    def _():
        pass_on(0)

    @pl.when(p.z == depth - 1)
    def _():
        pass_on(1)

    edge_gradient(0)

    @pl.when(p.z == 1)
    def _():
        pass_on(0)

    @pl.when(p.z == depth - 2)
    def _():
        pass_on(1)

    edge_gradient(1)

    @pl.when(p.z == 1)
    def _():
        pass_on(1)

    @pl.when(p.z == depth - 2)
    def _():
        pass_on(0)

    landed(k.vgot.at[2], k.v_recv.at[2])
    k.vput[3] = k.vput[2] + k.vgot[2]
    k.vz[p.z] = k.vput[3]
    for i in range(1, depth):
        to = lax.rem(p.z + i, depth)
        launch(k.vput.at[3], k.vz.at[p.z], k.v_send.at[2 + i], k.v_recv.at[2 + i], to, p.n)
    edge_gradient(2)
    square = jnp.zeros((8, width), f32)
    gsems = (k.g_send, k.g_recv)
    gbuf = lambda s, n: k.full.at[s, n]
    for s in range(slot_dev):

        @pl.when(p.z > 0)
        def _():
            landed(k.got_up.at[p.z, s], k.z_recv.at[0, p.z, s])

        @pl.when(p.z < depth - 1)
        def _():
            landed(k.got_down.at[p.z, s], k.z_recv.at[1, p.z, s])

        mine = part(p.z, s) + jnp.where(p.z > 0, k.got_up[p.z, s].astype(f32), 0.0)
        mine = mine + jnp.where(p.z < depth - 1, k.got_down[p.z, s].astype(f32), 0.0)
        k.full[s, p.n] = mine.astype(bf16)
        for copy in gather_start(p, gbuf, s, gsems):
            going.append((copy, None))
        square = square + eights(mine * mine)
    square = square[:, :128] + square[:, 128:256] + square[:, 256:384] + square[:, 384:]
    k.sput[...] = square
    k.sgot[p.n] = square
    for i in range(1, peers):
        to = lax.rem(p.n + i, peers)
        launch(k.sput, k.sgot.at[p.n], k.n_send.at[i], k.n_recv.at[i], p.z, to)
    edge_gradient(3)

    def collect(buffer, sems, finish):
        for s in range(slot_dev):
            going.extend((copy, None) for copy in gather_side(p, buffer, s, sems))
        for s in range(slot_dev):
            going.extend((copy, None) for copy in gather_far(p, buffer, s, sems))
        for s in range(slot_dev):
            gather_end(p, buffer, s, sems)
            finish(s)

    for i in range(1, peers):
        landed(k.sgot.at[0], k.n_recv.at[i])
    k.szput[...] = jnp.sum(k.sgot[...], axis=0)
    k.sz[p.z] = k.szput[...]
    for i in range(1, depth):
        to = lax.rem(p.z + i, depth)
        launch(k.szput, k.sz.at[p.z], k.n_send.at[peers - 1 + i], k.n_recv.at[peers - 1 + i], to, p.n)

    limit = math.sqrt(NBLOCK * width * width + 8 * width)
    found = []

    for i in range(1, peers):
        landed(k.hret.at[0], k.h_recv.at[1, i])
    back = k.hret[...].astype(f32).reshape(peers, roll, per_peer, width)
    for t in range(roll):
        rows_t = back[:, t].reshape(halo, width).astype(bf16)
        k.table[t, :nodes] = (k.table[t, :nodes].astype(f32) + dot(pick_t, rows_t)).astype(bf16)
    grown = k.ncot_v[...].reshape(roll * nodes, width).astype(f32) * row_live
    grown = grown + dot_tb(kept(0), weight(1)) + dot_tb(kept(1), weight(2)) + dot_tb(kept(2), weight(4))
    k.ngrad_v[0] = grown.astype(bf16).reshape(roll, nodes, width)

    def fix(beta, step):
        return 1.0 - jnp.exp2(math.log2(beta) * jnp.full((1, 1), step, jnp.int32).astype(f32))

    def norm():
        for i in range(1, depth):
            landed(k.vz.at[0], k.v_recv.at[2 + i])
            landed(k.sz.at[0], k.n_recv.at[peers - 1 + i])
        vectors = k.vz[0] + k.vz[1] + k.vz[2] + k.vz[3]
        square_sum = jnp.sum(k.sz[0] + k.sz[1] + k.sz[2] + k.sz[3], keepdims=True).reshape(1, 1)
        square_sum = square_sum + jnp.sum(vectors * vectors, keepdims=True).reshape(1, 1)
        value = jnp.sqrt(square_sum)
        k.norm_v[...] = jnp.broadcast_to(value, k.norm_v.shape)
        found.extend((vectors, jnp.minimum(1.0, limit / value)))

    def advance(s):
        part_left = dot(k.pre[2 * slot_dev + s].reshape(width, width), k.full[s].reshape(width, width))
        rotated = dot(part_left.astype(bf16), k.right_b[s])
        if s == 0:
            norm()
        k.grad[s] = rotated.reshape(peers, rows, width)
        step = k.step_ref[p.z * slot_dev + s]
        fix_one, fix_two = fix(beta_first, step), fix(beta_second, step)
        clip = found[1]

        def moments(first, second, turn):
            spun = turn * clip
            return (
                beta_first * first + (1.0 - beta_first) * spun,
                beta_second * second + (1.0 - beta_second) * spun * spun,
            )

        one, two = moments(
            k.pre[s].reshape(width, width).astype(f32),
            k.pre[slot_dev + s].reshape(width, width).astype(f32),
            rotated,
        )
        direction = adam_direction(one, two, fix_one, fix_two).astype(bf16)
        turned = dot_tb(direction, k.right_b[s]).astype(bf16)
        reverted = dot_ta(k.lgot[s].reshape(width, rows), turned)
        new = k.weight_v[s] - rate_matrix * (reverted + weight_decay * k.weight_v[s])
        k.wnew_v[s] = new
        k.wcopy_v[s] = new.astype(bf16)
        one, two = moments(k.first_v[s], k.second_v[s], k.grad[s, p.n])
        k.first_v[s] = one
        k.second_v[s] = two

    for i in range(1, peers):
        landed(k.lgot.at[:, 0], k.l_recv.at[i])
    for i in early:
        gather_end(p, pbuf, i, psems)
    collect(gbuf, gsems, advance)
    grad_vectors, clip = found
    step = k.step_ref[depth * slot_dev]
    spun = grad_vectors * clip
    one = beta_first * k.vfirst_ref[...] + (1.0 - beta_first) * spun
    two = beta_second * k.vsecond_ref[...] + (1.0 - beta_second) * spun * spun
    k.vstate_v[0] = vec[...] - rate_vector * adam_direction(
        one, two, fix(beta_first, step), fix(beta_second, step)
    )
    k.vstate_v[1] = one
    k.vstate_v[2] = two

    for copy, test in going:
        if test is None:
            copy.wait_send()
        else:
            pl.when(test)(copy.wait_send)
    for b in range(NBLOCK):
        for stage in range(3):
            hop(stage, b).wait_send()
    for i in range(depth - 1):
        for s in range(slot_dev):
            for test, target, way, put in (
                (p.z < depth - 1 - i, depth - 1 - i, 0, k.put_up),
                (p.z > i, i, 1, k.put_down),
            ):
                sent = remote(
                    put.at[target, s],
                    put.at[target, s],
                    k.z_send.at[way, target, s],
                    k.z_recv.at[way, target, s],
                    p.z,
                    p.sib,
                )
                pl.when(test)(sent.wait_send)


def store_kernel(*refs):
    count = (len(refs) - 3) // 2
    norm, norm_out, sem = refs[count], refs[-2], refs[-1]
    copies = []
    for i in range(count):
        copies.append(pltpu.make_async_copy(refs[i], refs[count + 1 + i], sem.at[i]))
        copies[-1].start()
    norm_out[0] = norm[0, 0]
    for copy in copies:
        copy.wait()


def whole_step(
    node_state,
    edge_state,
    node_cotangent,
    edge_cotangent,
    send_rows,
    edge_sender,
    edge_receiver,
    rollout_length,
    slot_block,
    step_count,
    weight_slots,
    moment_first,
    moment_second,
    basis_left,
    basis_right,
    vector_params,
    vector_first,
    vector_second,
):
    depth, peers = 4, 8
    _, roll, nodes, width = node_state.shape
    edges = edge_state.shape[2]
    slot_dev, rows = weight_slots.shape[:2]
    halo = send_rows.shape[1]
    per_peer = halo // peers
    padded = -(-(2 * nodes + halo) // 128) * 128
    own = (slot_dev, rows, width)
    tile = (8, 128)
    hbm = pl.BlockSpec(memory_space=pl.ANY)
    vmem = pl.BlockSpec(memory_space=pltpu.VMEM)
    smem = pl.BlockSpec(memory_space=pltpu.SMEM)
    shape = jax.ShapeDtypeStruct
    dma = pltpu.SemaphoreType.DMA
    ins = dict(
        rollout_ref=(rollout_length, smem),
        slot_block_ref=(slot_block, smem),
        step_ref=(step_count, smem),
        node_hbm=(node_state, hbm),
        edge_hbm=(edge_state, hbm),
        ncot_hbm=(node_cotangent, hbm),
        ecot_hbm=(edge_cotangent, hbm),
        rows_ref=(send_rows, vmem),
        sender_ref=(edge_sender, vmem),
        receiver_ref=(edge_receiver, vmem),
        weight_hbm=(weight_slots, hbm),
        first_hbm=(moment_first, hbm),
        second_hbm=(moment_second, hbm),
        left_hbm=(jnp.swapaxes(basis_left, 1, 2), hbm),
        right_hbm=(basis_right.reshape(slot_dev, peers, rows, width), hbm),
        vec_ref=(vector_params, vmem),
        vfirst_ref=(vector_first, vmem),
        vsecond_ref=(vector_second, vmem),
    )
    outs = dict(
        nout_v=shape(node_state.shape, bf16),
        eout_v=shape(edge_state.shape, bf16),
        ngrad_v=shape(node_state.shape, bf16),
        egrad_v=shape(edge_state.shape, bf16),
        first_v=shape(own, f32),
        second_v=shape(own, f32),
        wnew_v=shape(own, f32),
        wcopy_v=shape(own, bf16),
        vstate_v=shape((3, 8, width), f32),
        norm_v=shape(tile, f32),
    )
    v = pltpu.VMEM
    scratch = dict(
        weight_v=v(own, f32),
        node_v=v((roll, nodes, width), bf16),
        edge_v=v((roll, edges, width), bf16),
        ncot_v=v((roll, nodes, width), bf16),
        slots=v((slot_dev * depth, peers, rows, width), bf16),
        halo=v((peers, roll * per_peer, width), bf16),
        spread=v((peers, roll, per_peer, width), f32),
        hput=v((peers, roll * per_peer, width), bf16),
        hret=v((peers, roll * per_peer, width), bf16),
        pre=v((3 * slot_dev, peers, rows, width), bf16),
        lput=v((slot_dev, peers, rows, rows), bf16),
        lgot=v((slot_dev, peers, rows, rows), bf16),
        right_b=v((slot_dev, width, width), bf16),
        gather_t=v((padded, edges), bf16),
        gather=v((edges, padded), bf16),
        table=v((roll, padded, width), bf16),
        hidden_v=v((roll, edges, width), bf16),
        slope_v=v((roll, edges, width), bf16),
        normed_v=v((roll, edges, width), bf16),
        inv_v=v((roll, edges, 1), f32),
        summed_v=v((roll * nodes, width), bf16),
        acc=v((8, 8, width), f32),
        grad=v((NBLOCK, peers, rows, width), f32),
        cast=v((NBLOCK, peers // 2, rows, width), bf16),
        got_core=v((NBLOCK, peers // 2, rows, width), bf16),
        put_one=v((NBLOCK, 2, rows, width), bf16),
        got_one=v((NBLOCK, 2, rows, width), bf16),
        put_two=v((NBLOCK, rows, width), bf16),
        got_two=v((NBLOCK, rows, width), bf16),
        put_up=v((depth, *own), bf16),
        put_down=v((depth, *own), bf16),
        got_up=v((depth, *own), bf16),
        got_down=v((depth, *own), bf16),
        full=v((slot_dev, peers, rows, width), bf16),
        vput=v((4, 8, width), f32),
        vgot=v((3, 8, width), f32),
        vz=v((depth, 8, width), f32),
        sput=v(tile, f32),
        sgot=v((peers, *tile), f32),
        szput=v(tile, f32),
        sz=v((depth, *tile), f32),
        in_sem=dma((9,)),
        w_send=dma((7, depth * slot_dev)),
        w_recv=dma((7, depth * slot_dev)),
        wz_send=dma((2, depth * slot_dev)),
        wz_recv=dma((depth * slot_dev,)),
        h_send=dma((2, peers)),
        h_recv=dma((2, peers)),
        l_send=dma((peers,)),
        l_recv=dma((peers,)),
        r_send=dma((3 * NBLOCK,)),
        r_recv=dma((3 * NBLOCK,)),
        z_send=dma((2, depth, slot_dev)),
        z_recv=dma((2, depth, slot_dev)),
        g_send=dma((7, slot_dev)),
        g_recv=dma((7, slot_dev)),
        p_send=dma((7, 3 * slot_dev)),
        p_recv=dma((7, 3 * slot_dev)),
        v_send=dma((6,)),
        v_recv=dma((6,)),
        n_send=dma((peers + depth - 1,)),
        n_recv=dma((peers + depth - 1,)),
    )
    names = (*ins, *outs, *scratch)
    results = pl.pallas_call(
        functools.partial(step_kernel, names),
        out_shape=tuple(pltpu.VMEM(out.shape, out.dtype) for out in outs.values()),
        in_specs=[spec for _, spec in ins.values()],
        out_specs=(vmem,) * len(outs),
        scratch_shapes=list(scratch.values()),
        compiler_params=pltpu.CompilerParams(
            vmem_limit_bytes=52 << 20, collective_id=0, has_side_effects=True
        ),
        name="step",
    )(
        *(
            pltpu.with_memory_space_constraint(value, pltpu.HBM) if spec is hbm else value
            for value, spec in ins.values()
        )
    )
    final = [*outs.values()][:-1]
    return pl.pallas_call(
        store_kernel,
        out_shape=(*final, shape((1,), f32)),
        in_specs=[vmem] * len(outs),
        out_specs=(*([hbm] * len(final)), smem),
        scratch_shapes=[dma((len(final),))],
        compiler_params=pltpu.CompilerParams(vmem_limit_bytes=40 << 20),
        name="results",
    )(*results)


def local(
    node_state,
    edge_state,
    node_cotangent,
    edge_cotangent,
    send_rows,
    edge_sender,
    edge_receiver,
    rollout_length,
    slot_block,
    step_count,
    weight_slots,
    moment_first,
    moment_second,
    basis_left,
    basis_right,
    vector_params,
    vector_first,
    vector_second,
):
    width = node_state.shape[-1]
    roll, nodes = node_state.shape[1:3]
    clip_limit = math.sqrt(NBLOCK * width * width + 8 * width)
    slot_dev = weight_slots.shape[0]
    slot_total = slot_block.shape[0]
    halo_rows = send_rows.shape[1]
    peers = lax.axis_size("node")
    per_peer = halo_rows // peers
    if (lax.axis_size("dp"), peers) == (4, 8):
        return whole_step(
            node_state,
            edge_state,
            node_cotangent,
            edge_cotangent,
            send_rows,
            edge_sender,
            edge_receiver,
            rollout_length,
            slot_block,
            step_count,
            weight_slots,
            moment_first,
            moment_second,
            basis_left,
            basis_right,
            vector_params,
            vector_first,
            vector_second,
        )
    copies = lax.all_gather(weight_slots.astype(bf16), "node", axis=1, tiled=True)
    slots = lax.all_gather(copies, "dp", axis=0, tiled=True)
    back_onehot = (send_rows[0][:, None] == jnp.arange(nodes, dtype=jnp.int32)[None, :]).astype(bf16)
    outgoing = jnp.einsum("hk,tkd->htd", back_onehot, node_state[0], preferred_element_type=f32)
    outgoing = outgoing.astype(bf16).reshape(peers, per_peer, roll, width).transpose(0, 2, 1, 3)
    outgoing = outgoing.reshape(peers * roll * per_peer, width)
    halo = lax.all_to_all(outgoing, "node", split_axis=0, concat_axis=0, tiled=True)

    node_output, edge_output, node_base, edge_gradient, grads, grad_vectors, halo_back = layer(
        rollout_length,
        slot_block,
        node_state,
        edge_state,
        node_cotangent,
        edge_cotangent,
        edge_sender,
        edge_receiver,
        halo,
        slots,
        vector_params,
        per_peer,
    )
    returned = lax.all_to_all(halo_back, "node", split_axis=0, concat_axis=0, tiled=True)
    returned = returned.reshape(peers, roll, per_peer, width).transpose(0, 2, 1, 3)
    d_back = jnp.einsum(
        "hk,htd->tkd",
        back_onehot,
        returned.reshape(halo_rows, roll, width),
        preferred_element_type=f32,
    )
    node_gradient = node_base.reshape(roll, nodes, width) + d_back
    node_gradient = node_gradient.astype(bf16).reshape(node_state.shape)

    block_of_slot = slot_block[None, :] == jnp.arange(NBLOCK, dtype=jnp.int32)[:, None]
    first = lax.axis_index("dp") * slot_dev
    summed, grad_vectors = lax.psum((grads, grad_vectors), ("dp", "node"))
    own_square = jnp.sum(summed * summed)
    mine = lax.dynamic_slice_in_dim(block_of_slot.astype(f32), first, slot_dev, 1)
    owned_grads = jnp.einsum("bs,bij->sij", mine, summed, precision=highest)
    square_sum = own_square + jnp.sum(grad_vectors * grad_vectors)
    grad_norm = jnp.sqrt(square_sum)
    clip_scale = jnp.minimum(1.0, clip_limit / grad_norm)
    owned_grads = owned_grads * clip_scale
    grad_vectors = grad_vectors * clip_scale
    own_steps = lax.dynamic_slice_in_dim(step_count, first, slot_dev, 0)
    slot_steps = own_steps.astype(f32)[:, None, None]
    fix_one = 1.0 - jnp.power(f32(beta_first), slot_steps)
    fix_two = 1.0 - jnp.power(f32(beta_second), slot_steps)
    rotated = jnp.einsum("sij,sik->sjk", basis_left, owned_grads, precision=highest, preferred_element_type=f32)
    rotated = jnp.einsum("sjk,skl->sjl", rotated, basis_right, precision=highest, preferred_element_type=f32)
    moment_one = beta_first * moment_first + (1.0 - beta_first) * rotated
    moment_two = beta_second * moment_second + (1.0 - beta_second) * rotated * rotated
    direction = adam_direction(moment_one, moment_two, fix_one, fix_two)
    turned = jnp.einsum("sjl,sml->sjm", direction, basis_right, precision=highest, preferred_element_type=f32)
    reverted = jnp.einsum("sij,sjm->ism", basis_left, turned, precision=highest, preferred_element_type=f32)
    reverted = lax.psum_scatter(reverted.astype(bf16), "node", scatter_dimension=0, tiled=True).astype(f32)
    reverted = jnp.transpose(reverted, (1, 0, 2))
    new_weights = weight_slots - rate_matrix * (reverted + weight_decay * weight_slots)
    vec_step = step_count[slot_total].astype(f32)
    vfix_one = 1.0 - jnp.power(f32(beta_first), vec_step)
    vfix_two = 1.0 - jnp.power(f32(beta_second), vec_step)
    vec_one = beta_first * vector_first + (1.0 - beta_first) * grad_vectors
    vec_two = beta_second * vector_second + (1.0 - beta_second) * grad_vectors * grad_vectors
    vec_new = vector_params - rate_vector * adam_direction(vec_one, vec_two, vfix_one, vfix_two)
    vector_state = jnp.stack([vec_new, vec_one, vec_two])
    return (
        node_output,
        edge_output,
        node_gradient,
        edge_gradient,
        moment_one,
        moment_two,
        new_weights,
        new_weights.astype(bf16),
        vector_state,
        grad_norm.reshape(1),
    )


def solution(mesh):
    in_specs = (
        P("dp", None, "node", None),
        P("dp", None, "node", None),
        P("dp", None, "node", None),
        P("dp", None, "node", None),
        P("node", None),
        P("node"),
        P("node"),
        P("dp"),
        P(),
        P(),
        P("dp", "node", None),
        P("dp", "node", None),
        P("dp", "node", None),
        P("dp", None, "node"),
        P("dp", None, None),
        P(),
        P(),
        P(),
    )
    out_specs = (
        P("dp", None, "node", None),
        P("dp", None, "node", None),
        P("dp", None, "node", None),
        P("dp", None, "node", None),
        P("dp", "node", None),
        P("dp", "node", None),
        P("dp", "node", None),
        P("dp", "node", None),
        P(),
        P(),
    )
    return jax.shard_map(local, mesh=mesh, in_specs=in_specs, out_specs=out_specs, check_vma=False)
```

```python
import functools
import math

import jax
import jax.numpy as jnp
from jax import lax
from jax.experimental import pallas as pl
from jax.experimental.pallas import tpu as pltpu
from jax.sharding import PartitionSpec as P

NBLOCK = 7
f32 = jnp.float32
bf16 = jnp.bfloat16
highest = lax.Precision.HIGHEST
norm_epsilon = 1e-05
adam_epsilon = 1e-08
beta_first = 0.5
beta_second = 0.5
rate_matrix = 0.03
rate_vector = 0.4
weight_decay = 0.01


def dot(a, b):
    return jnp.dot(a, b, preferred_element_type=f32)


def dot_tb(a, b):
    return lax.dot_general(a, b, (((1,), (1,)), ((), ())), preferred_element_type=f32)


def dot_ta(a, b):
    return lax.dot_general(a, b, (((0,), (0,)), ((), ())), preferred_element_type=f32)


def eights(x):
    return jnp.sum(x.reshape(x.shape[0] // 8, 8, x.shape[1]), axis=0)


def sigmoid(z):
    return 0.5 * jnp.tanh(0.5 * z) + 0.5


def branch_forward(z, w_out, bias_out):
    s = sigmoid(z)
    h = z * s
    slope = s + h * (1.0 - s)
    hidden = h.astype(bf16)
    after = dot(hidden, w_out) + bias_out
    center = after - jnp.mean(after, axis=1, keepdims=True)
    spread = jnp.mean(center * center, axis=1, keepdims=True)
    inverse = lax.rsqrt(spread + norm_epsilon)
    return hidden, slope, center * inverse, inverse


def norm_backward(upstream, normed, inverse, gain):
    u = upstream * gain
    first = jnp.mean(u, axis=1, keepdims=True)
    second = jnp.mean(u * normed, axis=1, keepdims=True)
    return (inverse * (u - first - normed * second)).astype(bf16)


def layer_kernel(
    rollout_ref,
    slot_block_ref,
    node_hbm,
    edge_hbm,
    ncot_hbm,
    ecot_hbm,
    sender_ref,
    receiver_ref,
    halo_ref,
    w_ref,
    vec_ref,
    nout_ref,
    eout_hbm,
    nbase_ref,
    egrad_hbm,
    grad_ref,
    gvec_ref,
    hback_ref,
    node_v,
    edge_v,
    ncot_v,
    ecot_v,
    eout_v,
    egrad_v,
    gather_t,
    gather,
    table,
    hidden_v,
    slope_v,
    normed_v,
    inv_v,
    dz_v,
    da_v,
    summed_v,
    dsum_v,
    sc_own,
    sc_recv,
    sc_halo,
    acc,
    sem_in,
    sem_out,
):
    roll, nodes, width = node_v.shape
    edges = edge_v.shape[1]
    peers, per_peer = sc_halo.shape[0], sc_halo.shape[2]
    halo = peers * per_peer
    known = nodes + halo
    padded = table.shape[1]
    chunk = 256
    pieces = edges // chunk

    copies = []
    for i, (src, dst) in enumerate(
        ((node_hbm, node_v), (edge_hbm, edge_v), (ncot_hbm, ncot_v), (ecot_hbm, ecot_v))
    ):
        copies.append(pltpu.make_async_copy(src.at[0], dst, sem_in.at[i]))
        copies[-1].start()

    slot_of = []
    for b in range(NBLOCK):
        found = jnp.int32(0)
        for s in range(slot_block_ref.shape[0]):
            found = jnp.where(slot_block_ref[s] == b, jnp.int32(s), found)
        slot_of.append(found)

    def weight(b):
        return w_ref[slot_of[b]]

    def live(t):
        return jnp.where(t < rollout_ref[0], 1.0, 0.0).astype(f32)

    ids = lax.broadcasted_iota(jnp.int32, (padded, edges), 0)
    onehot = (ids == sender_ref[...]) | (ids == receiver_ref[...] + known)
    onehot = jnp.where(onehot, 1.0, 0.0).astype(f32)
    gather_t[...] = onehot.astype(bf16)
    gather[...] = onehot.T.astype(bf16)
    table[...] = jnp.zeros_like(table)
    acc[...] = jnp.zeros_like(acc)

    copies[0].wait()
    flat_nodes = node_v[...].reshape(roll * nodes, width)
    own_sent = dot(flat_nodes, weight(1))
    own_recv = dot(flat_nodes, weight(2))
    halo_sent = dot(halo_ref[...], weight(1)).reshape(peers, roll, per_peer, width)
    for t in range(roll):
        table[t, :nodes] = own_sent[t * nodes : (t + 1) * nodes].astype(bf16)
        table[t, nodes:known] = halo_sent[:, t].reshape(halo, width).astype(bf16)
        table[t, known : known + nodes] = own_recv[t * nodes : (t + 1) * nodes].astype(bf16)
    copies[1].wait()

    def forward(t, carry):
        lv = live(t)
        total = jnp.zeros((nodes, width), f32)
        for c in range(pieces):
            rows = pl.ds(c * chunk, chunk)
            edge = edge_v[t, rows]
            z = dot(edge, weight(0)) + dot(gather[rows], table[t]) + vec_ref[0:1]
            hidden, slope, normed, inverse = branch_forward(z, weight(3), vec_ref[1:2])
            hidden_v[t, rows] = hidden
            slope_v[t, rows] = slope.astype(bf16)
            normed_v[t, rows] = normed.astype(bf16)
            inv_v[t, rows] = inverse
            new = edge.astype(f32) + (normed * vec_ref[2:3] + vec_ref[3:4])
            eout_v[t, rows] = (new * lv).astype(bf16)
            total += dot(gather_t[known : known + nodes, rows], new.astype(bf16))
        summed_v[pl.ds(t * nodes, nodes)] = total.astype(bf16)
        pltpu.make_async_copy(eout_v.at[t], eout_hbm.at[0, t], sem_out.at[t]).start()
        return carry

    lax.fori_loop(0, roll, forward, 0)

    flat_nodes = node_v[...].reshape(roll * nodes, width)
    summed = summed_v[...]
    z = dot(flat_nodes, weight(4)) + dot(summed, weight(5)) + vec_ref[4:5]
    hidden, slope, normed, inverse = branch_forward(z, weight(6), vec_ref[5:6])
    row_t = lax.broadcasted_iota(jnp.int32, (roll * nodes, 1), 0) // nodes
    row_live = jnp.where(row_t < rollout_ref[0], 1.0, 0.0).astype(f32)
    new = flat_nodes.astype(f32) + (normed * vec_ref[6:7] + vec_ref[7:8])
    nout_ref[0] = (new * row_live).astype(bf16).reshape(roll, nodes, width)
    copies[2].wait()
    d_new = ncot_v[...].reshape(roll * nodes, width).astype(f32) * row_live
    acc[6] += eights(d_new * normed)
    acc[7] += eights(d_new)
    d_after = norm_backward(d_new, normed, inverse, vec_ref[6:7])
    acc[5] += eights(d_after.astype(f32))
    grad_ref[6] = dot_ta(hidden, d_after)
    d_before = (dot_tb(d_after, weight(6)) * slope).astype(bf16)
    acc[4] += eights(d_before.astype(f32))
    grad_ref[4] = dot_ta(flat_nodes, d_before)
    grad_ref[5] = dot_ta(summed, d_before)
    dsum_v[...] = dot_tb(d_before, weight(5)).astype(bf16)
    nbase_ref[...] = d_new + dot_tb(d_before, weight(4))
    grad_ref[0] = jnp.zeros((width, width), f32)
    grad_ref[3] = jnp.zeros((width, width), f32)
    copies[3].wait()

    def backward(t, carry):
        lv = live(t)
        for c in range(pieces):
            rows = pl.ds(c * chunk, chunk)
            d_new = ecot_v[t, rows].astype(f32) * lv + dot(
                gather[rows, known : known + nodes], dsum_v[pl.ds(t * nodes, nodes)]
            )
            normed = normed_v[t, rows].astype(f32)
            acc[2] += eights(d_new * normed)
            acc[3] += eights(d_new)
            d_after = norm_backward(d_new, normed, inv_v[t, rows], vec_ref[2:3])
            acc[1] += eights(d_after.astype(f32))
            da_v[rows] = d_after
            d_before = (dot_tb(d_after, weight(3)) * slope_v[t, rows].astype(f32)).astype(bf16)
            acc[0] += eights(d_before.astype(f32))
            dz_v[rows] = d_before
            egrad_v[t, rows] = (d_new + dot_tb(d_before, weight(0))).astype(bf16)
        pltpu.make_async_copy(egrad_v.at[t], egrad_hbm.at[0, t], sem_out.at[roll + t]).start()
        grad_ref[3] += dot_ta(hidden_v[t], da_v[...])
        grad_ref[0] += dot_ta(edge_v[t], dz_v[...])
        scattered = dot(gather_t[...], dz_v[...])
        sc_own[pl.ds(t * nodes, nodes)] = scattered[:nodes].astype(bf16)
        sc_recv[pl.ds(t * nodes, nodes)] = scattered[known : known + nodes].astype(bf16)
        sc_halo[:, t] = scattered[nodes:known].reshape(peers, per_peer, width)
        return carry

    lax.fori_loop(0, roll, backward, 0)

    halo_sum = sc_halo[...].reshape(roll * halo, width).astype(bf16)
    grad_ref[1] = dot_ta(flat_nodes, sc_own[...]) + dot_ta(halo_ref[...], halo_sum)
    grad_ref[2] = dot_ta(flat_nodes, sc_recv[...])
    hback_ref[...] = dot_tb(halo_sum, weight(1)).astype(bf16)
    nbase_ref[...] += dot_tb(sc_own[...], weight(1)) + dot_tb(sc_recv[...], weight(2))
    gvec_ref[...] = jnp.sum(acc[...], axis=1)

    for t in range(roll):
        pltpu.make_async_copy(eout_v.at[t], eout_hbm.at[0, t], sem_out.at[t]).wait()
        pltpu.make_async_copy(egrad_v.at[t], egrad_hbm.at[0, t], sem_out.at[roll + t]).wait()


def layer(
    rollout_length,
    slot_block,
    node_state,
    edge_state,
    node_cotangent,
    edge_cotangent,
    edge_sender,
    edge_receiver,
    halo,
    slots,
    vector_params,
    per_peer,
):
    _, roll, nodes, width = node_state.shape
    edges = edge_state.shape[2]
    peers = halo.shape[0] // (roll * per_peer)
    known = nodes + peers * per_peer
    padded = -(-(known + nodes) // 128) * 128
    vmem = pl.BlockSpec(memory_space=pltpu.VMEM)
    smem = pl.BlockSpec(memory_space=pltpu.SMEM)
    hbm = pl.BlockSpec(memory_space=pl.ANY)
    shape = jax.ShapeDtypeStruct
    return pl.pallas_call(
        layer_kernel,
        out_shape=(
            shape(node_state.shape, bf16),
            shape(edge_state.shape, bf16),
            shape((roll * nodes, width), f32),
            shape(edge_state.shape, bf16),
            shape((NBLOCK, width, width), f32),
            shape((8, width), f32),
            shape(halo.shape, bf16),
        ),
        in_specs=[smem, smem, hbm, hbm, hbm, hbm, vmem, vmem, vmem, vmem, vmem],
        out_specs=(vmem, hbm, vmem, hbm, vmem, vmem, vmem),
        scratch_shapes=[
            pltpu.VMEM((roll, nodes, width), bf16),
            pltpu.VMEM((roll, edges, width), bf16),
            pltpu.VMEM((roll, nodes, width), bf16),
            pltpu.VMEM((roll, edges, width), bf16),
            pltpu.VMEM((roll, edges, width), bf16),
            pltpu.VMEM((roll, edges, width), bf16),
            pltpu.VMEM((padded, edges), bf16),
            pltpu.VMEM((edges, padded), bf16),
            pltpu.VMEM((roll, padded, width), bf16),
            pltpu.VMEM((roll, edges, width), bf16),
            pltpu.VMEM((roll, edges, width), bf16),
            pltpu.VMEM((roll, edges, width), bf16),
            pltpu.VMEM((roll, edges, 1), f32),
            pltpu.VMEM((edges, width), bf16),
            pltpu.VMEM((edges, width), bf16),
            pltpu.VMEM((roll * nodes, width), bf16),
            pltpu.VMEM((roll * nodes, width), bf16),
            pltpu.VMEM((roll * nodes, width), bf16),
            pltpu.VMEM((roll * nodes, width), bf16),
            pltpu.VMEM((peers, roll, per_peer, width), f32),
            pltpu.VMEM((8, 8, width), f32),
            pltpu.SemaphoreType.DMA((4,)),
            pltpu.SemaphoreType.DMA((2 * roll,)),
        ],
        compiler_params=pltpu.CompilerParams(vmem_limit_bytes=60 << 20),
        name="layer",
    )(
        rollout_length,
        slot_block,
        node_state,
        edge_state,
        node_cotangent,
        edge_cotangent,
        edge_sender.reshape(1, edges),
        edge_receiver.reshape(1, edges),
        halo,
        slots,
        vector_params,
    )


def adam_direction(moment_one, moment_two, fix_one, fix_two):
    return moment_one / fix_one / (jnp.sqrt(moment_two / fix_two) + adam_epsilon)


MESH = pl.DeviceIdType.MESH


class Place:
    def __init__(self):
        self.z = lax.axis_index("dp")
        self.n = lax.axis_index("node")
        self.c = lax.rem(self.n, 2)
        self.x = lax.rem(self.n // 2, 2)
        self.y = self.n // 4
        self.xn = self.n + 2 - 4 * self.x
        self.yn = self.n + 4 - 8 * self.y
        self.sib = self.n + 1 - 2 * self.c
        self.diag = self.xn + 4 - 8 * self.y


def remote(src, dst, send, recv, z, n):
    return pltpu.make_async_remote_copy(
        src_ref=src, dst_ref=dst, send_sem=send, recv_sem=recv, device_id=(z, n), device_id_type=MESH
    )


def greet_start(p, depth, peers):
    barrier = pltpu.get_barrier_semaphore()
    for k in range(1, peers):
        to = lax.rem(p.n + k, peers)
        pl.semaphore_signal(barrier, inc=1, device_id=(p.z, to), device_id_type=MESH)
    for k in range(1, depth):
        to = lax.rem(p.z + k, depth)
        pl.semaphore_signal(barrier, inc=1, device_id=(to, p.n), device_id_type=MESH)


def greet_end(depth, peers):
    pl.semaphore_wait(pltpu.get_barrier_semaphore(), peers + depth - 2)


ORDER = ((0, 1, 2, 3), (1, 0, 2, 3), (2, 3, 1, 0), (3, 2, 1, 0))


def gather_start(p, buf, k, sems):
    send, recv = sems
    own = buf(k, p.n)
    copies = []
    for i, to in ((0, p.xn), (1, p.yn), (3, p.sib)):
        copies.append(remote(own, own, send.at[i, k], recv.at[i, k], p.z, to))
        copies[-1].start()
    return copies


def gather_side(p, buf, k, sems):
    send, recv = sems
    copies = []
    for i, owner in ((0, p.xn), (1, p.yn)):
        got = buf(k, owner)
        remote(got, got, send.at[i, k], recv.at[i, k], p.z, owner).wait_recv()
        on = remote(got, got, send.at[4 + i, k], recv.at[4 + i, k], p.z, p.sib)
        on.start()
        copies.append(on)
        over = remote(got, got, send.at[2, k], recv.at[2, k], p.z, p.yn if i == 0 else p.xn)
        pl.when(p.c == i)(over.start)
    copies.append(over)
    return copies


def gather_far(p, buf, k, sems):
    send, recv = sems
    got = buf(k, p.diag)
    remote(got, got, send.at[2, k], recv.at[2, k], p.z, p.xn).wait_recv()
    on = remote(got, got, send.at[6, k], recv.at[6, k], p.z, p.sib)
    on.start()
    return [on]


def gather_end(p, buf, k, sems):
    send, recv = sems
    for i in (3, 4, 5, 6):
        got = buf(k, p.sib)
        remote(got, got, send.at[i, k], recv.at[i, k], p.z, p.sib).wait_recv()


class Step:
    def __init__(self, **refs):
        self.__dict__.update(refs)


def step_kernel(names, *refs):
    k = Step(**dict(zip(names, refs, strict=True)))
    p = Place()
    depth, peers = 4, 8
    roll, nodes, width = k.node_v.shape
    edges = k.edge_v.shape[1]
    slot_dev, rows = k.weight_v.shape[:2]
    per_peer = k.halo.shape[1] // roll
    halo = peers * per_peer
    known = nodes + halo
    padded = k.table.shape[1]
    chunk = edges
    pieces = edges // chunk
    going = []

    def launch(src, dst, send, recv, z, n):
        copy = remote(src, dst, send, recv, z, n)
        copy.start()
        going.append((copy, None))

    def landed(dst, recv):
        remote(dst, dst, recv, recv, p.z, p.sib).wait_recv()

    loads = []
    for i, (src, dst) in enumerate(
        (
            (k.weight_hbm, k.weight_v),
            (k.node_hbm.at[0], k.node_v),
            (k.left_hbm, k.grad.at[2, :slot_dev]),
            (k.right_hbm, k.grad.at[:slot_dev]),
            (k.edge_hbm.at[0], k.edge_v),
            (k.ncot_hbm.at[0], k.ncot_v),
            (k.ecot_hbm.at[0], k.egrad_v.at[0]),
            (k.first_hbm, k.first_v),
            (k.second_hbm, k.second_v),
        )
    ):
        loads.append(pltpu.make_async_copy(src, dst, k.in_sem.at[i]))
        loads[-1].start()
    greet_start(p, depth, peers)

    cut = rows * 3 // 4

    def shard(j):
        top = cut if j % slot_dev == slot_dev - 1 else rows
        return lambda slot, n: k.slots.at[slot, n // 2, lax.rem(n, 2), :top]

    def rest(slot):
        return k.slots.at[slot, :, p.c, cut:]

    planes = []
    for j in range(depth):
        z_of = 0
        for z in range(depth):
            z_of = z_of + jnp.where(p.z == z, ORDER[z][j], 0)
        planes.append(z_of)

    def along_z(z_of):
        return (
            (0, (z_of <= p.z) & (p.z < depth - 1) & (p.z - z_of < depth - 2), p.z + 1),
            (1, (z_of >= p.z) & (p.z > 0) & (z_of - p.z < depth - 2), p.z - 1),
            (2, (z_of == p.z) & ((p.z == 0) | (p.z == depth - 1)), depth - 1 - p.z),
        )

    def rest_hop(s, i):
        own = k.slots.at[p.z * slot_dev + s, p.n // 2, p.c, cut:]
        to = (p.xn, p.yn, p.diag)[i]
        return remote(own, own, k.b_send.at[i, s], k.b_recv.at[i, s], p.z, to)

    def rest_start(s):
        for i in range(3):
            rest_hop(s, i).start()
            going.append((rest_hop(s, i), None))

    def rest_pass(j, s):
        slot = planes[j] * slot_dev + s
        ref = rest(slot)
        if j == 0:
            for i in range(3):
                rest_hop(s, i).wait_recv()
        else:
            remote(ref, ref, k.bz_send.at[0, slot], k.bz_recv.at[slot], p.z, p.sib).wait_recv()
        for i, test, to in along_z(planes[j]):
            if i == 2 and j:
                continue
            copy = remote(ref, ref, k.bz_send.at[i, slot], k.bz_recv.at[slot], to, p.n)
            pl.when(test)(copy.start)
            going.append((copy, test))
        copy = remote(ref, ref, k.bs_send.at[slot], k.bs_recv.at[slot], p.z, p.sib)
        copy.start()
        going.append((copy, None))

    def rest_end(slot):
        ref = rest(slot)
        remote(ref, ref, k.bs_send.at[slot], k.bs_recv.at[slot], p.z, p.sib).wait_recv()

    wsems = (k.w_send, k.w_recv)
    order = []

    def arrive(j):
        z_of = planes[j // slot_dev]
        slot = z_of * slot_dev + j % slot_dev
        order.append(slot)
        piece = shard(j)(slot, p.n)
        if j >= slot_dev:
            remote(piece, piece, k.wz_send.at[0, slot], k.wz_recv.at[slot], p.z, p.n).wait_recv()
        for i, test, to in along_z(z_of):
            if i == 2 and j >= slot_dev:
                continue
            copy = remote(piece, piece, k.wz_send.at[i, slot], k.wz_recv.at[slot], to, p.n)
            pl.when(test)(copy.start)
            going.append((copy, test))
        going.extend((copy, None) for copy in gather_start(p, shard(j), slot, wsems))

    def side(j):
        going.extend((copy, None) for copy in gather_side(p, shard(j), order[j], wsems))

    def far(j):
        going.extend((copy, None) for copy in gather_far(p, shard(j), order[j], wsems))

    loads[0].wait()
    k.slots[pl.ds(slot_dev * p.z, slot_dev), p.n // 2, p.c] = k.weight_v[...].astype(bf16)
    greet_end(depth, peers)

    def rounds(*names):
        for name in names:
            i = int(name[1:])
            if name[0] == "b":
                rest_pass(i // slot_dev, i % slot_dev)
            else:
                {"a": arrive, "s": side, "f": far}[name[0]](i)

    rest_start(slot_dev - 1)
    rounds("a0", "a1")
    loads[1].wait()
    node_ids = lax.broadcasted_iota(jnp.int32, (nodes, halo), 0)
    pick_t = jnp.where(node_ids == k.rows_ref[...], 1.0, 0.0).astype(bf16)
    for t in range(roll):
        k.spread[:, t] = dot_ta(pick_t, k.node_v[t]).reshape(peers, per_peer, width)
    k.hput[...] = k.spread[...].reshape(peers, roll * per_peer, width).astype(bf16)
    k.halo[p.n] = k.hput[p.n]
    rounds("a2", "a3", "s0", "s1")
    loads[2].wait()
    for s in range(slot_dev):
        k.pre[2 * slot_dev + s, p.n] = k.grad[2, s].astype(bf16)
        for m in range(peers):
            k.lput[s, m] = k.grad[2, s, :, m * rows : (m + 1) * rows].astype(bf16)
    k.lgot[:, p.n] = k.lput[:, p.n]
    rounds("a4", "a5", "s2", "s3", "b1", "f0", "f1")
    ids = lax.broadcasted_iota(jnp.int32, (padded, edges), 0)
    onehot = (ids == k.sender_ref[...].reshape(1, edges)) | (
        ids == k.receiver_ref[...].reshape(1, edges) + known
    )
    onehot = jnp.where(onehot, 1.0, 0.0).astype(f32)
    k.gather_t[...] = onehot.astype(bf16)
    rounds("a6", "a7", "s4", "s5", "b3", "f2", "f3")
    k.gather[...] = onehot.T.astype(bf16)
    k.table[:, known + nodes :] = jnp.zeros((roll, padded - known - nodes, width), bf16)
    k.acc[...] = jnp.zeros_like(k.acc)
    rounds("s6", "s7")
    hsent = []
    for i in range(1, peers):
        to = lax.rem(p.n + i, peers)
        hsent.append(remote(k.hput.at[to], k.halo.at[p.n], k.h_send.at[0, i], k.h_recv.at[0, i], p.z, to))
        hsent[-1].start()
    rounds("b5", "f4", "f5", "b7")
    loads[3].wait()
    for s in range(slot_dev):
        k.right_b[s] = k.grad[s].reshape(width, width).astype(bf16)
    rounds("f6", "f7")
    for j, slot in enumerate(order):
        gather_end(p, shard(j), slot, wsems)
        if j % slot_dev == slot_dev - 1:
            rest_end(slot)

    slot_of = []
    for b in range(NBLOCK):
        found = 0
        for s in range(depth * slot_dev):
            found = jnp.where(k.slot_block_ref[s] == b, s, found)
        slot_of.append(found)

    def weight(b):
        return k.slots[slot_of[b]].reshape(width, width)

    rollout = k.rollout_ref[0]
    vec = k.vec_ref

    def live(t):
        return jnp.where(t < rollout, 1.0, 0.0).astype(f32)

    def flat_nodes():
        return k.node_v[...].reshape(roll * nodes, width)

    own_sent = dot(flat_nodes(), weight(1))
    own_recv = dot(flat_nodes(), weight(2))
    for copy in hsent:
        copy.wait_send()
    for i in range(1, peers):
        landed(k.halo.at[0], k.h_recv.at[0, i])
    halo_flat = k.halo[...].reshape(roll * halo, width)
    halo_sent = dot(halo_flat, weight(1)).reshape(peers, roll, per_peer, width)
    for t in range(roll):
        k.table[t, :nodes] = own_sent[t * nodes : (t + 1) * nodes].astype(bf16)
        k.table[t, nodes:known] = halo_sent[:, t].reshape(halo, width).astype(bf16)
        k.table[t, known : known + nodes] = own_recv[t * nodes : (t + 1) * nodes].astype(bf16)
    loads[4].wait()

    for i in range(1, peers):
        to = lax.rem(p.n + i, peers)
        launch(k.lput.at[:, to], k.lgot.at[:, p.n], k.l_send.at[i], k.l_recv.at[i], p.z, to)
    loads[7].wait()
    loads[8].wait()
    psems = (k.p_send, k.p_recv)
    early = range(3 * slot_dev)
    pbuf = lambda i, n: k.pre.at[i, n]
    for s in range(slot_dev):
        k.pre[s, p.n] = k.first_v[s].astype(bf16)
        k.pre[slot_dev + s, p.n] = k.second_v[s].astype(bf16)
    for i in early:
        going.extend((copy, None) for copy in gather_start(p, pbuf, i, psems))

    def forward(t, carry):
        lv = live(t)
        total = jnp.zeros((nodes, width), f32)
        for c in range(pieces):
            at = pl.ds(c * chunk, chunk)
            edge = k.edge_v[t, at]
            z = dot(edge, weight(0)) + dot(k.gather[at], k.table[t]) + vec[0:1]
            hidden, slope, normed, inverse = branch_forward(z, weight(3), vec[1:2])
            k.hidden_v[t, at] = hidden
            k.slope_v[t, at] = slope.astype(bf16)
            k.normed_v[t, at] = normed.astype(bf16)
            k.inv_v[t, at] = inverse
            new = edge.astype(f32) + (normed * vec[2:3] + vec[3:4])
            k.eout_v[0, t, at] = (new * lv).astype(bf16)
            total += dot(k.gather_t[known : known + nodes, at], new.astype(bf16))
        k.summed_v[pl.ds(t * nodes, nodes)] = total.astype(bf16)
        return carry

    lax.fori_loop(0, roll, forward, 0)

    on_f = jnp.where(p.c == 0, p.x, p.y)
    on_g = jnp.where(p.c == 0, p.y, p.x)
    to_f = jnp.where(p.c == 0, p.xn, p.yn)
    to_g = jnp.where(p.c == 0, p.yn, p.xn)

    def spot(f, g):
        return jnp.where(p.c == 0, g * 2 + f, f * 2 + g)

    def hop(stage, b):
        put, got, to = (
            (k.cast, k.got_core, p.sib),
            (k.put_one, k.got_one, to_f),
            (k.put_two, k.got_two, to_g),
        )[stage]
        at = stage * NBLOCK + b
        return remote(put.at[b], got.at[b], k.r_send.at[at], k.r_recv.at[at], p.z, to)

    def to_core(b):
        for i in range(peers // 2):
            k.cast[b, i] = k.grad[b, 2 * i + 1 - p.c].astype(bf16)
        hop(0, b).start()

    def to_first(b):
        hop(0, b).wait_recv()
        for g in range(2):
            at = spot(1 - on_f, g)
            k.put_one[b, g] = (k.grad[b, 2 * at + p.c] + k.got_core[b, at].astype(f32)).astype(bf16)
        hop(1, b).start()
        for g in range(2):
            at = spot(on_f, g)
            k.grad[b, 2 * at + p.c] = k.grad[b, 2 * at + p.c] + k.got_core[b, at].astype(f32)

    def to_second(b):
        hop(1, b).wait_recv()
        at = spot(on_f, 1 - on_g)
        total = k.grad[b, 2 * at + p.c] + k.got_one[b, 1 - on_g].astype(f32)
        k.put_two[b] = total.astype(bf16)
        hop(2, b).start()
        k.grad[b, p.n] = k.grad[b, p.n] + k.got_one[b, on_g].astype(f32)

    def settle(b):
        hop(2, b).wait_recv()
        k.grad[b, p.n] = k.grad[b, p.n] + k.got_two[b].astype(f32)

    def put_grad(b, value):
        k.grad[b] = value.reshape(peers, rows, width)

    summed = k.summed_v[...]
    z = dot(flat_nodes(), weight(4)) + dot(summed, weight(5)) + vec[4:5]
    hidden, slope, normed, inverse = branch_forward(z, weight(6), vec[5:6])
    row_t = lax.broadcasted_iota(jnp.int32, (roll * nodes, 1), 0) // nodes
    row_live = jnp.where(row_t < rollout, 1.0, 0.0).astype(f32)
    new = flat_nodes().astype(f32) + (normed * vec[6:7] + vec[7:8])
    k.nout_v[0] = (new * row_live).astype(bf16).reshape(roll, nodes, width)
    loads[5].wait()
    d_new = k.ncot_v[...].reshape(roll * nodes, width).astype(f32) * row_live
    k.acc[6] = eights(d_new * normed)
    k.acc[7] = eights(d_new)
    d_after = norm_backward(d_new, normed, inverse, vec[6:7])
    k.acc[5] = eights(d_after.astype(f32))
    put_grad(6, dot_ta(hidden, d_after))
    to_core(6)
    d_before = (dot_tb(d_after, weight(6)) * slope).astype(bf16)
    k.acc[4] = eights(d_before.astype(f32))
    put_grad(4, dot_ta(flat_nodes(), d_before))
    to_core(4)
    put_grad(5, dot_ta(summed, d_before))
    to_core(5)
    k.summed_v[...] = dot_tb(d_before, weight(5)).astype(bf16)
    k.table[:, 2 * nodes : 3 * nodes] = d_before.reshape(roll, nodes, width)
    for i in early:
        going.extend((copy, None) for copy in gather_side(p, pbuf, i, psems))
    k.grad[0] = jnp.zeros((peers, rows, width), f32)
    k.grad[3] = jnp.zeros((peers, rows, width), f32)
    loads[6].wait()

    def backward(t, carry):
        lv = live(t)
        for c in range(pieces):
            at = pl.ds(c * chunk, chunk)
            d_new = k.egrad_v[0, t, at].astype(f32) * lv + dot(
                k.gather[at, known : known + nodes], k.summed_v[pl.ds(t * nodes, nodes)]
            )
            k.egrad_v[0, t, at] = d_new.astype(bf16)
            normed = k.normed_v[t, at].astype(f32)
            k.acc[2] += eights(d_new * normed)
            k.acc[3] += eights(d_new)
            d_after = norm_backward(d_new, normed, k.inv_v[t, at], vec[2:3])
            k.acc[1] += eights(d_after.astype(f32))
            k.normed_v[t, at] = d_after
            d_before = (dot_tb(d_after, weight(3)) * k.slope_v[t, at].astype(f32)).astype(bf16)
            k.acc[0] += eights(d_before.astype(f32))
            k.slope_v[t, at] = d_before
        k.grad[3] += dot_ta(k.hidden_v[t], k.normed_v[t]).reshape(peers, rows, width)
        k.grad[0] += dot_ta(k.edge_v[t], k.slope_v[t]).reshape(peers, rows, width)
        scattered = dot(k.gather_t[...], k.slope_v[t])
        k.table[t, :nodes] = scattered[:nodes].astype(bf16)
        k.table[t, nodes : 2 * nodes] = scattered[known : known + nodes].astype(bf16)
        k.spread[:, t] = scattered[nodes:known].reshape(peers, per_peer, width)
        for step, work in enumerate((to_first, to_second, settle)):

            @pl.when(t == step)
            def _():
                def one(b, carry):
                    work(b)
                    return carry

                lax.fori_loop(4, NBLOCK, one, 0)

        return carry

    lax.fori_loop(0, roll, backward, 0)

    def kept(i):
        return k.table[:, i * nodes : (i + 1) * nodes].reshape(roll * nodes, width)

    def edge_gradient(t):
        for c in range(pieces):
            at = pl.ds(c * chunk, chunk)
            grown = k.egrad_v[0, t, at].astype(f32) + dot_tb(k.slope_v[t, at], weight(0))
            k.egrad_v[0, t, at] = grown.astype(bf16)

    to_core(3)
    to_core(0)
    k.hput[...] = k.spread[...].reshape(peers, roll * per_peer, width).astype(bf16)
    put_grad(1, dot_ta(flat_nodes(), kept(0)) + dot_ta(halo_flat, k.hput[...].reshape(roll * halo, width)))
    to_core(1)
    to_first(3)
    put_grad(2, dot_ta(flat_nodes(), kept(1)))
    to_core(2)
    to_first(0)
    k.vput[0] = jnp.sum(k.acc[...], axis=1)
    launch(k.vput.at[0], k.vgot.at[0], k.v_send.at[0], k.v_recv.at[0], p.z, p.sib)
    to_first(1)
    to_second(3)
    to_first(2)
    landed(k.vgot.at[0], k.v_recv.at[0])
    k.vput[1] = k.vput[0] + k.vgot[0]
    launch(k.vput.at[1], k.vgot.at[1], k.v_send.at[1], k.v_recv.at[1], p.z, p.xn)
    to_second(0)
    for i in early:
        going.extend((copy, None) for copy in gather_far(p, pbuf, i, psems))
    to_second(1)
    settle(3)
    to_second(2)
    settle(0)
    landed(k.vgot.at[1], k.v_recv.at[1])
    k.vput[2] = k.vput[1] + k.vgot[1]
    launch(k.vput.at[2], k.vgot.at[2], k.v_send.at[2], k.v_recv.at[2], p.z, p.yn)
    for i in range(1, peers):
        to = lax.rem(p.n + i, peers)
        launch(k.hput.at[to], k.hret.at[p.n], k.h_send.at[1, i], k.h_recv.at[1, i], p.z, to)
    k.hret[p.n] = k.hput[p.n]
    settle(1)
    settle(2)

    def part(target, s):
        b = k.slot_block_ref[target * slot_dev + s]
        held = k.grad[jnp.minimum(b, NBLOCK - 1), p.n]
        return jnp.where(b < NBLOCK, held, 0.0)

    last = depth - 1

    def z_hop(way, target, s, to):
        put, got = (k.put_up, k.got_up) if way == 0 else (k.put_down, k.got_down)
        return remote(
            put.at[target, s], got.at[target, s], k.z_send.at[way, target, s], k.z_recv.at[way, target, s], to, p.n
        )

    def far_hop(s):
        return remote(k.put_far.at[s], k.got_far.at[s], k.f_send.at[s], k.f_recv.at[s], last - p.z, p.n)

    def pass_on(way):
        put, got = (k.put_up, k.got_up) if way == 0 else (k.put_down, k.got_down)
        to = p.z + 1 if way == 0 else p.z - 1
        for step in (last, last - 1, 1):
            target = step if way == 0 else last - step
            test = p.z < target if way == 0 else p.z > target
            if step == last:
                end = last if way == 0 else 0
                test = test & (p.z != last - end)
                source = (p.z != last - end) & (p.z != (1 if way == 0 else last - 1))
            else:
                source = p.z > 0 if way == 0 else p.z < last

            @pl.when(test)
            def _():
                for s in range(slot_dev):

                    @pl.when(source)
                    def _():
                        z_hop(way, target, s, to).wait_recv()
                        total = part(target, s) + got[target, s].astype(f32)
                        put[target, s] = total.astype(bf16)

                    @pl.when(jnp.logical_not(source))
                    def _():
                        put[target, s] = part(target, s).astype(bf16)

                    z_hop(way, target, s, to).start()

            if step == last - 1:

                @pl.when(p.z == (0 if way == 0 else last))
                def _():
                    for s in range(slot_dev):
                        k.put_far[s] = part(last - p.z, s).astype(bf16)
                        far_hop(s).start()

    @pl.when(p.z == 0)
    def _():
        pass_on(0)

    @pl.when(p.z == depth - 1)
    def _():
        pass_on(1)

    edge_gradient(0)

    @pl.when(p.z == 1)
    def _():
        pass_on(0)

    @pl.when(p.z == depth - 2)
    def _():
        pass_on(1)

    edge_gradient(1)

    @pl.when(p.z == 1)
    def _():
        pass_on(1)

    @pl.when(p.z == depth - 2)
    def _():
        pass_on(0)

    landed(k.vgot.at[2], k.v_recv.at[2])
    k.vput[3] = k.vput[2] + k.vgot[2]
    k.vz[p.z] = k.vput[3]
    for i in range(1, depth):
        to = lax.rem(p.z + i, depth)
        launch(k.vput.at[3], k.vz.at[p.z], k.v_send.at[2 + i], k.v_recv.at[2 + i], to, p.n)
    edge_gradient(2)
    square = jnp.zeros((8, width), f32)
    gsems = (k.g_send, k.g_recv)
    gbuf = lambda s, n: k.full.at[s, n]
    for s in range(slot_dev):

        @pl.when(p.z > 0)
        def _():
            landed(k.got_up.at[p.z, s], k.z_recv.at[0, p.z, s])

        @pl.when(p.z < depth - 1)
        def _():
            landed(k.got_down.at[p.z, s], k.z_recv.at[1, p.z, s])

        mine = part(p.z, s) + jnp.where(p.z > 0, k.got_up[p.z, s].astype(f32), 0.0)
        mine = mine + jnp.where(p.z < depth - 1, k.got_down[p.z, s].astype(f32), 0.0)

        @pl.when((p.z == 0) | (p.z == last))
        def _():
            far_hop(s).wait_recv()

        mine = mine + jnp.where((p.z == 0) | (p.z == last), k.got_far[s].astype(f32), 0.0)
        k.full[s, p.n] = mine.astype(bf16)
        for copy in gather_start(p, gbuf, s, gsems):
            going.append((copy, None))
        square = square + eights(mine * mine)
    square = square[:, :128] + square[:, 128:256] + square[:, 256:384] + square[:, 384:]
    k.sput[...] = square
    k.sgot[p.n] = square
    for i in range(1, peers):
        to = lax.rem(p.n + i, peers)
        launch(k.sput, k.sgot.at[p.n], k.n_send.at[i], k.n_recv.at[i], p.z, to)
    edge_gradient(3)

    def collect(buffer, sems, between, finish):
        for s in range(slot_dev):
            going.extend((copy, None) for copy in gather_side(p, buffer, s, sems))
        between()
        for s in range(slot_dev):
            going.extend((copy, None) for copy in gather_far(p, buffer, s, sems))
        for s in range(slot_dev):
            gather_end(p, buffer, s, sems)
            finish(s)

    for i in range(1, peers):
        landed(k.sgot.at[0], k.n_recv.at[i])
    k.szput[...] = jnp.sum(k.sgot[...], axis=0)
    k.sz[p.z] = k.szput[...]
    for i in range(1, depth):
        to = lax.rem(p.z + i, depth)
        launch(k.szput, k.sz.at[p.z], k.n_send.at[peers - 1 + i], k.n_recv.at[peers - 1 + i], to, p.n)

    limit = math.sqrt(NBLOCK * width * width + 8 * width)
    found = []

    def fix(beta, step):
        return 1.0 - jnp.exp2(math.log2(beta) * jnp.full((1, 1), step, jnp.int32).astype(f32))

    def norm():
        for i in range(1, depth):
            landed(k.vz.at[0], k.v_recv.at[2 + i])
            landed(k.sz.at[0], k.n_recv.at[peers - 1 + i])
        vectors = k.vz[0] + k.vz[1] + k.vz[2] + k.vz[3]
        square_sum = jnp.sum(k.sz[0] + k.sz[1] + k.sz[2] + k.sz[3], keepdims=True).reshape(1, 1)
        square_sum = square_sum + jnp.sum(vectors * vectors, keepdims=True).reshape(1, 1)
        value = jnp.sqrt(square_sum)
        k.norm_v[...] = jnp.broadcast_to(value, k.norm_v.shape)
        found.extend((vectors, jnp.minimum(1.0, limit / value)))

    def advance(s):
        part_left = dot(k.pre[2 * slot_dev + s].reshape(width, width), k.full[s].reshape(width, width))
        rotated = dot(part_left.astype(bf16), k.right_b[s])
        if s == 0:
            norm()
        k.grad[s] = rotated.reshape(peers, rows, width)
        step = k.step_ref[p.z * slot_dev + s]
        fix_one, fix_two = fix(beta_first, step), fix(beta_second, step)
        clip = found[1]

        def moments(first, second, turn):
            spun = turn * clip
            return (
                beta_first * first + (1.0 - beta_first) * spun,
                beta_second * second + (1.0 - beta_second) * spun * spun,
            )

        one, two = moments(
            k.pre[s].reshape(width, width).astype(f32),
            k.pre[slot_dev + s].reshape(width, width).astype(f32),
            rotated,
        )
        direction = adam_direction(one, two, fix_one, fix_two).astype(bf16)
        turned = dot_tb(direction, k.right_b[s]).astype(bf16)
        reverted = dot_ta(k.lgot[s].reshape(width, rows), turned)
        new = k.weight_v[s] - rate_matrix * (reverted + weight_decay * k.weight_v[s])
        k.wnew_v[s] = new
        k.wcopy_v[s] = new.astype(bf16)
        one, two = moments(k.first_v[s], k.second_v[s], k.grad[s, p.n])
        k.first_v[s] = one
        k.second_v[s] = two

    for i in range(1, peers):
        landed(k.lgot.at[:, 0], k.l_recv.at[i])
    for i in early:
        gather_end(p, pbuf, i, psems)
    def node_gradient():
        for i in range(1, peers):
            landed(k.hret.at[0], k.h_recv.at[1, i])
        back = k.hret[...].astype(f32).reshape(peers, roll, per_peer, width)
        for t in range(roll):
            rows_t = back[:, t].reshape(halo, width).astype(bf16)
            k.table[t, :nodes] = (k.table[t, :nodes].astype(f32) + dot(pick_t, rows_t)).astype(bf16)
        grown = k.ncot_v[...].reshape(roll * nodes, width).astype(f32) * row_live
        grown = grown + dot_tb(kept(0), weight(1)) + dot_tb(kept(1), weight(2)) + dot_tb(kept(2), weight(4))
        k.ngrad_v[0] = grown.astype(bf16).reshape(roll, nodes, width)

    collect(gbuf, gsems, node_gradient, advance)
    grad_vectors, clip = found
    step = k.step_ref[depth * slot_dev]
    spun = grad_vectors * clip
    one = beta_first * k.vfirst_ref[...] + (1.0 - beta_first) * spun
    two = beta_second * k.vsecond_ref[...] + (1.0 - beta_second) * spun * spun
    k.vstate_v[0] = vec[...] - rate_vector * adam_direction(
        one, two, fix(beta_first, step), fix(beta_second, step)
    )
    k.vstate_v[1] = one
    k.vstate_v[2] = two

    for copy, test in going:
        if test is None:
            copy.wait_send()
        else:
            pl.when(test)(copy.wait_send)
    for b in range(NBLOCK):
        for stage in range(3):
            hop(stage, b).wait_send()
    for way in range(2):
        for step in (last, last - 1, 1):
            target = step if way == 0 else last - step
            test = p.z < target if way == 0 else p.z > target
            if step == last:
                test = test & (p.z != last - target)
            for s in range(slot_dev):
                pl.when(test)(z_hop(way, target, s, lax.rem(p.z + 1, depth)).wait_send)
    for s in range(slot_dev):
        pl.when((p.z == 0) | (p.z == last))(far_hop(s).wait_send)


def store_kernel(*refs):
    count = (len(refs) - 3) // 2
    norm, norm_out, sem = refs[count], refs[-2], refs[-1]
    copies = []
    for i in range(count):
        copies.append(pltpu.make_async_copy(refs[i], refs[count + 1 + i], sem.at[i]))
        copies[-1].start()
    norm_out[0] = norm[0, 0]
    for copy in copies:
        copy.wait()


def whole_step(
    node_state,
    edge_state,
    node_cotangent,
    edge_cotangent,
    send_rows,
    edge_sender,
    edge_receiver,
    rollout_length,
    slot_block,
    step_count,
    weight_slots,
    moment_first,
    moment_second,
    basis_left,
    basis_right,
    vector_params,
    vector_first,
    vector_second,
):
    depth, peers = 4, 8
    _, roll, nodes, width = node_state.shape
    edges = edge_state.shape[2]
    slot_dev, rows = weight_slots.shape[:2]
    halo = send_rows.shape[1]
    per_peer = halo // peers
    padded = -(-(2 * nodes + halo) // 128) * 128
    own = (slot_dev, rows, width)
    tile = (8, 128)
    hbm = pl.BlockSpec(memory_space=pl.ANY)
    vmem = pl.BlockSpec(memory_space=pltpu.VMEM)
    smem = pl.BlockSpec(memory_space=pltpu.SMEM)
    shape = jax.ShapeDtypeStruct
    dma = pltpu.SemaphoreType.DMA
    ins = dict(
        rollout_ref=(rollout_length, smem),
        slot_block_ref=(slot_block, smem),
        step_ref=(step_count, smem),
        node_hbm=(node_state, hbm),
        edge_hbm=(edge_state, hbm),
        ncot_hbm=(node_cotangent, hbm),
        ecot_hbm=(edge_cotangent, hbm),
        rows_ref=(send_rows, vmem),
        sender_ref=(edge_sender, vmem),
        receiver_ref=(edge_receiver, vmem),
        weight_hbm=(weight_slots, hbm),
        first_hbm=(moment_first, hbm),
        second_hbm=(moment_second, hbm),
        left_hbm=(jnp.swapaxes(basis_left, 1, 2), hbm),
        right_hbm=(basis_right.reshape(slot_dev, peers, rows, width), hbm),
        vec_ref=(vector_params, vmem),
        vfirst_ref=(vector_first, vmem),
        vsecond_ref=(vector_second, vmem),
    )
    outs = dict(
        nout_v=shape(node_state.shape, bf16),
        eout_v=shape(edge_state.shape, bf16),
        ngrad_v=shape(node_state.shape, bf16),
        egrad_v=shape(edge_state.shape, bf16),
        first_v=shape(own, f32),
        second_v=shape(own, f32),
        wnew_v=shape(own, f32),
        wcopy_v=shape(own, bf16),
        vstate_v=shape((3, 8, width), f32),
        norm_v=shape(tile, f32),
    )
    v = pltpu.VMEM
    scratch = dict(
        weight_v=v(own, f32),
        node_v=v((roll, nodes, width), bf16),
        edge_v=v((roll, edges, width), bf16),
        ncot_v=v((roll, nodes, width), bf16),
        slots=v((slot_dev * depth, peers // 2, 2, rows, width), bf16),
        halo=v((peers, roll * per_peer, width), bf16),
        spread=v((peers, roll, per_peer, width), f32),
        hput=v((peers, roll * per_peer, width), bf16),
        hret=v((peers, roll * per_peer, width), bf16),
        pre=v((3 * slot_dev, peers, rows, width), bf16),
        lput=v((slot_dev, peers, rows, rows), bf16),
        lgot=v((slot_dev, peers, rows, rows), bf16),
        right_b=v((slot_dev, width, width), bf16),
        gather_t=v((padded, edges), bf16),
        gather=v((edges, padded), bf16),
        table=v((roll, padded, width), bf16),
        hidden_v=v((roll, edges, width), bf16),
        slope_v=v((roll, edges, width), bf16),
        normed_v=v((roll, edges, width), bf16),
        inv_v=v((roll, edges, 1), f32),
        summed_v=v((roll * nodes, width), bf16),
        acc=v((8, 8, width), f32),
        grad=v((NBLOCK, peers, rows, width), f32),
        cast=v((NBLOCK, peers // 2, rows, width), bf16),
        got_core=v((NBLOCK, peers // 2, rows, width), bf16),
        put_one=v((NBLOCK, 2, rows, width), bf16),
        got_one=v((NBLOCK, 2, rows, width), bf16),
        put_two=v((NBLOCK, rows, width), bf16),
        got_two=v((NBLOCK, rows, width), bf16),
        put_up=v((depth, *own), bf16),
        put_down=v((depth, *own), bf16),
        got_up=v((depth, *own), bf16),
        got_down=v((depth, *own), bf16),
        put_far=v(own, bf16),
        got_far=v(own, bf16),
        full=v((slot_dev, peers, rows, width), bf16),
        vput=v((4, 8, width), f32),
        vgot=v((3, 8, width), f32),
        vz=v((depth, 8, width), f32),
        sput=v(tile, f32),
        sgot=v((peers, *tile), f32),
        szput=v(tile, f32),
        sz=v((depth, *tile), f32),
        in_sem=dma((9,)),
        w_send=dma((7, depth * slot_dev)),
        w_recv=dma((7, depth * slot_dev)),
        wz_send=dma((3, depth * slot_dev)),
        wz_recv=dma((depth * slot_dev,)),
        b_send=dma((3, slot_dev)),
        b_recv=dma((3, slot_dev)),
        bz_send=dma((3, depth * slot_dev)),
        bz_recv=dma((depth * slot_dev,)),
        bs_send=dma((depth * slot_dev,)),
        bs_recv=dma((depth * slot_dev,)),
        h_send=dma((2, peers)),
        h_recv=dma((2, peers)),
        l_send=dma((peers,)),
        l_recv=dma((peers,)),
        r_send=dma((3 * NBLOCK,)),
        r_recv=dma((3 * NBLOCK,)),
        z_send=dma((2, depth, slot_dev)),
        z_recv=dma((2, depth, slot_dev)),
        f_send=dma((slot_dev,)),
        f_recv=dma((slot_dev,)),
        g_send=dma((7, slot_dev)),
        g_recv=dma((7, slot_dev)),
        p_send=dma((7, 3 * slot_dev)),
        p_recv=dma((7, 3 * slot_dev)),
        v_send=dma((6,)),
        v_recv=dma((6,)),
        n_send=dma((peers + depth - 1,)),
        n_recv=dma((peers + depth - 1,)),
    )
    names = (*ins, *outs, *scratch)
    results = pl.pallas_call(
        functools.partial(step_kernel, names),
        out_shape=tuple(pltpu.VMEM(out.shape, out.dtype) for out in outs.values()),
        in_specs=[spec for _, spec in ins.values()],
        out_specs=(vmem,) * len(outs),
        scratch_shapes=list(scratch.values()),
        compiler_params=pltpu.CompilerParams(
            vmem_limit_bytes=52 << 20, collective_id=0, has_side_effects=True
        ),
        name="step",
    )(
        *(
            pltpu.with_memory_space_constraint(value, pltpu.HBM) if spec is hbm else value
            for value, spec in ins.values()
        )
    )
    final = [*outs.values()][:-1]
    return pl.pallas_call(
        store_kernel,
        out_shape=(*final, shape((1,), f32)),
        in_specs=[vmem] * len(outs),
        out_specs=(*([hbm] * len(final)), smem),
        scratch_shapes=[dma((len(final),))],
        compiler_params=pltpu.CompilerParams(vmem_limit_bytes=40 << 20),
        name="results",
    )(*results)


def local(
    node_state,
    edge_state,
    node_cotangent,
    edge_cotangent,
    send_rows,
    edge_sender,
    edge_receiver,
    rollout_length,
    slot_block,
    step_count,
    weight_slots,
    moment_first,
    moment_second,
    basis_left,
    basis_right,
    vector_params,
    vector_first,
    vector_second,
):
    width = node_state.shape[-1]
    roll, nodes = node_state.shape[1:3]
    clip_limit = math.sqrt(NBLOCK * width * width + 8 * width)
    slot_dev = weight_slots.shape[0]
    slot_total = slot_block.shape[0]
    halo_rows = send_rows.shape[1]
    peers = lax.axis_size("node")
    per_peer = halo_rows // peers
    if (lax.axis_size("dp"), peers) == (4, 8):
        return whole_step(
            node_state,
            edge_state,
            node_cotangent,
            edge_cotangent,
            send_rows,
            edge_sender,
            edge_receiver,
            rollout_length,
            slot_block,
            step_count,
            weight_slots,
            moment_first,
            moment_second,
            basis_left,
            basis_right,
            vector_params,
            vector_first,
            vector_second,
        )
    copies = lax.all_gather(weight_slots.astype(bf16), "node", axis=1, tiled=True)
    slots = lax.all_gather(copies, "dp", axis=0, tiled=True)
    back_onehot = (send_rows[0][:, None] == jnp.arange(nodes, dtype=jnp.int32)[None, :]).astype(bf16)
    outgoing = jnp.einsum("hk,tkd->htd", back_onehot, node_state[0], preferred_element_type=f32)
    outgoing = outgoing.astype(bf16).reshape(peers, per_peer, roll, width).transpose(0, 2, 1, 3)
    outgoing = outgoing.reshape(peers * roll * per_peer, width)
    halo = lax.all_to_all(outgoing, "node", split_axis=0, concat_axis=0, tiled=True)

    node_output, edge_output, node_base, edge_gradient, grads, grad_vectors, halo_back = layer(
        rollout_length,
        slot_block,
        node_state,
        edge_state,
        node_cotangent,
        edge_cotangent,
        edge_sender,
        edge_receiver,
        halo,
        slots,
        vector_params,
        per_peer,
    )
    returned = lax.all_to_all(halo_back, "node", split_axis=0, concat_axis=0, tiled=True)
    returned = returned.reshape(peers, roll, per_peer, width).transpose(0, 2, 1, 3)
    d_back = jnp.einsum(
        "hk,htd->tkd",
        back_onehot,
        returned.reshape(halo_rows, roll, width),
        preferred_element_type=f32,
    )
    node_gradient = node_base.reshape(roll, nodes, width) + d_back
    node_gradient = node_gradient.astype(bf16).reshape(node_state.shape)

    block_of_slot = slot_block[None, :] == jnp.arange(NBLOCK, dtype=jnp.int32)[:, None]
    first = lax.axis_index("dp") * slot_dev
    summed, grad_vectors = lax.psum((grads, grad_vectors), ("dp", "node"))
    own_square = jnp.sum(summed * summed)
    mine = lax.dynamic_slice_in_dim(block_of_slot.astype(f32), first, slot_dev, 1)
    owned_grads = jnp.einsum("bs,bij->sij", mine, summed, precision=highest)
    square_sum = own_square + jnp.sum(grad_vectors * grad_vectors)
    grad_norm = jnp.sqrt(square_sum)
    clip_scale = jnp.minimum(1.0, clip_limit / grad_norm)
    owned_grads = owned_grads * clip_scale
    grad_vectors = grad_vectors * clip_scale
    own_steps = lax.dynamic_slice_in_dim(step_count, first, slot_dev, 0)
    slot_steps = own_steps.astype(f32)[:, None, None]
    fix_one = 1.0 - jnp.power(f32(beta_first), slot_steps)
    fix_two = 1.0 - jnp.power(f32(beta_second), slot_steps)
    rotated = jnp.einsum("sij,sik->sjk", basis_left, owned_grads, precision=highest, preferred_element_type=f32)
    rotated = jnp.einsum("sjk,skl->sjl", rotated, basis_right, precision=highest, preferred_element_type=f32)
    moment_one = beta_first * moment_first + (1.0 - beta_first) * rotated
    moment_two = beta_second * moment_second + (1.0 - beta_second) * rotated * rotated
    direction = adam_direction(moment_one, moment_two, fix_one, fix_two)
    turned = jnp.einsum("sjl,sml->sjm", direction, basis_right, precision=highest, preferred_element_type=f32)
    reverted = jnp.einsum("sij,sjm->ism", basis_left, turned, precision=highest, preferred_element_type=f32)
    reverted = lax.psum_scatter(reverted.astype(bf16), "node", scatter_dimension=0, tiled=True).astype(f32)
    reverted = jnp.transpose(reverted, (1, 0, 2))
    new_weights = weight_slots - rate_matrix * (reverted + weight_decay * weight_slots)
    vec_step = step_count[slot_total].astype(f32)
    vfix_one = 1.0 - jnp.power(f32(beta_first), vec_step)
    vfix_two = 1.0 - jnp.power(f32(beta_second), vec_step)
    vec_one = beta_first * vector_first + (1.0 - beta_first) * grad_vectors
    vec_two = beta_second * vector_second + (1.0 - beta_second) * grad_vectors * grad_vectors
    vec_new = vector_params - rate_vector * adam_direction(vec_one, vec_two, vfix_one, vfix_two)
    vector_state = jnp.stack([vec_new, vec_one, vec_two])
    return (
        node_output,
        edge_output,
        node_gradient,
        edge_gradient,
        moment_one,
        moment_two,
        new_weights,
        new_weights.astype(bf16),
        vector_state,
        grad_norm.reshape(1),
    )


def solution(mesh):
    in_specs = (
        P("dp", None, "node", None),
        P("dp", None, "node", None),
        P("dp", None, "node", None),
        P("dp", None, "node", None),
        P("node", None),
        P("node"),
        P("node"),
        P("dp"),
        P(),
        P(),
        P("dp", "node", None),
        P("dp", "node", None),
        P("dp", "node", None),
        P("dp", None, "node"),
        P("dp", None, None),
        P(),
        P(),
        P(),
    )
    out_specs = (
        P("dp", None, "node", None),
        P("dp", None, "node", None),
        P("dp", None, "node", None),
        P("dp", None, "node", None),
        P("dp", "node", None),
        P("dp", "node", None),
        P("dp", "node", None),
        P("dp", "node", None),
        P(),
        P(),
    )
    return jax.shard_map(local, mesh=mesh, in_specs=in_specs, out_specs=out_specs, check_vma=False)
```

```python
import functools
import math

import jax
import jax.numpy as jnp
from jax import lax
from jax.experimental import pallas as pl
from jax.experimental.pallas import tpu as pltpu
from jax.sharding import PartitionSpec as P

NBLOCK = 7
f32 = jnp.float32
bf16 = jnp.bfloat16
highest = lax.Precision.HIGHEST
norm_epsilon = 1e-05
adam_epsilon = 1e-08
beta_first = 0.5
beta_second = 0.5
rate_matrix = 0.03
rate_vector = 0.4
weight_decay = 0.01


def dot(a, b):
    return jnp.dot(a, b, preferred_element_type=f32)


def dot_tb(a, b):
    return lax.dot_general(a, b, (((1,), (1,)), ((), ())), preferred_element_type=f32)


def dot_ta(a, b):
    return lax.dot_general(a, b, (((0,), (0,)), ((), ())), preferred_element_type=f32)


def eights(x):
    return jnp.sum(x.reshape(x.shape[0] // 8, 8, x.shape[1]), axis=0)


def sigmoid(z):
    return 0.5 * jnp.tanh(0.5 * z) + 0.5


def branch_forward(z, w_out, bias_out):
    s = sigmoid(z)
    h = z * s
    slope = s + h * (1.0 - s)
    hidden = h.astype(bf16)
    after = dot(hidden, w_out) + bias_out
    center = after - jnp.mean(after, axis=1, keepdims=True)
    spread = jnp.mean(center * center, axis=1, keepdims=True)
    inverse = lax.rsqrt(spread + norm_epsilon)
    return hidden, slope, center * inverse, inverse


def norm_backward(upstream, normed, inverse, gain):
    u = upstream * gain
    first = jnp.mean(u, axis=1, keepdims=True)
    second = jnp.mean(u * normed, axis=1, keepdims=True)
    return (inverse * (u - first - normed * second)).astype(bf16)


def layer_kernel(
    rollout_ref,
    slot_block_ref,
    node_hbm,
    edge_hbm,
    ncot_hbm,
    ecot_hbm,
    sender_ref,
    receiver_ref,
    halo_ref,
    w_ref,
    vec_ref,
    nout_ref,
    eout_hbm,
    nbase_ref,
    egrad_hbm,
    grad_ref,
    gvec_ref,
    hback_ref,
    node_v,
    edge_v,
    ncot_v,
    ecot_v,
    eout_v,
    egrad_v,
    gather_t,
    gather,
    table,
    hidden_v,
    slope_v,
    normed_v,
    inv_v,
    dz_v,
    da_v,
    summed_v,
    dsum_v,
    sc_own,
    sc_recv,
    sc_halo,
    acc,
    sem_in,
    sem_out,
):
    roll, nodes, width = node_v.shape
    edges = edge_v.shape[1]
    peers, per_peer = sc_halo.shape[0], sc_halo.shape[2]
    halo = peers * per_peer
    known = nodes + halo
    padded = table.shape[1]
    chunk = 256
    pieces = edges // chunk

    copies = []
    for i, (src, dst) in enumerate(
        ((node_hbm, node_v), (edge_hbm, edge_v), (ncot_hbm, ncot_v), (ecot_hbm, ecot_v))
    ):
        copies.append(pltpu.make_async_copy(src.at[0], dst, sem_in.at[i]))
        copies[-1].start()

    slot_of = []
    for b in range(NBLOCK):
        found = jnp.int32(0)
        for s in range(slot_block_ref.shape[0]):
            found = jnp.where(slot_block_ref[s] == b, jnp.int32(s), found)
        slot_of.append(found)

    def weight(b):
        return w_ref[slot_of[b]]

    def live(t):
        return jnp.where(t < rollout_ref[0], 1.0, 0.0).astype(f32)

    ids = lax.broadcasted_iota(jnp.int32, (padded, edges), 0)
    onehot = (ids == sender_ref[...]) | (ids == receiver_ref[...] + known)
    onehot = jnp.where(onehot, 1.0, 0.0).astype(f32)
    gather_t[...] = onehot.astype(bf16)
    gather[...] = onehot.T.astype(bf16)
    table[...] = jnp.zeros_like(table)
    acc[...] = jnp.zeros_like(acc)

    copies[0].wait()
    flat_nodes = node_v[...].reshape(roll * nodes, width)
    own_sent = dot(flat_nodes, weight(1))
    own_recv = dot(flat_nodes, weight(2))
    halo_sent = dot(halo_ref[...], weight(1)).reshape(peers, roll, per_peer, width)
    for t in range(roll):
        table[t, :nodes] = own_sent[t * nodes : (t + 1) * nodes].astype(bf16)
        table[t, nodes:known] = halo_sent[:, t].reshape(halo, width).astype(bf16)
        table[t, known : known + nodes] = own_recv[t * nodes : (t + 1) * nodes].astype(bf16)
    copies[1].wait()

    def forward(t, carry):
        lv = live(t)
        total = jnp.zeros((nodes, width), f32)
        for c in range(pieces):
            rows = pl.ds(c * chunk, chunk)
            edge = edge_v[t, rows]
            z = dot(edge, weight(0)) + dot(gather[rows], table[t]) + vec_ref[0:1]
            hidden, slope, normed, inverse = branch_forward(z, weight(3), vec_ref[1:2])
            hidden_v[t, rows] = hidden
            slope_v[t, rows] = slope.astype(bf16)
            normed_v[t, rows] = normed.astype(bf16)
            inv_v[t, rows] = inverse
            new = edge.astype(f32) + (normed * vec_ref[2:3] + vec_ref[3:4])
            eout_v[t, rows] = (new * lv).astype(bf16)
            total += dot(gather_t[known : known + nodes, rows], new.astype(bf16))
        summed_v[pl.ds(t * nodes, nodes)] = total.astype(bf16)
        pltpu.make_async_copy(eout_v.at[t], eout_hbm.at[0, t], sem_out.at[t]).start()
        return carry

    lax.fori_loop(0, roll, forward, 0)

    flat_nodes = node_v[...].reshape(roll * nodes, width)
    summed = summed_v[...]
    z = dot(flat_nodes, weight(4)) + dot(summed, weight(5)) + vec_ref[4:5]
    hidden, slope, normed, inverse = branch_forward(z, weight(6), vec_ref[5:6])
    row_t = lax.broadcasted_iota(jnp.int32, (roll * nodes, 1), 0) // nodes
    row_live = jnp.where(row_t < rollout_ref[0], 1.0, 0.0).astype(f32)
    new = flat_nodes.astype(f32) + (normed * vec_ref[6:7] + vec_ref[7:8])
    nout_ref[0] = (new * row_live).astype(bf16).reshape(roll, nodes, width)
    copies[2].wait()
    d_new = ncot_v[...].reshape(roll * nodes, width).astype(f32) * row_live
    acc[6] += eights(d_new * normed)
    acc[7] += eights(d_new)
    d_after = norm_backward(d_new, normed, inverse, vec_ref[6:7])
    acc[5] += eights(d_after.astype(f32))
    grad_ref[6] = dot_ta(hidden, d_after)
    d_before = (dot_tb(d_after, weight(6)) * slope).astype(bf16)
    acc[4] += eights(d_before.astype(f32))
    grad_ref[4] = dot_ta(flat_nodes, d_before)
    grad_ref[5] = dot_ta(summed, d_before)
    dsum_v[...] = dot_tb(d_before, weight(5)).astype(bf16)
    nbase_ref[...] = d_new + dot_tb(d_before, weight(4))
    grad_ref[0] = jnp.zeros((width, width), f32)
    grad_ref[3] = jnp.zeros((width, width), f32)
    copies[3].wait()

    def backward(t, carry):
        lv = live(t)
        for c in range(pieces):
            rows = pl.ds(c * chunk, chunk)
            d_new = ecot_v[t, rows].astype(f32) * lv + dot(
                gather[rows, known : known + nodes], dsum_v[pl.ds(t * nodes, nodes)]
            )
            normed = normed_v[t, rows].astype(f32)
            acc[2] += eights(d_new * normed)
            acc[3] += eights(d_new)
            d_after = norm_backward(d_new, normed, inv_v[t, rows], vec_ref[2:3])
            acc[1] += eights(d_after.astype(f32))
            da_v[rows] = d_after
            d_before = (dot_tb(d_after, weight(3)) * slope_v[t, rows].astype(f32)).astype(bf16)
            acc[0] += eights(d_before.astype(f32))
            dz_v[rows] = d_before
            egrad_v[t, rows] = (d_new + dot_tb(d_before, weight(0))).astype(bf16)
        pltpu.make_async_copy(egrad_v.at[t], egrad_hbm.at[0, t], sem_out.at[roll + t]).start()
        grad_ref[3] += dot_ta(hidden_v[t], da_v[...])
        grad_ref[0] += dot_ta(edge_v[t], dz_v[...])
        scattered = dot(gather_t[...], dz_v[...])
        sc_own[pl.ds(t * nodes, nodes)] = scattered[:nodes].astype(bf16)
        sc_recv[pl.ds(t * nodes, nodes)] = scattered[known : known + nodes].astype(bf16)
        sc_halo[:, t] = scattered[nodes:known].reshape(peers, per_peer, width)
        return carry

    lax.fori_loop(0, roll, backward, 0)

    halo_sum = sc_halo[...].reshape(roll * halo, width).astype(bf16)
    grad_ref[1] = dot_ta(flat_nodes, sc_own[...]) + dot_ta(halo_ref[...], halo_sum)
    grad_ref[2] = dot_ta(flat_nodes, sc_recv[...])
    hback_ref[...] = dot_tb(halo_sum, weight(1)).astype(bf16)
    nbase_ref[...] += dot_tb(sc_own[...], weight(1)) + dot_tb(sc_recv[...], weight(2))
    gvec_ref[...] = jnp.sum(acc[...], axis=1)

    for t in range(roll):
        pltpu.make_async_copy(eout_v.at[t], eout_hbm.at[0, t], sem_out.at[t]).wait()
        pltpu.make_async_copy(egrad_v.at[t], egrad_hbm.at[0, t], sem_out.at[roll + t]).wait()


def layer(
    rollout_length,
    slot_block,
    node_state,
    edge_state,
    node_cotangent,
    edge_cotangent,
    edge_sender,
    edge_receiver,
    halo,
    slots,
    vector_params,
    per_peer,
):
    _, roll, nodes, width = node_state.shape
    edges = edge_state.shape[2]
    peers = halo.shape[0] // (roll * per_peer)
    known = nodes + peers * per_peer
    padded = -(-(known + nodes) // 128) * 128
    vmem = pl.BlockSpec(memory_space=pltpu.VMEM)
    smem = pl.BlockSpec(memory_space=pltpu.SMEM)
    hbm = pl.BlockSpec(memory_space=pl.ANY)
    shape = jax.ShapeDtypeStruct
    return pl.pallas_call(
        layer_kernel,
        out_shape=(
            shape(node_state.shape, bf16),
            shape(edge_state.shape, bf16),
            shape((roll * nodes, width), f32),
            shape(edge_state.shape, bf16),
            shape((NBLOCK, width, width), f32),
            shape((8, width), f32),
            shape(halo.shape, bf16),
        ),
        in_specs=[smem, smem, hbm, hbm, hbm, hbm, vmem, vmem, vmem, vmem, vmem],
        out_specs=(vmem, hbm, vmem, hbm, vmem, vmem, vmem),
        scratch_shapes=[
            pltpu.VMEM((roll, nodes, width), bf16),
            pltpu.VMEM((roll, edges, width), bf16),
            pltpu.VMEM((roll, nodes, width), bf16),
            pltpu.VMEM((roll, edges, width), bf16),
            pltpu.VMEM((roll, edges, width), bf16),
            pltpu.VMEM((roll, edges, width), bf16),
            pltpu.VMEM((padded, edges), bf16),
            pltpu.VMEM((edges, padded), bf16),
            pltpu.VMEM((roll, padded, width), bf16),
            pltpu.VMEM((roll, edges, width), bf16),
            pltpu.VMEM((roll, edges, width), bf16),
            pltpu.VMEM((roll, edges, width), bf16),
            pltpu.VMEM((roll, edges, 1), f32),
            pltpu.VMEM((edges, width), bf16),
            pltpu.VMEM((edges, width), bf16),
            pltpu.VMEM((roll * nodes, width), bf16),
            pltpu.VMEM((roll * nodes, width), bf16),
            pltpu.VMEM((roll * nodes, width), bf16),
            pltpu.VMEM((roll * nodes, width), bf16),
            pltpu.VMEM((peers, roll, per_peer, width), f32),
            pltpu.VMEM((8, 8, width), f32),
            pltpu.SemaphoreType.DMA((4,)),
            pltpu.SemaphoreType.DMA((2 * roll,)),
        ],
        compiler_params=pltpu.CompilerParams(vmem_limit_bytes=60 << 20),
        name="layer",
    )(
        rollout_length,
        slot_block,
        node_state,
        edge_state,
        node_cotangent,
        edge_cotangent,
        edge_sender.reshape(1, edges),
        edge_receiver.reshape(1, edges),
        halo,
        slots,
        vector_params,
    )


def adam_direction(moment_one, moment_two, fix_one, fix_two):
    return moment_one / fix_one / (jnp.sqrt(moment_two / fix_two) + adam_epsilon)


MESH = pl.DeviceIdType.MESH


class Place:
    def __init__(self):
        self.z = lax.axis_index("dp")
        self.n = lax.axis_index("node")
        self.c = lax.rem(self.n, 2)
        self.x = lax.rem(self.n // 2, 2)
        self.y = self.n // 4
        self.xn = self.n + 2 - 4 * self.x
        self.yn = self.n + 4 - 8 * self.y
        self.sib = self.n + 1 - 2 * self.c
        self.diag = self.xn + 4 - 8 * self.y


def remote(src, dst, send, recv, z, n):
    return pltpu.make_async_remote_copy(
        src_ref=src, dst_ref=dst, send_sem=send, recv_sem=recv, device_id=(z, n), device_id_type=MESH
    )


def greet_start(p, depth, peers):
    barrier = pltpu.get_barrier_semaphore()
    for k in range(1, peers):
        to = lax.rem(p.n + k, peers)
        pl.semaphore_signal(barrier, inc=1, device_id=(p.z, to), device_id_type=MESH)
    for k in range(1, depth):
        to = lax.rem(p.z + k, depth)
        pl.semaphore_signal(barrier, inc=1, device_id=(to, p.n), device_id_type=MESH)


def greet_end(depth, peers):
    pl.semaphore_wait(pltpu.get_barrier_semaphore(), peers + depth - 2)


ORDER = ((0, 1, 2, 3), (1, 0, 2, 3), (2, 3, 1, 0), (3, 2, 1, 0))


def gather_start(p, buf, k, sems):
    send, recv = sems
    own = buf(k, p.n)
    copies = []
    for i, to in ((0, p.xn), (1, p.yn), (3, p.sib)):
        copies.append(remote(own, own, send.at[i, k], recv.at[i, k], p.z, to))
        copies[-1].start()
    return copies


def gather_side(p, buf, k, sems, over_far=True):
    send, recv = sems
    copies = []
    for i, owner in ((0, p.xn), (1, p.yn)):
        got = buf(k, owner)
        remote(got, got, send.at[i, k], recv.at[i, k], p.z, owner).wait_recv()
        on = remote(got, got, send.at[4 + i, k], recv.at[4 + i, k], p.z, p.sib)
        on.start()
        copies.append(on)
        if over_far:
            over = remote(got, got, send.at[2, k], recv.at[2, k], p.z, p.yn if i == 0 else p.xn)
            pl.when(p.c == i)(over.start)
    if over_far:
        copies.append(over)
    return copies


def gather_far(p, buf, k, sems):
    send, recv = sems
    got = buf(k, p.diag)
    remote(got, got, send.at[2, k], recv.at[2, k], p.z, p.xn).wait_recv()
    on = remote(got, got, send.at[6, k], recv.at[6, k], p.z, p.sib)
    on.start()
    return [on]


def gather_end(p, buf, k, sems):
    send, recv = sems
    for i in (3, 4, 5, 6):
        got = buf(k, p.sib)
        remote(got, got, send.at[i, k], recv.at[i, k], p.z, p.sib).wait_recv()


class Step:
    def __init__(self, **refs):
        self.__dict__.update(refs)


def step_kernel(names, *refs):
    k = Step(**dict(zip(names, refs, strict=True)))
    p = Place()
    depth, peers = 4, 8
    roll, nodes, width = k.node_v.shape
    edges = k.edge_v.shape[1]
    slot_dev, rows = k.weight_v.shape[:2]
    per_peer = k.halo.shape[1] // roll
    halo = peers * per_peer
    known = nodes + halo
    padded = k.table.shape[1]
    chunk = edges
    pieces = edges // chunk
    going = []

    def launch(src, dst, send, recv, z, n):
        copy = remote(src, dst, send, recv, z, n)
        copy.start()
        going.append((copy, None))

    def landed(dst, recv):
        remote(dst, dst, recv, recv, p.z, p.sib).wait_recv()

    loads = []
    for i, (src, dst) in enumerate(
        (
            (k.weight_hbm, k.weight_v),
            (k.node_hbm.at[0], k.node_v),
            (k.left_hbm, k.grad.at[2, :slot_dev]),
            (k.right_hbm, k.grad.at[:slot_dev]),
            (k.edge_hbm.at[0], k.edge_v),
            (k.ncot_hbm.at[0], k.ncot_v),
            (k.ecot_hbm.at[0], k.egrad_v.at[0]),
            (k.first_hbm, k.first_v),
            (k.second_hbm, k.second_v),
        )
    ):
        loads.append(pltpu.make_async_copy(src, dst, k.in_sem.at[i]))
        loads[-1].start()
    greet_start(p, depth, peers)

    cut = rows * 3 // 4

    def shard(j):
        top = cut if j % slot_dev == slot_dev - 1 else rows
        return lambda slot, n: k.slots.at[slot, n // 2, lax.rem(n, 2), :top]

    def rest(slot):
        return k.slots.at[slot, :, p.c, cut:]

    planes = []
    for j in range(depth):
        z_of = 0
        for z in range(depth):
            z_of = z_of + jnp.where(p.z == z, ORDER[z][j], 0)
        planes.append(z_of)

    def along_z(z_of):
        return (
            (0, (z_of <= p.z) & (p.z < depth - 1) & (p.z - z_of < depth - 2), p.z + 1),
            (1, (z_of >= p.z) & (p.z > 0) & (z_of - p.z < depth - 2), p.z - 1),
            (2, (z_of == p.z) & ((p.z == 0) | (p.z == depth - 1)), depth - 1 - p.z),
        )

    def rest_hop(s, i):
        own = k.slots.at[p.z * slot_dev + s, p.n // 2, p.c, cut:]
        to = (p.xn, p.yn, p.diag)[i]
        return remote(own, own, k.b_send.at[i, s], k.b_recv.at[i, s], p.z, to)

    def rest_start(s):
        for i in range(3):
            rest_hop(s, i).start()
            going.append((rest_hop(s, i), None))

    def rest_pass(j, s):
        slot = planes[j] * slot_dev + s
        ref = rest(slot)
        if j == 0:
            for i in range(3):
                rest_hop(s, i).wait_recv()
        else:
            remote(ref, ref, k.bz_send.at[0, slot], k.bz_recv.at[slot], p.z, p.sib).wait_recv()
        for i, test, to in along_z(planes[j]):
            if i == 2 and j:
                continue
            copy = remote(ref, ref, k.bz_send.at[i, slot], k.bz_recv.at[slot], to, p.n)
            pl.when(test)(copy.start)
            going.append((copy, test))
        copy = remote(ref, ref, k.bs_send.at[slot], k.bs_recv.at[slot], p.z, p.sib)
        copy.start()
        going.append((copy, None))

    def rest_end(slot):
        ref = rest(slot)
        remote(ref, ref, k.bs_send.at[slot], k.bs_recv.at[slot], p.z, p.sib).wait_recv()

    wsems = (k.w_send, k.w_recv)
    order = []

    def arrive(j):
        z_of = planes[j // slot_dev]
        slot = z_of * slot_dev + j % slot_dev
        order.append(slot)
        piece = shard(j)(slot, p.n)
        if j >= slot_dev:
            remote(piece, piece, k.wz_send.at[0, slot], k.wz_recv.at[slot], p.z, p.n).wait_recv()
        for i, test, to in along_z(z_of):
            if i == 2 and j >= slot_dev:
                continue
            copy = remote(piece, piece, k.wz_send.at[i, slot], k.wz_recv.at[slot], to, p.n)
            pl.when(test)(copy.start)
            going.append((copy, test))
        going.extend((copy, None) for copy in gather_start(p, shard(j), slot, wsems))

    def side(j):
        going.extend((copy, None) for copy in gather_side(p, shard(j), order[j], wsems))

    def far(j):
        going.extend((copy, None) for copy in gather_far(p, shard(j), order[j], wsems))

    loads[0].wait()
    k.slots[pl.ds(slot_dev * p.z, slot_dev), p.n // 2, p.c] = k.weight_v[...].astype(bf16)
    greet_end(depth, peers)

    def rounds(*names):
        for name in names:
            i = int(name[1:])
            if name[0] == "b":
                rest_pass(i // slot_dev, i % slot_dev)
            else:
                {"a": arrive, "s": side, "f": far}[name[0]](i)

    rest_start(slot_dev - 1)
    rounds("a0", "a1")
    loads[1].wait()
    node_ids = lax.broadcasted_iota(jnp.int32, (nodes, halo), 0)
    pick_t = jnp.where(node_ids == k.rows_ref[...], 1.0, 0.0).astype(bf16)
    for t in range(roll):
        k.spread[:, t] = dot_ta(pick_t, k.node_v[t]).reshape(peers, per_peer, width)
    k.hput[...] = k.spread[...].reshape(peers, roll * per_peer, width).astype(bf16)
    k.halo[p.n] = k.hput[p.n]
    rounds("a2", "a3", "s0", "s1")
    loads[2].wait()
    for s in range(slot_dev):
        k.pre[2 * slot_dev + s, p.n] = k.grad[2, s].astype(bf16)
        for m in range(peers):
            k.lput[s, m] = k.grad[2, s, :, m * rows : (m + 1) * rows].astype(bf16)
    k.lgot[:, p.n] = k.lput[:, p.n]
    rounds("a4", "a5", "s2", "s3", "b1", "f0", "f1")
    ids = lax.broadcasted_iota(jnp.int32, (padded, edges), 0)
    onehot = (ids == k.sender_ref[...].reshape(1, edges)) | (
        ids == k.receiver_ref[...].reshape(1, edges) + known
    )
    onehot = jnp.where(onehot, 1.0, 0.0).astype(f32)
    k.gather_t[...] = onehot.astype(bf16)
    rounds("a6", "a7", "s4", "s5", "b3", "f2", "f3")
    k.gather[...] = onehot.T.astype(bf16)
    k.table[:, known + nodes :] = jnp.zeros((roll, padded - known - nodes, width), bf16)
    k.acc[...] = jnp.zeros_like(k.acc)
    rounds("s6", "s7")
    hsent = []
    for i in range(1, peers):
        to = lax.rem(p.n + i, peers)
        hsent.append(remote(k.hput.at[to], k.halo.at[p.n], k.h_send.at[0, i], k.h_recv.at[0, i], p.z, to))
        hsent[-1].start()
    rounds("b5", "f4", "f5", "b7")
    loads[3].wait()
    for s in range(slot_dev):
        k.right_b[s] = k.grad[s].reshape(width, width).astype(bf16)
    rounds("f6", "f7")
    for j, slot in enumerate(order):
        gather_end(p, shard(j), slot, wsems)
        if j % slot_dev == slot_dev - 1:
            rest_end(slot)

    slot_of = []
    for b in range(NBLOCK):
        found = 0
        for s in range(depth * slot_dev):
            found = jnp.where(k.slot_block_ref[s] == b, s, found)
        slot_of.append(found)

    def weight(b):
        return k.slots[slot_of[b]].reshape(width, width)

    rollout = k.rollout_ref[0]
    vec = k.vec_ref

    def live(t):
        return jnp.where(t < rollout, 1.0, 0.0).astype(f32)

    def flat_nodes():
        return k.node_v[...].reshape(roll * nodes, width)

    own_sent = dot(flat_nodes(), weight(1))
    own_recv = dot(flat_nodes(), weight(2))
    for copy in hsent:
        copy.wait_send()
    for i in range(1, peers):
        landed(k.halo.at[0], k.h_recv.at[0, i])
    halo_flat = k.halo[...].reshape(roll * halo, width)
    halo_sent = dot(halo_flat, weight(1)).reshape(peers, roll, per_peer, width)
    for t in range(roll):
        k.table[t, :nodes] = own_sent[t * nodes : (t + 1) * nodes].astype(bf16)
        k.table[t, nodes:known] = halo_sent[:, t].reshape(halo, width).astype(bf16)
        k.table[t, known : known + nodes] = own_recv[t * nodes : (t + 1) * nodes].astype(bf16)
    loads[4].wait()

    for i in range(1, peers):
        to = lax.rem(p.n + i, peers)
        launch(k.lput.at[:, to], k.lgot.at[:, p.n], k.l_send.at[i], k.l_recv.at[i], p.z, to)
    loads[7].wait()
    loads[8].wait()
    psems = (k.p_send, k.p_recv)
    early = range(3 * slot_dev)
    pbuf = lambda i, n: k.pre.at[i, n]
    for s in range(slot_dev):
        k.pre[s, p.n] = k.first_v[s].astype(bf16)
        k.pre[slot_dev + s, p.n] = k.second_v[s].astype(bf16)
    for i in early:
        going.extend((copy, None) for copy in gather_start(p, pbuf, i, psems))

    def forward(t, carry):
        lv = live(t)
        total = jnp.zeros((nodes, width), f32)
        for c in range(pieces):
            at = pl.ds(c * chunk, chunk)
            edge = k.edge_v[t, at]
            z = dot(edge, weight(0)) + dot(k.gather[at], k.table[t]) + vec[0:1]
            hidden, slope, normed, inverse = branch_forward(z, weight(3), vec[1:2])
            k.hidden_v[t, at] = hidden
            k.slope_v[t, at] = slope.astype(bf16)
            k.normed_v[t, at] = normed.astype(bf16)
            k.inv_v[t, at] = inverse
            new = edge.astype(f32) + (normed * vec[2:3] + vec[3:4])
            k.eout_v[0, t, at] = (new * lv).astype(bf16)
            total += dot(k.gather_t[known : known + nodes, at], new.astype(bf16))
        k.summed_v[pl.ds(t * nodes, nodes)] = total.astype(bf16)
        return carry

    for t in range(roll):
        forward(t, 0)

    on_f = jnp.where(p.c == 0, p.x, p.y)
    on_g = jnp.where(p.c == 0, p.y, p.x)
    to_f = jnp.where(p.c == 0, p.xn, p.yn)
    to_g = jnp.where(p.c == 0, p.yn, p.xn)

    def spot(f, g):
        return jnp.where(p.c == 0, g * 2 + f, f * 2 + g)

    def hop(stage, b):
        put, got, to = (
            (k.cast, k.got_core, p.sib),
            (k.put_one, k.got_one, to_f),
            (k.put_two, k.got_two, to_g),
        )[stage]
        at = stage * NBLOCK + b
        return remote(put.at[b], got.at[b], k.r_send.at[at], k.r_recv.at[at], p.z, to)

    def to_core(b):
        for i in range(peers // 2):
            k.cast[b, i] = k.grad[b, 2 * i + 1 - p.c].astype(bf16)
        hop(0, b).start()

    def to_first(b):
        hop(0, b).wait_recv()
        for g in range(2):
            at = spot(1 - on_f, g)
            k.put_one[b, g] = (k.grad[b, 2 * at + p.c] + k.got_core[b, at].astype(f32)).astype(bf16)
        hop(1, b).start()
        for g in range(2):
            at = spot(on_f, g)
            k.grad[b, 2 * at + p.c] = k.grad[b, 2 * at + p.c] + k.got_core[b, at].astype(f32)

    def to_second(b):
        hop(1, b).wait_recv()
        at = spot(on_f, 1 - on_g)
        total = k.grad[b, 2 * at + p.c] + k.got_one[b, 1 - on_g].astype(f32)
        k.put_two[b] = total.astype(bf16)
        hop(2, b).start()
        k.grad[b, p.n] = k.grad[b, p.n] + k.got_one[b, on_g].astype(f32)

    def settle(b):
        hop(2, b).wait_recv()
        k.grad[b, p.n] = k.grad[b, p.n] + k.got_two[b].astype(f32)

    def put_grad(b, value):
        k.grad[b] = value.reshape(peers, rows, width)

    summed = k.summed_v[...]
    z = dot(flat_nodes(), weight(4)) + dot(summed, weight(5)) + vec[4:5]
    hidden, slope, normed, inverse = branch_forward(z, weight(6), vec[5:6])
    row_t = lax.broadcasted_iota(jnp.int32, (roll * nodes, 1), 0) // nodes
    row_live = jnp.where(row_t < rollout, 1.0, 0.0).astype(f32)
    new = flat_nodes().astype(f32) + (normed * vec[6:7] + vec[7:8])
    k.nout_v[0] = (new * row_live).astype(bf16).reshape(roll, nodes, width)
    loads[5].wait()
    d_new = k.ncot_v[...].reshape(roll * nodes, width).astype(f32) * row_live
    k.acc[6] = eights(d_new * normed)
    k.acc[7] = eights(d_new)
    d_after = norm_backward(d_new, normed, inverse, vec[6:7])
    k.acc[5] = eights(d_after.astype(f32))
    put_grad(6, dot_ta(hidden, d_after))
    to_core(6)
    d_before = (dot_tb(d_after, weight(6)) * slope).astype(bf16)
    k.acc[4] = eights(d_before.astype(f32))
    put_grad(4, dot_ta(flat_nodes(), d_before))
    to_core(4)
    put_grad(5, dot_ta(summed, d_before))
    to_core(5)
    k.summed_v[...] = dot_tb(d_before, weight(5)).astype(bf16)
    k.table[:, 2 * nodes : 3 * nodes] = d_before.reshape(roll, nodes, width)
    for i in early:
        going.extend((copy, None) for copy in gather_side(p, pbuf, i, psems))
    k.grad[0] = jnp.zeros((peers, rows, width), f32)
    k.grad[3] = jnp.zeros((peers, rows, width), f32)
    loads[6].wait()

    def backward(t, carry):
        lv = live(t)
        for c in range(pieces):
            at = pl.ds(c * chunk, chunk)
            d_new = k.egrad_v[0, t, at].astype(f32) * lv + dot(
                k.gather[at, known : known + nodes], k.summed_v[pl.ds(t * nodes, nodes)]
            )
            k.egrad_v[0, t, at] = d_new.astype(bf16)
            normed = k.normed_v[t, at].astype(f32)
            k.acc[2] += eights(d_new * normed)
            k.acc[3] += eights(d_new)
            d_after = norm_backward(d_new, normed, k.inv_v[t, at], vec[2:3])
            k.acc[1] += eights(d_after.astype(f32))
            k.normed_v[t, at] = d_after
            d_before = (dot_tb(d_after, weight(3)) * k.slope_v[t, at].astype(f32)).astype(bf16)
            k.acc[0] += eights(d_before.astype(f32))
            k.slope_v[t, at] = d_before
        k.grad[3] += dot_ta(k.hidden_v[t], k.normed_v[t]).reshape(peers, rows, width)
        k.grad[0] += dot_ta(k.edge_v[t], k.slope_v[t]).reshape(peers, rows, width)
        scattered = dot(k.gather_t[...], k.slope_v[t])
        k.table[t, :nodes] = scattered[:nodes].astype(bf16)
        k.table[t, nodes : 2 * nodes] = scattered[known : known + nodes].astype(bf16)
        k.spread[:, t] = scattered[nodes:known].reshape(peers, per_peer, width)
        for step, work in enumerate((to_first, to_second, settle)):

            @pl.when(t == step)
            def _():
                def one(b, carry):
                    work(b)
                    return carry

                lax.fori_loop(4, NBLOCK, one, 0)

        return carry

    lax.fori_loop(0, roll, backward, 0)

    def kept(i):
        return k.table[:, i * nodes : (i + 1) * nodes].reshape(roll * nodes, width)

    def edge_gradient(t):
        for c in range(pieces):
            at = pl.ds(c * chunk, chunk)
            grown = k.egrad_v[0, t, at].astype(f32) + dot_tb(k.slope_v[t, at], weight(0))
            k.egrad_v[0, t, at] = grown.astype(bf16)

    to_core(3)
    to_core(0)
    k.hput[...] = k.spread[...].reshape(peers, roll * per_peer, width).astype(bf16)
    put_grad(1, dot_ta(flat_nodes(), kept(0)) + dot_ta(halo_flat, k.hput[...].reshape(roll * halo, width)))
    to_core(1)
    to_first(3)
    put_grad(2, dot_ta(flat_nodes(), kept(1)))
    to_core(2)
    to_first(0)
    k.vput[0] = jnp.sum(k.acc[...], axis=1)
    launch(k.vput.at[0], k.vgot.at[0], k.v_send.at[0], k.v_recv.at[0], p.z, p.sib)
    to_first(1)
    to_second(3)
    to_first(2)
    landed(k.vgot.at[0], k.v_recv.at[0])
    k.vput[1] = k.vput[0] + k.vgot[0]
    launch(k.vput.at[1], k.vgot.at[1], k.v_send.at[1], k.v_recv.at[1], p.z, p.xn)
    to_second(0)
    for i in early:
        going.extend((copy, None) for copy in gather_far(p, pbuf, i, psems))
    to_second(1)
    settle(3)
    to_second(2)
    settle(0)
    landed(k.vgot.at[1], k.v_recv.at[1])
    k.vput[2] = k.vput[1] + k.vgot[1]
    launch(k.vput.at[2], k.vgot.at[2], k.v_send.at[2], k.v_recv.at[2], p.z, p.yn)
    for i in range(1, peers):
        to = lax.rem(p.n + i, peers)
        launch(k.hput.at[to], k.hret.at[p.n], k.h_send.at[1, i], k.h_recv.at[1, i], p.z, to)
    k.hret[p.n] = k.hput[p.n]
    settle(1)
    settle(2)

    def part(target, s):
        b = k.slot_block_ref[target * slot_dev + s]
        held = k.grad[jnp.minimum(b, NBLOCK - 1), p.n]
        return jnp.where(b < NBLOCK, held, 0.0)

    last = depth - 1

    def z_hop(way, target, s, to):
        put, got = (k.put_up, k.got_up) if way == 0 else (k.put_down, k.got_down)
        return remote(
            put.at[target, s], got.at[target, s], k.z_send.at[way, target, s], k.z_recv.at[way, target, s], to, p.n
        )

    def far_hop(s):
        return remote(k.put_far.at[s], k.got_far.at[s], k.f_send.at[s], k.f_recv.at[s], last - p.z, p.n)

    def pass_on(way):
        put, got = (k.put_up, k.got_up) if way == 0 else (k.put_down, k.got_down)
        to = p.z + 1 if way == 0 else p.z - 1
        for step in (last, last - 1, 1):
            target = step if way == 0 else last - step
            test = p.z < target if way == 0 else p.z > target
            if step == last:
                end = last if way == 0 else 0
                test = test & (p.z != last - end)
                source = (p.z != last - end) & (p.z != (1 if way == 0 else last - 1))
            else:
                source = p.z > 0 if way == 0 else p.z < last

            @pl.when(test)
            def _():
                for s in range(slot_dev):

                    @pl.when(source)
                    def _():
                        z_hop(way, target, s, to).wait_recv()
                        total = part(target, s) + got[target, s].astype(f32)
                        put[target, s] = total.astype(bf16)

                    @pl.when(jnp.logical_not(source))
                    def _():
                        put[target, s] = part(target, s).astype(bf16)

                    z_hop(way, target, s, to).start()

            if step == last - 1:

                @pl.when(p.z == (0 if way == 0 else last))
                def _():
                    for s in range(slot_dev):
                        k.put_far[s] = part(last - p.z, s).astype(bf16)
                        far_hop(s).start()

    @pl.when(p.z == 0)
    def _():
        pass_on(0)

    @pl.when(p.z == depth - 1)
    def _():
        pass_on(1)

    edge_gradient(0)

    @pl.when(p.z == 1)
    def _():
        pass_on(0)

    @pl.when(p.z == depth - 2)
    def _():
        pass_on(1)

    edge_gradient(1)

    @pl.when(p.z == 1)
    def _():
        pass_on(1)

    @pl.when(p.z == depth - 2)
    def _():
        pass_on(0)

    landed(k.vgot.at[2], k.v_recv.at[2])
    k.vput[3] = k.vput[2] + k.vgot[2]
    k.vz[p.z] = k.vput[3]
    for i in range(1, depth):
        to = lax.rem(p.z + i, depth)
        launch(k.vput.at[3], k.vz.at[p.z], k.v_send.at[2 + i], k.v_recv.at[2 + i], to, p.n)
    edge_gradient(2)
    square = jnp.zeros((8, width), f32)
    gsems = (k.g_send, k.g_recv)
    gbuf = lambda s, n: k.full.at[s, n]
    for s in range(slot_dev):

        @pl.when(p.z > 0)
        def _():
            landed(k.got_up.at[p.z, s], k.z_recv.at[0, p.z, s])

        @pl.when(p.z < depth - 1)
        def _():
            landed(k.got_down.at[p.z, s], k.z_recv.at[1, p.z, s])

        mine = part(p.z, s) + jnp.where(p.z > 0, k.got_up[p.z, s].astype(f32), 0.0)
        mine = mine + jnp.where(p.z < depth - 1, k.got_down[p.z, s].astype(f32), 0.0)

        @pl.when((p.z == 0) | (p.z == last))
        def _():
            far_hop(s).wait_recv()

        mine = mine + jnp.where((p.z == 0) | (p.z == last), k.got_far[s].astype(f32), 0.0)
        k.full[s, p.n] = mine.astype(bf16)
        for copy in gather_start(p, gbuf, s, gsems):
            going.append((copy, None))
        launch(gbuf(s, p.n), gbuf(s, p.n), k.g_send.at[2, s], k.g_recv.at[2, s], p.z, p.diag)
        square = square + eights(mine * mine)
    square = square[:, :128] + square[:, 128:256] + square[:, 256:384] + square[:, 384:]
    k.sput[...] = square
    k.sgot[p.n] = square
    for i in range(1, peers):
        to = lax.rem(p.n + i, peers)
        launch(k.sput, k.sgot.at[p.n], k.n_send.at[i], k.n_recv.at[i], p.z, to)
    edge_gradient(3)

    def collect(buffer, sems, between, finish):
        for s in range(slot_dev):
            going.extend((copy, None) for copy in gather_side(p, buffer, s, sems, False))
        for s in range(slot_dev):
            going.extend((copy, None) for copy in gather_far(p, buffer, s, sems))
        between()
        for s in range(slot_dev):
            gather_end(p, buffer, s, sems)
            finish(s)

    for i in range(1, peers):
        landed(k.sgot.at[0], k.n_recv.at[i])
    k.szput[...] = jnp.sum(k.sgot[...], axis=0)
    k.sz[p.z] = k.szput[...]
    for i in range(1, depth):
        to = lax.rem(p.z + i, depth)
        launch(k.szput, k.sz.at[p.z], k.n_send.at[peers - 1 + i], k.n_recv.at[peers - 1 + i], to, p.n)

    limit = math.sqrt(NBLOCK * width * width + 8 * width)
    found = []

    def fix(beta, step):
        return 1.0 - jnp.exp2(math.log2(beta) * jnp.full((1, 1), step, jnp.int32).astype(f32))

    def norm():
        for i in range(1, depth):
            landed(k.vz.at[0], k.v_recv.at[2 + i])
            landed(k.sz.at[0], k.n_recv.at[peers - 1 + i])
        vectors = k.vz[0] + k.vz[1] + k.vz[2] + k.vz[3]
        square_sum = jnp.sum(k.sz[0] + k.sz[1] + k.sz[2] + k.sz[3], keepdims=True).reshape(1, 1)
        square_sum = square_sum + jnp.sum(vectors * vectors, keepdims=True).reshape(1, 1)
        value = jnp.sqrt(square_sum)
        k.norm_v[...] = jnp.broadcast_to(value, k.norm_v.shape)
        found.extend((vectors, jnp.minimum(1.0, limit / value)))

    def advance(s):
        part_left = dot(k.pre[2 * slot_dev + s].reshape(width, width), k.full[s].reshape(width, width))
        rotated = dot(part_left.astype(bf16), k.right_b[s])
        if s == 0:
            norm()
        k.grad[s] = rotated.reshape(peers, rows, width)
        step = k.step_ref[p.z * slot_dev + s]
        fix_one, fix_two = fix(beta_first, step), fix(beta_second, step)
        clip = found[1]

        def moments(first, second, turn):
            spun = turn * clip
            return (
                beta_first * first + (1.0 - beta_first) * spun,
                beta_second * second + (1.0 - beta_second) * spun * spun,
            )

        one, two = moments(
            k.pre[s].reshape(width, width).astype(f32),
            k.pre[slot_dev + s].reshape(width, width).astype(f32),
            rotated,
        )
        direction = adam_direction(one, two, fix_one, fix_two).astype(bf16)
        turned = dot_tb(direction, k.right_b[s]).astype(bf16)
        reverted = dot_ta(k.lgot[s].reshape(width, rows), turned)
        new = k.weight_v[s] - rate_matrix * (reverted + weight_decay * k.weight_v[s])
        k.wnew_v[s] = new
        k.wcopy_v[s] = new.astype(bf16)
        one, two = moments(k.first_v[s], k.second_v[s], k.grad[s, p.n])
        k.first_v[s] = one
        k.second_v[s] = two

    for i in range(1, peers):
        landed(k.lgot.at[:, 0], k.l_recv.at[i])
    for i in early:
        gather_end(p, pbuf, i, psems)
    def node_gradient():
        for i in range(1, peers):
            landed(k.hret.at[0], k.h_recv.at[1, i])
        back = k.hret[...].astype(f32).reshape(peers, roll, per_peer, width)
        for t in range(roll):
            rows_t = back[:, t].reshape(halo, width).astype(bf16)
            k.table[t, :nodes] = (k.table[t, :nodes].astype(f32) + dot(pick_t, rows_t)).astype(bf16)
        grown = k.ncot_v[...].reshape(roll * nodes, width).astype(f32) * row_live
        grown = grown + dot_tb(kept(0), weight(1)) + dot_tb(kept(1), weight(2)) + dot_tb(kept(2), weight(4))
        k.ngrad_v[0] = grown.astype(bf16).reshape(roll, nodes, width)

    collect(gbuf, gsems, node_gradient, advance)
    grad_vectors, clip = found
    step = k.step_ref[depth * slot_dev]
    spun = grad_vectors * clip
    one = beta_first * k.vfirst_ref[...] + (1.0 - beta_first) * spun
    two = beta_second * k.vsecond_ref[...] + (1.0 - beta_second) * spun * spun
    k.vstate_v[0] = vec[...] - rate_vector * adam_direction(
        one, two, fix(beta_first, step), fix(beta_second, step)
    )
    k.vstate_v[1] = one
    k.vstate_v[2] = two

    for copy, test in going:
        if test is None:
            copy.wait_send()
        else:
            pl.when(test)(copy.wait_send)
    for b in range(NBLOCK):
        for stage in range(3):
            hop(stage, b).wait_send()
    for way in range(2):
        for step in (last, last - 1, 1):
            target = step if way == 0 else last - step
            test = p.z < target if way == 0 else p.z > target
            if step == last:
                test = test & (p.z != last - target)
            for s in range(slot_dev):
                pl.when(test)(z_hop(way, target, s, lax.rem(p.z + 1, depth)).wait_send)
    for s in range(slot_dev):
        pl.when((p.z == 0) | (p.z == last))(far_hop(s).wait_send)


def store_kernel(*refs):
    count = (len(refs) - 3) // 2
    norm, norm_out, sem = refs[count], refs[-2], refs[-1]
    copies = []
    for i in range(count):
        copies.append(pltpu.make_async_copy(refs[i], refs[count + 1 + i], sem.at[i]))
        copies[-1].start()
    norm_out[0] = norm[0, 0]
    for copy in copies:
        copy.wait()


def whole_step(
    node_state,
    edge_state,
    node_cotangent,
    edge_cotangent,
    send_rows,
    edge_sender,
    edge_receiver,
    rollout_length,
    slot_block,
    step_count,
    weight_slots,
    moment_first,
    moment_second,
    basis_left,
    basis_right,
    vector_params,
    vector_first,
    vector_second,
):
    depth, peers = 4, 8
    _, roll, nodes, width = node_state.shape
    edges = edge_state.shape[2]
    slot_dev, rows = weight_slots.shape[:2]
    halo = send_rows.shape[1]
    per_peer = halo // peers
    padded = -(-(2 * nodes + halo) // 128) * 128
    own = (slot_dev, rows, width)
    tile = (8, 128)
    hbm = pl.BlockSpec(memory_space=pl.ANY)
    vmem = pl.BlockSpec(memory_space=pltpu.VMEM)
    smem = pl.BlockSpec(memory_space=pltpu.SMEM)
    shape = jax.ShapeDtypeStruct
    dma = pltpu.SemaphoreType.DMA
    ins = dict(
        rollout_ref=(rollout_length, smem),
        slot_block_ref=(slot_block, smem),
        step_ref=(step_count, smem),
        node_hbm=(node_state, hbm),
        edge_hbm=(edge_state, hbm),
        ncot_hbm=(node_cotangent, hbm),
        ecot_hbm=(edge_cotangent, hbm),
        rows_ref=(send_rows, vmem),
        sender_ref=(edge_sender, vmem),
        receiver_ref=(edge_receiver, vmem),
        weight_hbm=(weight_slots, hbm),
        first_hbm=(moment_first, hbm),
        second_hbm=(moment_second, hbm),
        left_hbm=(jnp.swapaxes(basis_left, 1, 2), hbm),
        right_hbm=(basis_right.reshape(slot_dev, peers, rows, width), hbm),
        vec_ref=(vector_params, vmem),
        vfirst_ref=(vector_first, vmem),
        vsecond_ref=(vector_second, vmem),
    )
    outs = dict(
        nout_v=shape(node_state.shape, bf16),
        eout_v=shape(edge_state.shape, bf16),
        ngrad_v=shape(node_state.shape, bf16),
        egrad_v=shape(edge_state.shape, bf16),
        first_v=shape(own, f32),
        second_v=shape(own, f32),
        wnew_v=shape(own, f32),
        wcopy_v=shape(own, bf16),
        vstate_v=shape((3, 8, width), f32),
        norm_v=shape(tile, f32),
    )
    v = pltpu.VMEM
    scratch = dict(
        weight_v=v(own, f32),
        node_v=v((roll, nodes, width), bf16),
        edge_v=v((roll, edges, width), bf16),
        ncot_v=v((roll, nodes, width), bf16),
        slots=v((slot_dev * depth, peers // 2, 2, rows, width), bf16),
        halo=v((peers, roll * per_peer, width), bf16),
        spread=v((peers, roll, per_peer, width), f32),
        hput=v((peers, roll * per_peer, width), bf16),
        hret=v((peers, roll * per_peer, width), bf16),
        pre=v((3 * slot_dev, peers, rows, width), bf16),
        lput=v((slot_dev, peers, rows, rows), bf16),
        lgot=v((slot_dev, peers, rows, rows), bf16),
        right_b=v((slot_dev, width, width), bf16),
        gather_t=v((padded, edges), bf16),
        gather=v((edges, padded), bf16),
        table=v((roll, padded, width), bf16),
        hidden_v=v((roll, edges, width), bf16),
        slope_v=v((roll, edges, width), bf16),
        normed_v=v((roll, edges, width), bf16),
        inv_v=v((roll, edges, 1), f32),
        summed_v=v((roll * nodes, width), bf16),
        acc=v((8, 8, width), f32),
        grad=v((NBLOCK, peers, rows, width), f32),
        cast=v((NBLOCK, peers // 2, rows, width), bf16),
        got_core=v((NBLOCK, peers // 2, rows, width), bf16),
        put_one=v((NBLOCK, 2, rows, width), bf16),
        got_one=v((NBLOCK, 2, rows, width), bf16),
        put_two=v((NBLOCK, rows, width), bf16),
        got_two=v((NBLOCK, rows, width), bf16),
        put_up=v((depth, *own), bf16),
        put_down=v((depth, *own), bf16),
        got_up=v((depth, *own), bf16),
        got_down=v((depth, *own), bf16),
        put_far=v(own, bf16),
        got_far=v(own, bf16),
        full=v((slot_dev, peers, rows, width), bf16),
        vput=v((4, 8, width), f32),
        vgot=v((3, 8, width), f32),
        vz=v((depth, 8, width), f32),
        sput=v(tile, f32),
        sgot=v((peers, *tile), f32),
        szput=v(tile, f32),
        sz=v((depth, *tile), f32),
        in_sem=dma((9,)),
        w_send=dma((7, depth * slot_dev)),
        w_recv=dma((7, depth * slot_dev)),
        wz_send=dma((3, depth * slot_dev)),
        wz_recv=dma((depth * slot_dev,)),
        b_send=dma((3, slot_dev)),
        b_recv=dma((3, slot_dev)),
        bz_send=dma((3, depth * slot_dev)),
        bz_recv=dma((depth * slot_dev,)),
        bs_send=dma((depth * slot_dev,)),
        bs_recv=dma((depth * slot_dev,)),
        h_send=dma((2, peers)),
        h_recv=dma((2, peers)),
        l_send=dma((peers,)),
        l_recv=dma((peers,)),
        r_send=dma((3 * NBLOCK,)),
        r_recv=dma((3 * NBLOCK,)),
        z_send=dma((2, depth, slot_dev)),
        z_recv=dma((2, depth, slot_dev)),
        f_send=dma((slot_dev,)),
        f_recv=dma((slot_dev,)),
        g_send=dma((7, slot_dev)),
        g_recv=dma((7, slot_dev)),
        p_send=dma((7, 3 * slot_dev)),
        p_recv=dma((7, 3 * slot_dev)),
        v_send=dma((6,)),
        v_recv=dma((6,)),
        n_send=dma((peers + depth - 1,)),
        n_recv=dma((peers + depth - 1,)),
    )
    names = (*ins, *outs, *scratch)
    results = pl.pallas_call(
        functools.partial(step_kernel, names),
        out_shape=tuple(pltpu.VMEM(out.shape, out.dtype) for out in outs.values()),
        in_specs=[spec for _, spec in ins.values()],
        out_specs=(vmem,) * len(outs),
        scratch_shapes=list(scratch.values()),
        compiler_params=pltpu.CompilerParams(
            vmem_limit_bytes=52 << 20, collective_id=0, has_side_effects=True
        ),
        name="step",
    )(
        *(
            pltpu.with_memory_space_constraint(value, pltpu.HBM) if spec is hbm else value
            for value, spec in ins.values()
        )
    )
    final = [*outs.values()][:-1]
    return pl.pallas_call(
        store_kernel,
        out_shape=(*final, shape((1,), f32)),
        in_specs=[vmem] * len(outs),
        out_specs=(*([hbm] * len(final)), smem),
        scratch_shapes=[dma((len(final),))],
        compiler_params=pltpu.CompilerParams(vmem_limit_bytes=40 << 20),
        name="results",
    )(*results)


def local(
    node_state,
    edge_state,
    node_cotangent,
    edge_cotangent,
    send_rows,
    edge_sender,
    edge_receiver,
    rollout_length,
    slot_block,
    step_count,
    weight_slots,
    moment_first,
    moment_second,
    basis_left,
    basis_right,
    vector_params,
    vector_first,
    vector_second,
):
    width = node_state.shape[-1]
    roll, nodes = node_state.shape[1:3]
    clip_limit = math.sqrt(NBLOCK * width * width + 8 * width)
    slot_dev = weight_slots.shape[0]
    slot_total = slot_block.shape[0]
    halo_rows = send_rows.shape[1]
    peers = lax.axis_size("node")
    per_peer = halo_rows // peers
    if (lax.axis_size("dp"), peers) == (4, 8):
        return whole_step(
            node_state,
            edge_state,
            node_cotangent,
            edge_cotangent,
            send_rows,
            edge_sender,
            edge_receiver,
            rollout_length,
            slot_block,
            step_count,
            weight_slots,
            moment_first,
            moment_second,
            basis_left,
            basis_right,
            vector_params,
            vector_first,
            vector_second,
        )
    copies = lax.all_gather(weight_slots.astype(bf16), "node", axis=1, tiled=True)
    slots = lax.all_gather(copies, "dp", axis=0, tiled=True)
    back_onehot = (send_rows[0][:, None] == jnp.arange(nodes, dtype=jnp.int32)[None, :]).astype(bf16)
    outgoing = jnp.einsum("hk,tkd->htd", back_onehot, node_state[0], preferred_element_type=f32)
    outgoing = outgoing.astype(bf16).reshape(peers, per_peer, roll, width).transpose(0, 2, 1, 3)
    outgoing = outgoing.reshape(peers * roll * per_peer, width)
    halo = lax.all_to_all(outgoing, "node", split_axis=0, concat_axis=0, tiled=True)

    node_output, edge_output, node_base, edge_gradient, grads, grad_vectors, halo_back = layer(
        rollout_length,
        slot_block,
        node_state,
        edge_state,
        node_cotangent,
        edge_cotangent,
        edge_sender,
        edge_receiver,
        halo,
        slots,
        vector_params,
        per_peer,
    )
    returned = lax.all_to_all(halo_back, "node", split_axis=0, concat_axis=0, tiled=True)
    returned = returned.reshape(peers, roll, per_peer, width).transpose(0, 2, 1, 3)
    d_back = jnp.einsum(
        "hk,htd->tkd",
        back_onehot,
        returned.reshape(halo_rows, roll, width),
        preferred_element_type=f32,
    )
    node_gradient = node_base.reshape(roll, nodes, width) + d_back
    node_gradient = node_gradient.astype(bf16).reshape(node_state.shape)

    block_of_slot = slot_block[None, :] == jnp.arange(NBLOCK, dtype=jnp.int32)[:, None]
    first = lax.axis_index("dp") * slot_dev
    summed, grad_vectors = lax.psum((grads, grad_vectors), ("dp", "node"))
    own_square = jnp.sum(summed * summed)
    mine = lax.dynamic_slice_in_dim(block_of_slot.astype(f32), first, slot_dev, 1)
    owned_grads = jnp.einsum("bs,bij->sij", mine, summed, precision=highest)
    square_sum = own_square + jnp.sum(grad_vectors * grad_vectors)
    grad_norm = jnp.sqrt(square_sum)
    clip_scale = jnp.minimum(1.0, clip_limit / grad_norm)
    owned_grads = owned_grads * clip_scale
    grad_vectors = grad_vectors * clip_scale
    own_steps = lax.dynamic_slice_in_dim(step_count, first, slot_dev, 0)
    slot_steps = own_steps.astype(f32)[:, None, None]
    fix_one = 1.0 - jnp.power(f32(beta_first), slot_steps)
    fix_two = 1.0 - jnp.power(f32(beta_second), slot_steps)
    rotated = jnp.einsum("sij,sik->sjk", basis_left, owned_grads, precision=highest, preferred_element_type=f32)
    rotated = jnp.einsum("sjk,skl->sjl", rotated, basis_right, precision=highest, preferred_element_type=f32)
    moment_one = beta_first * moment_first + (1.0 - beta_first) * rotated
    moment_two = beta_second * moment_second + (1.0 - beta_second) * rotated * rotated
    direction = adam_direction(moment_one, moment_two, fix_one, fix_two)
    turned = jnp.einsum("sjl,sml->sjm", direction, basis_right, precision=highest, preferred_element_type=f32)
    reverted = jnp.einsum("sij,sjm->ism", basis_left, turned, precision=highest, preferred_element_type=f32)
    reverted = lax.psum_scatter(reverted.astype(bf16), "node", scatter_dimension=0, tiled=True).astype(f32)
    reverted = jnp.transpose(reverted, (1, 0, 2))
    new_weights = weight_slots - rate_matrix * (reverted + weight_decay * weight_slots)
    vec_step = step_count[slot_total].astype(f32)
    vfix_one = 1.0 - jnp.power(f32(beta_first), vec_step)
    vfix_two = 1.0 - jnp.power(f32(beta_second), vec_step)
    vec_one = beta_first * vector_first + (1.0 - beta_first) * grad_vectors
    vec_two = beta_second * vector_second + (1.0 - beta_second) * grad_vectors * grad_vectors
    vec_new = vector_params - rate_vector * adam_direction(vec_one, vec_two, vfix_one, vfix_two)
    vector_state = jnp.stack([vec_new, vec_one, vec_two])
    return (
        node_output,
        edge_output,
        node_gradient,
        edge_gradient,
        moment_one,
        moment_two,
        new_weights,
        new_weights.astype(bf16),
        vector_state,
        grad_norm.reshape(1),
    )


def solution(mesh):
    in_specs = (
        P("dp", None, "node", None),
        P("dp", None, "node", None),
        P("dp", None, "node", None),
        P("dp", None, "node", None),
        P("node", None),
        P("node"),
        P("node"),
        P("dp"),
        P(),
        P(),
        P("dp", "node", None),
        P("dp", "node", None),
        P("dp", "node", None),
        P("dp", None, "node"),
        P("dp", None, None),
        P(),
        P(),
        P(),
    )
    out_specs = (
        P("dp", None, "node", None),
        P("dp", None, "node", None),
        P("dp", None, "node", None),
        P("dp", None, "node", None),
        P("dp", "node", None),
        P("dp", "node", None),
        P("dp", "node", None),
        P("dp", "node", None),
        P(),
        P(),
    )
    return jax.shard_map(local, mesh=mesh, in_specs=in_specs, out_specs=out_specs, check_vma=False)
```

```python
import functools
import math

import jax
import jax.numpy as jnp
from jax import lax
from jax.experimental import pallas as pl
from jax.experimental.pallas import tpu as pltpu
from jax.sharding import PartitionSpec as P

NBLOCK = 7
f32 = jnp.float32
bf16 = jnp.bfloat16
highest = lax.Precision.HIGHEST
norm_epsilon = 1e-05
adam_epsilon = 1e-08
beta_first = 0.5
beta_second = 0.5
rate_matrix = 0.03
rate_vector = 0.4
weight_decay = 0.01


def dot(a, b):
    return jnp.dot(a, b, preferred_element_type=f32)


def dot_tb(a, b):
    return lax.dot_general(a, b, (((1,), (1,)), ((), ())), preferred_element_type=f32)


def dot_ta(a, b):
    return lax.dot_general(a, b, (((0,), (0,)), ((), ())), preferred_element_type=f32)


def eights(x):
    return jnp.sum(x.reshape(x.shape[0] // 8, 8, x.shape[1]), axis=0)


def sigmoid(z):
    return 0.5 * jnp.tanh(0.5 * z) + 0.5


def branch_forward(z, w_out, bias_out):
    s = sigmoid(z)
    h = z * s
    slope = s + h * (1.0 - s)
    hidden = h.astype(bf16)
    after = dot(hidden, w_out) + bias_out
    center = after - jnp.mean(after, axis=1, keepdims=True)
    spread = jnp.mean(center * center, axis=1, keepdims=True)
    inverse = lax.rsqrt(spread + norm_epsilon)
    return hidden, slope, center * inverse, inverse


def norm_backward(upstream, normed, inverse, gain):
    u = upstream * gain
    first = jnp.mean(u, axis=1, keepdims=True)
    second = jnp.mean(u * normed, axis=1, keepdims=True)
    return (inverse * (u - first - normed * second)).astype(bf16)


def layer_kernel(
    rollout_ref,
    slot_block_ref,
    node_hbm,
    edge_hbm,
    ncot_hbm,
    ecot_hbm,
    sender_ref,
    receiver_ref,
    halo_ref,
    w_ref,
    vec_ref,
    nout_ref,
    eout_hbm,
    nbase_ref,
    egrad_hbm,
    grad_ref,
    gvec_ref,
    hback_ref,
    node_v,
    edge_v,
    ncot_v,
    ecot_v,
    eout_v,
    egrad_v,
    gather_t,
    gather,
    table,
    hidden_v,
    slope_v,
    normed_v,
    inv_v,
    dz_v,
    da_v,
    summed_v,
    dsum_v,
    sc_own,
    sc_recv,
    sc_halo,
    acc,
    sem_in,
    sem_out,
):
    roll, nodes, width = node_v.shape
    edges = edge_v.shape[1]
    peers, per_peer = sc_halo.shape[0], sc_halo.shape[2]
    halo = peers * per_peer
    known = nodes + halo
    padded = table.shape[1]
    chunk = 256
    pieces = edges // chunk

    copies = []
    for i, (src, dst) in enumerate(
        ((node_hbm, node_v), (edge_hbm, edge_v), (ncot_hbm, ncot_v), (ecot_hbm, ecot_v))
    ):
        copies.append(pltpu.make_async_copy(src.at[0], dst, sem_in.at[i]))
        copies[-1].start()

    slot_of = []
    for b in range(NBLOCK):
        found = jnp.int32(0)
        for s in range(slot_block_ref.shape[0]):
            found = jnp.where(slot_block_ref[s] == b, jnp.int32(s), found)
        slot_of.append(found)

    def weight(b):
        return w_ref[slot_of[b]]

    def live(t):
        return jnp.where(t < rollout_ref[0], 1.0, 0.0).astype(f32)

    ids = lax.broadcasted_iota(jnp.int32, (padded, edges), 0)
    onehot = (ids == sender_ref[...]) | (ids == receiver_ref[...] + known)
    onehot = jnp.where(onehot, 1.0, 0.0).astype(f32)
    gather_t[...] = onehot.astype(bf16)
    gather[...] = onehot.T.astype(bf16)
    table[...] = jnp.zeros_like(table)
    acc[...] = jnp.zeros_like(acc)

    copies[0].wait()
    flat_nodes = node_v[...].reshape(roll * nodes, width)
    own_sent = dot(flat_nodes, weight(1))
    own_recv = dot(flat_nodes, weight(2))
    halo_sent = dot(halo_ref[...], weight(1)).reshape(peers, roll, per_peer, width)
    for t in range(roll):
        table[t, :nodes] = own_sent[t * nodes : (t + 1) * nodes].astype(bf16)
        table[t, nodes:known] = halo_sent[:, t].reshape(halo, width).astype(bf16)
        table[t, known : known + nodes] = own_recv[t * nodes : (t + 1) * nodes].astype(bf16)
    copies[1].wait()

    def forward(t, carry):
        lv = live(t)
        total = jnp.zeros((nodes, width), f32)
        for c in range(pieces):
            rows = pl.ds(c * chunk, chunk)
            edge = edge_v[t, rows]
            z = dot(edge, weight(0)) + dot(gather[rows], table[t]) + vec_ref[0:1]
            hidden, slope, normed, inverse = branch_forward(z, weight(3), vec_ref[1:2])
            hidden_v[t, rows] = hidden
            slope_v[t, rows] = slope.astype(bf16)
            normed_v[t, rows] = normed.astype(bf16)
            inv_v[t, rows] = inverse
            new = edge.astype(f32) + (normed * vec_ref[2:3] + vec_ref[3:4])
            eout_v[t, rows] = (new * lv).astype(bf16)
            total += dot(gather_t[known : known + nodes, rows], new.astype(bf16))
        summed_v[pl.ds(t * nodes, nodes)] = total.astype(bf16)
        pltpu.make_async_copy(eout_v.at[t], eout_hbm.at[0, t], sem_out.at[t]).start()
        return carry

    lax.fori_loop(0, roll, forward, 0)

    flat_nodes = node_v[...].reshape(roll * nodes, width)
    summed = summed_v[...]
    z = dot(flat_nodes, weight(4)) + dot(summed, weight(5)) + vec_ref[4:5]
    hidden, slope, normed, inverse = branch_forward(z, weight(6), vec_ref[5:6])
    row_t = lax.broadcasted_iota(jnp.int32, (roll * nodes, 1), 0) // nodes
    row_live = jnp.where(row_t < rollout_ref[0], 1.0, 0.0).astype(f32)
    new = flat_nodes.astype(f32) + (normed * vec_ref[6:7] + vec_ref[7:8])
    nout_ref[0] = (new * row_live).astype(bf16).reshape(roll, nodes, width)
    copies[2].wait()
    d_new = ncot_v[...].reshape(roll * nodes, width).astype(f32) * row_live
    acc[6] += eights(d_new * normed)
    acc[7] += eights(d_new)
    d_after = norm_backward(d_new, normed, inverse, vec_ref[6:7])
    acc[5] += eights(d_after.astype(f32))
    grad_ref[6] = dot_ta(hidden, d_after)
    d_before = (dot_tb(d_after, weight(6)) * slope).astype(bf16)
    acc[4] += eights(d_before.astype(f32))
    grad_ref[4] = dot_ta(flat_nodes, d_before)
    grad_ref[5] = dot_ta(summed, d_before)
    dsum_v[...] = dot_tb(d_before, weight(5)).astype(bf16)
    nbase_ref[...] = d_new + dot_tb(d_before, weight(4))
    grad_ref[0] = jnp.zeros((width, width), f32)
    grad_ref[3] = jnp.zeros((width, width), f32)
    copies[3].wait()

    def backward(t, carry):
        lv = live(t)
        for c in range(pieces):
            rows = pl.ds(c * chunk, chunk)
            d_new = ecot_v[t, rows].astype(f32) * lv + dot(
                gather[rows, known : known + nodes], dsum_v[pl.ds(t * nodes, nodes)]
            )
            normed = normed_v[t, rows].astype(f32)
            acc[2] += eights(d_new * normed)
            acc[3] += eights(d_new)
            d_after = norm_backward(d_new, normed, inv_v[t, rows], vec_ref[2:3])
            acc[1] += eights(d_after.astype(f32))
            da_v[rows] = d_after
            d_before = (dot_tb(d_after, weight(3)) * slope_v[t, rows].astype(f32)).astype(bf16)
            acc[0] += eights(d_before.astype(f32))
            dz_v[rows] = d_before
            egrad_v[t, rows] = (d_new + dot_tb(d_before, weight(0))).astype(bf16)
        pltpu.make_async_copy(egrad_v.at[t], egrad_hbm.at[0, t], sem_out.at[roll + t]).start()
        grad_ref[3] += dot_ta(hidden_v[t], da_v[...])
        grad_ref[0] += dot_ta(edge_v[t], dz_v[...])
        scattered = dot(gather_t[...], dz_v[...])
        sc_own[pl.ds(t * nodes, nodes)] = scattered[:nodes].astype(bf16)
        sc_recv[pl.ds(t * nodes, nodes)] = scattered[known : known + nodes].astype(bf16)
        sc_halo[:, t] = scattered[nodes:known].reshape(peers, per_peer, width)
        return carry

    lax.fori_loop(0, roll, backward, 0)

    halo_sum = sc_halo[...].reshape(roll * halo, width).astype(bf16)
    grad_ref[1] = dot_ta(flat_nodes, sc_own[...]) + dot_ta(halo_ref[...], halo_sum)
    grad_ref[2] = dot_ta(flat_nodes, sc_recv[...])
    hback_ref[...] = dot_tb(halo_sum, weight(1)).astype(bf16)
    nbase_ref[...] += dot_tb(sc_own[...], weight(1)) + dot_tb(sc_recv[...], weight(2))
    gvec_ref[...] = jnp.sum(acc[...], axis=1)

    for t in range(roll):
        pltpu.make_async_copy(eout_v.at[t], eout_hbm.at[0, t], sem_out.at[t]).wait()
        pltpu.make_async_copy(egrad_v.at[t], egrad_hbm.at[0, t], sem_out.at[roll + t]).wait()


def layer(
    rollout_length,
    slot_block,
    node_state,
    edge_state,
    node_cotangent,
    edge_cotangent,
    edge_sender,
    edge_receiver,
    halo,
    slots,
    vector_params,
    per_peer,
):
    _, roll, nodes, width = node_state.shape
    edges = edge_state.shape[2]
    peers = halo.shape[0] // (roll * per_peer)
    known = nodes + peers * per_peer
    padded = -(-(known + nodes) // 128) * 128
    vmem = pl.BlockSpec(memory_space=pltpu.VMEM)
    smem = pl.BlockSpec(memory_space=pltpu.SMEM)
    hbm = pl.BlockSpec(memory_space=pl.ANY)
    shape = jax.ShapeDtypeStruct
    return pl.pallas_call(
        layer_kernel,
        out_shape=(
            shape(node_state.shape, bf16),
            shape(edge_state.shape, bf16),
            shape((roll * nodes, width), f32),
            shape(edge_state.shape, bf16),
            shape((NBLOCK, width, width), f32),
            shape((8, width), f32),
            shape(halo.shape, bf16),
        ),
        in_specs=[smem, smem, hbm, hbm, hbm, hbm, vmem, vmem, vmem, vmem, vmem],
        out_specs=(vmem, hbm, vmem, hbm, vmem, vmem, vmem),
        scratch_shapes=[
            pltpu.VMEM((roll, nodes, width), bf16),
            pltpu.VMEM((roll, edges, width), bf16),
            pltpu.VMEM((roll, nodes, width), bf16),
            pltpu.VMEM((roll, edges, width), bf16),
            pltpu.VMEM((roll, edges, width), bf16),
            pltpu.VMEM((roll, edges, width), bf16),
            pltpu.VMEM((padded, edges), bf16),
            pltpu.VMEM((edges, padded), bf16),
            pltpu.VMEM((roll, padded, width), bf16),
            pltpu.VMEM((roll, edges, width), bf16),
            pltpu.VMEM((roll, edges, width), bf16),
            pltpu.VMEM((roll, edges, width), bf16),
            pltpu.VMEM((roll, edges, 1), f32),
            pltpu.VMEM((edges, width), bf16),
            pltpu.VMEM((edges, width), bf16),
            pltpu.VMEM((roll * nodes, width), bf16),
            pltpu.VMEM((roll * nodes, width), bf16),
            pltpu.VMEM((roll * nodes, width), bf16),
            pltpu.VMEM((roll * nodes, width), bf16),
            pltpu.VMEM((peers, roll, per_peer, width), f32),
            pltpu.VMEM((8, 8, width), f32),
            pltpu.SemaphoreType.DMA((4,)),
            pltpu.SemaphoreType.DMA((2 * roll,)),
        ],
        compiler_params=pltpu.CompilerParams(vmem_limit_bytes=60 << 20),
        name="layer",
    )(
        rollout_length,
        slot_block,
        node_state,
        edge_state,
        node_cotangent,
        edge_cotangent,
        edge_sender.reshape(1, edges),
        edge_receiver.reshape(1, edges),
        halo,
        slots,
        vector_params,
    )


def adam_direction(moment_one, moment_two, fix_one, fix_two):
    return moment_one / fix_one / (jnp.sqrt(moment_two / fix_two) + adam_epsilon)


MESH = pl.DeviceIdType.MESH


class Place:
    def __init__(self):
        self.z = lax.axis_index("dp")
        self.n = lax.axis_index("node")
        self.c = lax.rem(self.n, 2)
        self.x = lax.rem(self.n // 2, 2)
        self.y = self.n // 4
        self.xn = self.n + 2 - 4 * self.x
        self.yn = self.n + 4 - 8 * self.y
        self.sib = self.n + 1 - 2 * self.c
        self.diag = self.xn + 4 - 8 * self.y


def remote(src, dst, send, recv, z, n):
    return pltpu.make_async_remote_copy(
        src_ref=src, dst_ref=dst, send_sem=send, recv_sem=recv, device_id=(z, n), device_id_type=MESH
    )


def greet_start(p, depth, peers):
    barrier = pltpu.get_barrier_semaphore()
    for k in range(1, peers):
        to = lax.rem(p.n + k, peers)
        pl.semaphore_signal(barrier, inc=1, device_id=(p.z, to), device_id_type=MESH)
    for k in range(1, depth):
        to = lax.rem(p.z + k, depth)
        pl.semaphore_signal(barrier, inc=1, device_id=(to, p.n), device_id_type=MESH)


def greet_end(depth, peers):
    pl.semaphore_wait(pltpu.get_barrier_semaphore(), peers + depth - 2)


ORDER = ((0, 1, 2, 3), (1, 0, 2, 3), (2, 3, 1, 0), (3, 2, 1, 0))


def gather_start(p, buf, k, sems):
    send, recv = sems
    own = buf(k, p.n)
    copies = []
    for i, to in ((0, p.xn), (1, p.yn), (3, p.sib)):
        copies.append(remote(own, own, send.at[i, k], recv.at[i, k], p.z, to))
        copies[-1].start()
    return copies


def gather_side(p, buf, k, sems, over_far=True):
    send, recv = sems
    copies = []
    for i, owner in ((0, p.xn), (1, p.yn)):
        got = buf(k, owner)
        remote(got, got, send.at[i, k], recv.at[i, k], p.z, owner).wait_recv()
        on = remote(got, got, send.at[4 + i, k], recv.at[4 + i, k], p.z, p.sib)
        on.start()
        copies.append(on)
        if over_far:
            over = remote(got, got, send.at[2, k], recv.at[2, k], p.z, p.yn if i == 0 else p.xn)
            pl.when(p.c == i)(over.start)
    if over_far:
        copies.append(over)
    return copies


def gather_far(p, buf, k, sems):
    send, recv = sems
    got = buf(k, p.diag)
    remote(got, got, send.at[2, k], recv.at[2, k], p.z, p.xn).wait_recv()
    on = remote(got, got, send.at[6, k], recv.at[6, k], p.z, p.sib)
    on.start()
    return [on]


def gather_end(p, buf, k, sems):
    send, recv = sems
    for i in (3, 4, 5, 6):
        got = buf(k, p.sib)
        remote(got, got, send.at[i, k], recv.at[i, k], p.z, p.sib).wait_recv()


class Step:
    def __init__(self, **refs):
        self.__dict__.update(refs)


def step_kernel(names, *refs):
    k = Step(**dict(zip(names, refs, strict=True)))
    p = Place()
    depth, peers = 4, 8
    roll, nodes, width = k.node_v.shape
    edges = k.edge_v.shape[1]
    slot_dev, rows = k.weight_v.shape[:2]
    per_peer = k.halo.shape[1] // roll
    halo = peers * per_peer
    known = nodes + halo
    padded = k.table.shape[1]
    chunk = edges
    pieces = edges // chunk
    going = []

    def launch(src, dst, send, recv, z, n):
        copy = remote(src, dst, send, recv, z, n)
        copy.start()
        going.append((copy, None))

    def landed(dst, recv):
        remote(dst, dst, recv, recv, p.z, p.sib).wait_recv()

    loads = []
    for i, (src, dst) in enumerate(
        (
            (k.weight_hbm, k.weight_v),
            (k.node_hbm.at[0], k.node_v),
            (k.left_hbm, k.grad.at[2, :slot_dev]),
            (k.right_hbm, k.grad.at[:slot_dev]),
            (k.edge_hbm.at[0], k.edge_v),
            (k.ncot_hbm.at[0], k.ncot_v),
            (k.ecot_hbm.at[0], k.egrad_v.at[0]),
            (k.first_hbm, k.first_v),
            (k.second_hbm, k.second_v),
        )
    ):
        loads.append(pltpu.make_async_copy(src, dst, k.in_sem.at[i]))
        loads[-1].start()
    greet_start(p, depth, peers)

    cut = rows * 3 // 4

    def shard(j):
        top = cut if j % slot_dev == slot_dev - 1 else rows
        return lambda slot, n: k.slots.at[slot, n // 2, lax.rem(n, 2), :top]

    def rest(slot):
        return k.slots.at[slot, :, p.c, cut:]

    planes = []
    for j in range(depth):
        z_of = 0
        for z in range(depth):
            z_of = z_of + jnp.where(p.z == z, ORDER[z][j], 0)
        planes.append(z_of)

    def along_z(z_of):
        return (
            (0, (z_of <= p.z) & (p.z < depth - 1) & (p.z - z_of < depth - 2), p.z + 1),
            (1, (z_of >= p.z) & (p.z > 0) & (z_of - p.z < depth - 2), p.z - 1),
            (2, (z_of == p.z) & ((p.z == 0) | (p.z == depth - 1)), depth - 1 - p.z),
        )

    def rest_hop(s, i):
        own = k.slots.at[p.z * slot_dev + s, p.n // 2, p.c, cut:]
        to = (p.xn, p.yn, p.diag)[i]
        return remote(own, own, k.b_send.at[i, s], k.b_recv.at[i, s], p.z, to)

    def rest_start(s):
        for i in range(3):
            rest_hop(s, i).start()
            going.append((rest_hop(s, i), None))

    def rest_pass(j, s):
        slot = planes[j] * slot_dev + s
        ref = rest(slot)
        if j == 0:
            for i in range(3):
                rest_hop(s, i).wait_recv()
        else:
            remote(ref, ref, k.bz_send.at[0, slot], k.bz_recv.at[slot], p.z, p.sib).wait_recv()
        for i, test, to in along_z(planes[j]):
            if i == 2 and j:
                continue
            copy = remote(ref, ref, k.bz_send.at[i, slot], k.bz_recv.at[slot], to, p.n)
            pl.when(test)(copy.start)
            going.append((copy, test))
        copy = remote(ref, ref, k.bs_send.at[slot], k.bs_recv.at[slot], p.z, p.sib)
        copy.start()
        going.append((copy, None))

    def rest_end(slot):
        ref = rest(slot)
        remote(ref, ref, k.bs_send.at[slot], k.bs_recv.at[slot], p.z, p.sib).wait_recv()

    wsems = (k.w_send, k.w_recv)
    order = []

    straight = depth * slot_dev - 1

    def arrive(j):
        z_of = planes[j // slot_dev]
        slot = z_of * slot_dev + j % slot_dev
        order.append(slot)
        piece = shard(j)(slot, p.n)
        if j >= slot_dev:
            remote(piece, piece, k.wz_send.at[0, slot], k.wz_recv.at[slot], p.z, p.n).wait_recv()
        for i, test, to in along_z(z_of):
            if i == 2 and j >= slot_dev:
                continue
            copy = remote(piece, piece, k.wz_send.at[i, slot], k.wz_recv.at[slot], to, p.n)
            pl.when(test)(copy.start)
            going.append((copy, test))
        going.extend((copy, None) for copy in gather_start(p, shard(j), slot, wsems))
        if j >= straight:
            launch(piece, piece, k.w_send.at[2, slot], k.w_recv.at[2, slot], p.z, p.diag)

    def side(j):
        going.extend((copy, None) for copy in gather_side(p, shard(j), order[j], wsems, j < straight))

    def far(j):
        going.extend((copy, None) for copy in gather_far(p, shard(j), order[j], wsems))

    loads[0].wait()
    k.slots[pl.ds(slot_dev * p.z, slot_dev), p.n // 2, p.c] = k.weight_v[...].astype(bf16)
    greet_end(depth, peers)

    def rounds(*names):
        for name in names:
            i = int(name[1:])
            if name[0] == "b":
                rest_pass(i // slot_dev, i % slot_dev)
            else:
                {"a": arrive, "s": side, "f": far}[name[0]](i)

    rest_start(slot_dev - 1)
    rounds("a0", "a1")
    loads[1].wait()
    node_ids = lax.broadcasted_iota(jnp.int32, (nodes, halo), 0)
    pick_t = jnp.where(node_ids == k.rows_ref[...], 1.0, 0.0).astype(bf16)
    for t in range(roll):
        k.spread[:, t] = dot_ta(pick_t, k.node_v[t]).reshape(peers, per_peer, width)
    k.hput[...] = k.spread[...].reshape(peers, roll * per_peer, width).astype(bf16)
    k.halo[p.n] = k.hput[p.n]
    rounds("a2", "a3", "s0", "s1")
    loads[2].wait()
    for s in range(slot_dev):
        k.pre[2 * slot_dev + s, p.n] = k.grad[2, s].astype(bf16)
        for m in range(peers):
            k.lput[s, m] = k.grad[2, s, :, m * rows : (m + 1) * rows].astype(bf16)
    k.lgot[:, p.n] = k.lput[:, p.n]
    rounds("a4", "a5", "s2", "s3", "b1", "f0", "f1")
    ids = lax.broadcasted_iota(jnp.int32, (padded, edges), 0)
    onehot = (ids == k.sender_ref[...].reshape(1, edges)) | (
        ids == k.receiver_ref[...].reshape(1, edges) + known
    )
    onehot = jnp.where(onehot, 1.0, 0.0).astype(f32)
    k.gather_t[...] = onehot.astype(bf16)
    rounds("a6", "a7", "s4", "s5", "b3", "f2", "f3")
    k.gather[...] = onehot.T.astype(bf16)
    k.table[:, known + nodes :] = jnp.zeros((roll, padded - known - nodes, width), bf16)
    k.acc[...] = jnp.zeros_like(k.acc)
    rounds("s6", "s7")
    hsent = []
    for i in range(1, peers):
        to = lax.rem(p.n + i, peers)
        hsent.append(remote(k.hput.at[to], k.halo.at[p.n], k.h_send.at[0, i], k.h_recv.at[0, i], p.z, to))
        hsent[-1].start()
    rounds("b5", "f4", "f5", "b7")
    loads[3].wait()
    for s in range(slot_dev):
        k.right_b[s] = k.grad[s].reshape(width, width).astype(bf16)
    rounds("f6", "f7")
    for j, slot in enumerate(order):
        gather_end(p, shard(j), slot, wsems)
        if j % slot_dev == slot_dev - 1:
            rest_end(slot)

    slot_of = []
    for b in range(NBLOCK):
        found = 0
        for s in range(depth * slot_dev):
            found = jnp.where(k.slot_block_ref[s] == b, s, found)
        slot_of.append(found)

    def weight(b):
        return k.slots[slot_of[b]].reshape(width, width)

    rollout = k.rollout_ref[0]
    vec = k.vec_ref

    def live(t):
        return jnp.where(t < rollout, 1.0, 0.0).astype(f32)

    def flat_nodes():
        return k.node_v[...].reshape(roll * nodes, width)

    own_sent = dot(flat_nodes(), weight(1))
    own_recv = dot(flat_nodes(), weight(2))
    for copy in hsent:
        copy.wait_send()
    for i in range(1, peers):
        landed(k.halo.at[0], k.h_recv.at[0, i])
    halo_flat = k.halo[...].reshape(roll * halo, width)
    halo_sent = dot(halo_flat, weight(1)).reshape(peers, roll, per_peer, width)
    for t in range(roll):
        k.table[t, :nodes] = own_sent[t * nodes : (t + 1) * nodes].astype(bf16)
        k.table[t, nodes:known] = halo_sent[:, t].reshape(halo, width).astype(bf16)
        k.table[t, known : known + nodes] = own_recv[t * nodes : (t + 1) * nodes].astype(bf16)
    loads[4].wait()

    for i in range(1, peers):
        to = lax.rem(p.n + i, peers)
        launch(k.lput.at[:, to], k.lgot.at[:, p.n], k.l_send.at[i], k.l_recv.at[i], p.z, to)
    loads[7].wait()
    loads[8].wait()
    psems = (k.p_send, k.p_recv)
    early = range(3 * slot_dev)
    pbuf = lambda i, n: k.pre.at[i, n]
    for s in range(slot_dev):
        k.pre[s, p.n] = k.first_v[s].astype(bf16)
        k.pre[slot_dev + s, p.n] = k.second_v[s].astype(bf16)
    for i in early:
        going.extend((copy, None) for copy in gather_start(p, pbuf, i, psems))

    def forward(t, carry):
        lv = live(t)
        total = jnp.zeros((nodes, width), f32)
        for c in range(pieces):
            at = pl.ds(c * chunk, chunk)
            edge = k.edge_v[t, at]
            z = dot(edge, weight(0)) + dot(k.gather[at], k.table[t]) + vec[0:1]
            hidden, slope, normed, inverse = branch_forward(z, weight(3), vec[1:2])
            k.hidden_v[t, at] = hidden
            k.slope_v[t, at] = slope.astype(bf16)
            k.normed_v[t, at] = normed.astype(bf16)
            k.inv_v[t, at] = inverse
            new = edge.astype(f32) + (normed * vec[2:3] + vec[3:4])
            k.eout_v[0, t, at] = (new * lv).astype(bf16)
            total += dot(k.gather_t[known : known + nodes, at], new.astype(bf16))
        k.summed_v[pl.ds(t * nodes, nodes)] = total.astype(bf16)
        return carry

    for t in range(roll):
        forward(t, 0)

    on_f = jnp.where(p.c == 0, p.x, p.y)
    on_g = jnp.where(p.c == 0, p.y, p.x)
    to_f = jnp.where(p.c == 0, p.xn, p.yn)
    to_g = jnp.where(p.c == 0, p.yn, p.xn)

    def spot(f, g):
        return jnp.where(p.c == 0, g * 2 + f, f * 2 + g)

    def hop(stage, b):
        put, got, to = (
            (k.cast, k.got_core, p.sib),
            (k.put_one, k.got_one, to_f),
            (k.put_two, k.got_two, to_g),
        )[stage]
        at = stage * NBLOCK + b
        return remote(put.at[b], got.at[b], k.r_send.at[at], k.r_recv.at[at], p.z, to)

    def to_core(b):
        for i in range(peers // 2):
            k.cast[b, i] = k.grad[b, 2 * i + 1 - p.c].astype(bf16)
        hop(0, b).start()

    def to_first(b):
        hop(0, b).wait_recv()
        for g in range(2):
            at = spot(1 - on_f, g)
            k.put_one[b, g] = (k.grad[b, 2 * at + p.c] + k.got_core[b, at].astype(f32)).astype(bf16)
        hop(1, b).start()
        for g in range(2):
            at = spot(on_f, g)
            k.grad[b, 2 * at + p.c] = k.grad[b, 2 * at + p.c] + k.got_core[b, at].astype(f32)

    def to_second(b):
        hop(1, b).wait_recv()
        at = spot(on_f, 1 - on_g)
        total = k.grad[b, 2 * at + p.c] + k.got_one[b, 1 - on_g].astype(f32)
        k.put_two[b] = total.astype(bf16)
        hop(2, b).start()
        k.grad[b, p.n] = k.grad[b, p.n] + k.got_one[b, on_g].astype(f32)

    def settle(b):
        hop(2, b).wait_recv()
        k.grad[b, p.n] = k.grad[b, p.n] + k.got_two[b].astype(f32)

    def put_grad(b, value):
        k.grad[b] = value.reshape(peers, rows, width)

    summed = k.summed_v[...]
    z = dot(flat_nodes(), weight(4)) + dot(summed, weight(5)) + vec[4:5]
    hidden, slope, normed, inverse = branch_forward(z, weight(6), vec[5:6])
    row_t = lax.broadcasted_iota(jnp.int32, (roll * nodes, 1), 0) // nodes
    row_live = jnp.where(row_t < rollout, 1.0, 0.0).astype(f32)
    new = flat_nodes().astype(f32) + (normed * vec[6:7] + vec[7:8])
    k.nout_v[0] = (new * row_live).astype(bf16).reshape(roll, nodes, width)
    loads[5].wait()
    d_new = k.ncot_v[...].reshape(roll * nodes, width).astype(f32) * row_live
    k.acc[6] = eights(d_new * normed)
    k.acc[7] = eights(d_new)
    d_after = norm_backward(d_new, normed, inverse, vec[6:7])
    k.acc[5] = eights(d_after.astype(f32))
    put_grad(6, dot_ta(hidden, d_after))
    to_core(6)
    d_before = (dot_tb(d_after, weight(6)) * slope).astype(bf16)
    k.acc[4] = eights(d_before.astype(f32))
    put_grad(4, dot_ta(flat_nodes(), d_before))
    to_core(4)
    put_grad(5, dot_ta(summed, d_before))
    to_core(5)
    k.summed_v[...] = dot_tb(d_before, weight(5)).astype(bf16)
    k.table[:, 2 * nodes : 3 * nodes] = d_before.reshape(roll, nodes, width)
    for i in early:
        going.extend((copy, None) for copy in gather_side(p, pbuf, i, psems))
    k.grad[0] = jnp.zeros((peers, rows, width), f32)
    k.grad[3] = jnp.zeros((peers, rows, width), f32)
    loads[6].wait()

    def backward(t, carry):
        lv = live(t)
        for c in range(pieces):
            at = pl.ds(c * chunk, chunk)
            d_new = k.egrad_v[0, t, at].astype(f32) * lv + dot(
                k.gather[at, known : known + nodes], k.summed_v[pl.ds(t * nodes, nodes)]
            )
            k.egrad_v[0, t, at] = d_new.astype(bf16)
            normed = k.normed_v[t, at].astype(f32)
            k.acc[2] += eights(d_new * normed)
            k.acc[3] += eights(d_new)
            d_after = norm_backward(d_new, normed, k.inv_v[t, at], vec[2:3])
            k.acc[1] += eights(d_after.astype(f32))
            k.normed_v[t, at] = d_after
            d_before = (dot_tb(d_after, weight(3)) * k.slope_v[t, at].astype(f32)).astype(bf16)
            k.acc[0] += eights(d_before.astype(f32))
            k.slope_v[t, at] = d_before
        k.grad[3] += dot_ta(k.hidden_v[t], k.normed_v[t]).reshape(peers, rows, width)
        k.grad[0] += dot_ta(k.edge_v[t], k.slope_v[t]).reshape(peers, rows, width)
        scattered = dot(k.gather_t[...], k.slope_v[t])
        k.table[t, :nodes] = scattered[:nodes].astype(bf16)
        k.table[t, nodes : 2 * nodes] = scattered[known : known + nodes].astype(bf16)
        k.spread[:, t] = scattered[nodes:known].reshape(peers, per_peer, width)
        for step, work in enumerate((to_first, to_second, settle)):

            @pl.when(t == step)
            def _():
                def one(b, carry):
                    work(b)
                    return carry

                lax.fori_loop(4, NBLOCK, one, 0)

        return carry

    lax.fori_loop(0, roll, backward, 0)

    def kept(i):
        return k.table[:, i * nodes : (i + 1) * nodes].reshape(roll * nodes, width)

    def edge_gradient(t):
        for c in range(pieces):
            at = pl.ds(c * chunk, chunk)
            grown = k.egrad_v[0, t, at].astype(f32) + dot_tb(k.slope_v[t, at], weight(0))
            k.egrad_v[0, t, at] = grown.astype(bf16)

    to_core(3)
    to_core(0)
    k.hput[...] = k.spread[...].reshape(peers, roll * per_peer, width).astype(bf16)
    put_grad(1, dot_ta(flat_nodes(), kept(0)) + dot_ta(halo_flat, k.hput[...].reshape(roll * halo, width)))
    to_core(1)
    to_first(3)
    put_grad(2, dot_ta(flat_nodes(), kept(1)))
    to_core(2)
    to_first(0)
    k.vput[0] = jnp.sum(k.acc[...], axis=1)
    launch(k.vput.at[0], k.vgot.at[0], k.v_send.at[0], k.v_recv.at[0], p.z, p.sib)
    to_first(1)
    to_second(3)
    to_first(2)
    landed(k.vgot.at[0], k.v_recv.at[0])
    k.vput[1] = k.vput[0] + k.vgot[0]
    launch(k.vput.at[1], k.vgot.at[1], k.v_send.at[1], k.v_recv.at[1], p.z, p.xn)
    to_second(0)
    for i in early:
        going.extend((copy, None) for copy in gather_far(p, pbuf, i, psems))
    to_second(1)
    settle(3)
    to_second(2)
    settle(0)
    landed(k.vgot.at[1], k.v_recv.at[1])
    k.vput[2] = k.vput[1] + k.vgot[1]
    launch(k.vput.at[2], k.vgot.at[2], k.v_send.at[2], k.v_recv.at[2], p.z, p.yn)
    for i in range(1, peers):
        to = lax.rem(p.n + i, peers)
        launch(k.hput.at[to], k.hret.at[p.n], k.h_send.at[1, i], k.h_recv.at[1, i], p.z, to)
    k.hret[p.n] = k.hput[p.n]
    settle(1)
    settle(2)

    def part(target, s):
        b = k.slot_block_ref[target * slot_dev + s]
        held = k.grad[jnp.minimum(b, NBLOCK - 1), p.n]
        return jnp.where(b < NBLOCK, held, 0.0)

    last = depth - 1

    def z_hop(way, target, s, to):
        put, got = (k.put_up, k.got_up) if way == 0 else (k.put_down, k.got_down)
        return remote(
            put.at[target, s], got.at[target, s], k.z_send.at[way, target, s], k.z_recv.at[way, target, s], to, p.n
        )

    def far_hop(s):
        return remote(k.put_far.at[s], k.got_far.at[s], k.f_send.at[s], k.f_recv.at[s], last - p.z, p.n)

    def pass_on(way):
        put, got = (k.put_up, k.got_up) if way == 0 else (k.put_down, k.got_down)
        to = p.z + 1 if way == 0 else p.z - 1
        for step in (last, last - 1, 1):
            target = step if way == 0 else last - step
            test = p.z < target if way == 0 else p.z > target
            if step == last:
                end = last if way == 0 else 0
                test = test & (p.z != last - end)
                source = (p.z != last - end) & (p.z != (1 if way == 0 else last - 1))
            else:
                source = p.z > 0 if way == 0 else p.z < last

            @pl.when(test)
            def _():
                for s in range(slot_dev):

                    @pl.when(source)
                    def _():
                        z_hop(way, target, s, to).wait_recv()
                        total = part(target, s) + got[target, s].astype(f32)
                        put[target, s] = total.astype(bf16)

                    @pl.when(jnp.logical_not(source))
                    def _():
                        put[target, s] = part(target, s).astype(bf16)

                    z_hop(way, target, s, to).start()

            if step == last - 1:

                @pl.when(p.z == (0 if way == 0 else last))
                def _():
                    for s in range(slot_dev):
                        k.put_far[s] = part(last - p.z, s).astype(bf16)
                        far_hop(s).start()

    @pl.when(p.z == 0)
    def _():
        pass_on(0)

    @pl.when(p.z == depth - 1)
    def _():
        pass_on(1)

    edge_gradient(0)

    @pl.when(p.z == 1)
    def _():
        pass_on(0)

    @pl.when(p.z == depth - 2)
    def _():
        pass_on(1)

    edge_gradient(1)

    @pl.when(p.z == 1)
    def _():
        pass_on(1)

    @pl.when(p.z == depth - 2)
    def _():
        pass_on(0)

    landed(k.vgot.at[2], k.v_recv.at[2])
    k.vput[3] = k.vput[2] + k.vgot[2]
    k.vz[p.z] = k.vput[3]
    for i in range(1, depth):
        to = lax.rem(p.z + i, depth)
        launch(k.vput.at[3], k.vz.at[p.z], k.v_send.at[2 + i], k.v_recv.at[2 + i], to, p.n)
    edge_gradient(2)
    square = jnp.zeros((8, width), f32)
    gsems = (k.g_send, k.g_recv)
    gbuf = lambda s, n: k.full.at[s, n]
    for s in range(slot_dev):

        @pl.when(p.z > 0)
        def _():
            landed(k.got_up.at[p.z, s], k.z_recv.at[0, p.z, s])

        @pl.when(p.z < depth - 1)
        def _():
            landed(k.got_down.at[p.z, s], k.z_recv.at[1, p.z, s])

        mine = part(p.z, s) + jnp.where(p.z > 0, k.got_up[p.z, s].astype(f32), 0.0)
        mine = mine + jnp.where(p.z < depth - 1, k.got_down[p.z, s].astype(f32), 0.0)

        @pl.when((p.z == 0) | (p.z == last))
        def _():
            far_hop(s).wait_recv()

        mine = mine + jnp.where((p.z == 0) | (p.z == last), k.got_far[s].astype(f32), 0.0)
        k.full[s, p.n] = mine.astype(bf16)
        for copy in gather_start(p, gbuf, s, gsems):
            going.append((copy, None))
        launch(gbuf(s, p.n), gbuf(s, p.n), k.g_send.at[2, s], k.g_recv.at[2, s], p.z, p.diag)
        square = square + eights(mine * mine)
    square = square[:, :128] + square[:, 128:256] + square[:, 256:384] + square[:, 384:]
    k.sput[...] = square
    k.sgot[p.n] = square
    for i in range(1, peers):
        to = lax.rem(p.n + i, peers)
        launch(k.sput, k.sgot.at[p.n], k.n_send.at[i], k.n_recv.at[i], p.z, to)
    edge_gradient(3)

    def collect(buffer, sems, between, finish):
        for s in range(slot_dev):
            going.extend((copy, None) for copy in gather_side(p, buffer, s, sems, False))
        for s in range(slot_dev):
            going.extend((copy, None) for copy in gather_far(p, buffer, s, sems))
        between()
        for s in range(slot_dev):
            gather_end(p, buffer, s, sems)
            finish(s)

    for i in range(1, peers):
        landed(k.sgot.at[0], k.n_recv.at[i])
    k.szput[...] = jnp.sum(k.sgot[...], axis=0)
    k.sz[p.z] = k.szput[...]
    for i in range(1, depth):
        to = lax.rem(p.z + i, depth)
        launch(k.szput, k.sz.at[p.z], k.n_send.at[peers - 1 + i], k.n_recv.at[peers - 1 + i], to, p.n)

    limit = math.sqrt(NBLOCK * width * width + 8 * width)
    found = []

    def fix(beta, step):
        return 1.0 - jnp.exp2(math.log2(beta) * jnp.full((1, 1), step, jnp.int32).astype(f32))

    def norm():
        for i in range(1, depth):
            landed(k.vz.at[0], k.v_recv.at[2 + i])
            landed(k.sz.at[0], k.n_recv.at[peers - 1 + i])
        vectors = k.vz[0] + k.vz[1] + k.vz[2] + k.vz[3]
        square_sum = jnp.sum(k.sz[0] + k.sz[1] + k.sz[2] + k.sz[3], keepdims=True).reshape(1, 1)
        square_sum = square_sum + jnp.sum(vectors * vectors, keepdims=True).reshape(1, 1)
        value = jnp.sqrt(square_sum)
        k.norm_v[...] = jnp.broadcast_to(value, k.norm_v.shape)
        found.extend((vectors, jnp.minimum(1.0, limit / value)))

    def advance(s):
        part_left = dot(k.pre[2 * slot_dev + s].reshape(width, width), k.full[s].reshape(width, width))
        rotated = dot(part_left.astype(bf16), k.right_b[s])
        if s == 0:
            norm()
        k.grad[s] = rotated.reshape(peers, rows, width)
        step = k.step_ref[p.z * slot_dev + s]
        fix_one, fix_two = fix(beta_first, step), fix(beta_second, step)
        clip = found[1]

        def moments(first, second, turn):
            spun = turn * clip
            return (
                beta_first * first + (1.0 - beta_first) * spun,
                beta_second * second + (1.0 - beta_second) * spun * spun,
            )

        one, two = moments(
            k.pre[s].reshape(width, width).astype(f32),
            k.pre[slot_dev + s].reshape(width, width).astype(f32),
            rotated,
        )
        direction = adam_direction(one, two, fix_one, fix_two).astype(bf16)
        turned = dot_tb(direction, k.right_b[s]).astype(bf16)
        reverted = dot_ta(k.lgot[s].reshape(width, rows), turned)
        new = k.weight_v[s] - rate_matrix * (reverted + weight_decay * k.weight_v[s])
        k.wnew_v[s] = new
        k.wcopy_v[s] = new.astype(bf16)
        one, two = moments(k.first_v[s], k.second_v[s], k.grad[s, p.n])
        k.first_v[s] = one
        k.second_v[s] = two

    for i in range(1, peers):
        landed(k.lgot.at[:, 0], k.l_recv.at[i])
    for i in early:
        gather_end(p, pbuf, i, psems)
    def node_gradient():
        for i in range(1, peers):
            landed(k.hret.at[0], k.h_recv.at[1, i])
        back = k.hret[...].astype(f32).reshape(peers, roll, per_peer, width)
        for t in range(roll):
            rows_t = back[:, t].reshape(halo, width).astype(bf16)
            k.table[t, :nodes] = (k.table[t, :nodes].astype(f32) + dot(pick_t, rows_t)).astype(bf16)
        grown = k.ncot_v[...].reshape(roll * nodes, width).astype(f32) * row_live
        grown = grown + dot_tb(kept(0), weight(1)) + dot_tb(kept(1), weight(2)) + dot_tb(kept(2), weight(4))
        k.ngrad_v[0] = grown.astype(bf16).reshape(roll, nodes, width)

    collect(gbuf, gsems, node_gradient, advance)
    grad_vectors, clip = found
    step = k.step_ref[depth * slot_dev]
    spun = grad_vectors * clip
    one = beta_first * k.vfirst_ref[...] + (1.0 - beta_first) * spun
    two = beta_second * k.vsecond_ref[...] + (1.0 - beta_second) * spun * spun
    k.vstate_v[0] = vec[...] - rate_vector * adam_direction(
        one, two, fix(beta_first, step), fix(beta_second, step)
    )
    k.vstate_v[1] = one
    k.vstate_v[2] = two

    for copy, test in going:
        if test is None:
            copy.wait_send()
        else:
            pl.when(test)(copy.wait_send)
    for b in range(NBLOCK):
        for stage in range(3):
            hop(stage, b).wait_send()
    for way in range(2):
        for step in (last, last - 1, 1):
            target = step if way == 0 else last - step
            test = p.z < target if way == 0 else p.z > target
            if step == last:
                test = test & (p.z != last - target)
            for s in range(slot_dev):
                pl.when(test)(z_hop(way, target, s, lax.rem(p.z + 1, depth)).wait_send)
    for s in range(slot_dev):
        pl.when((p.z == 0) | (p.z == last))(far_hop(s).wait_send)


def store_kernel(*refs):
    count = (len(refs) - 3) // 2
    norm, norm_out, sem = refs[count], refs[-2], refs[-1]
    copies = []
    for i in range(count):
        copies.append(pltpu.make_async_copy(refs[i], refs[count + 1 + i], sem.at[i]))
        copies[-1].start()
    norm_out[0] = norm[0, 0]
    for copy in copies:
        copy.wait()


def whole_step(
    node_state,
    edge_state,
    node_cotangent,
    edge_cotangent,
    send_rows,
    edge_sender,
    edge_receiver,
    rollout_length,
    slot_block,
    step_count,
    weight_slots,
    moment_first,
    moment_second,
    basis_left,
    basis_right,
    vector_params,
    vector_first,
    vector_second,
):
    depth, peers = 4, 8
    _, roll, nodes, width = node_state.shape
    edges = edge_state.shape[2]
    slot_dev, rows = weight_slots.shape[:2]
    halo = send_rows.shape[1]
    per_peer = halo // peers
    padded = -(-(2 * nodes + halo) // 128) * 128
    own = (slot_dev, rows, width)
    tile = (8, 128)
    hbm = pl.BlockSpec(memory_space=pl.ANY)
    vmem = pl.BlockSpec(memory_space=pltpu.VMEM)
    smem = pl.BlockSpec(memory_space=pltpu.SMEM)
    shape = jax.ShapeDtypeStruct
    dma = pltpu.SemaphoreType.DMA
    ins = dict(
        rollout_ref=(rollout_length, smem),
        slot_block_ref=(slot_block, smem),
        step_ref=(step_count, smem),
        node_hbm=(node_state, hbm),
        edge_hbm=(edge_state, hbm),
        ncot_hbm=(node_cotangent, hbm),
        ecot_hbm=(edge_cotangent, hbm),
        rows_ref=(send_rows, vmem),
        sender_ref=(edge_sender, vmem),
        receiver_ref=(edge_receiver, vmem),
        weight_hbm=(weight_slots, hbm),
        first_hbm=(moment_first, hbm),
        second_hbm=(moment_second, hbm),
        left_hbm=(jnp.swapaxes(basis_left, 1, 2), hbm),
        right_hbm=(basis_right.reshape(slot_dev, peers, rows, width), hbm),
        vec_ref=(vector_params, vmem),
        vfirst_ref=(vector_first, vmem),
        vsecond_ref=(vector_second, vmem),
    )
    outs = dict(
        nout_v=shape(node_state.shape, bf16),
        eout_v=shape(edge_state.shape, bf16),
        ngrad_v=shape(node_state.shape, bf16),
        egrad_v=shape(edge_state.shape, bf16),
        first_v=shape(own, f32),
        second_v=shape(own, f32),
        wnew_v=shape(own, f32),
        wcopy_v=shape(own, bf16),
        vstate_v=shape((3, 8, width), f32),
        norm_v=shape(tile, f32),
    )
    v = pltpu.VMEM
    scratch = dict(
        weight_v=v(own, f32),
        node_v=v((roll, nodes, width), bf16),
        edge_v=v((roll, edges, width), bf16),
        ncot_v=v((roll, nodes, width), bf16),
        slots=v((slot_dev * depth, peers // 2, 2, rows, width), bf16),
        halo=v((peers, roll * per_peer, width), bf16),
        spread=v((peers, roll, per_peer, width), f32),
        hput=v((peers, roll * per_peer, width), bf16),
        hret=v((peers, roll * per_peer, width), bf16),
        pre=v((3 * slot_dev, peers, rows, width), bf16),
        lput=v((slot_dev, peers, rows, rows), bf16),
        lgot=v((slot_dev, peers, rows, rows), bf16),
        right_b=v((slot_dev, width, width), bf16),
        gather_t=v((padded, edges), bf16),
        gather=v((edges, padded), bf16),
        table=v((roll, padded, width), bf16),
        hidden_v=v((roll, edges, width), bf16),
        slope_v=v((roll, edges, width), bf16),
        normed_v=v((roll, edges, width), bf16),
        inv_v=v((roll, edges, 1), f32),
        summed_v=v((roll * nodes, width), bf16),
        acc=v((8, 8, width), f32),
        grad=v((NBLOCK, peers, rows, width), f32),
        cast=v((NBLOCK, peers // 2, rows, width), bf16),
        got_core=v((NBLOCK, peers // 2, rows, width), bf16),
        put_one=v((NBLOCK, 2, rows, width), bf16),
        got_one=v((NBLOCK, 2, rows, width), bf16),
        put_two=v((NBLOCK, rows, width), bf16),
        got_two=v((NBLOCK, rows, width), bf16),
        put_up=v((depth, *own), bf16),
        put_down=v((depth, *own), bf16),
        got_up=v((depth, *own), bf16),
        got_down=v((depth, *own), bf16),
        put_far=v(own, bf16),
        got_far=v(own, bf16),
        full=v((slot_dev, peers, rows, width), bf16),
        vput=v((4, 8, width), f32),
        vgot=v((3, 8, width), f32),
        vz=v((depth, 8, width), f32),
        sput=v(tile, f32),
        sgot=v((peers, *tile), f32),
        szput=v(tile, f32),
        sz=v((depth, *tile), f32),
        in_sem=dma((9,)),
        w_send=dma((7, depth * slot_dev)),
        w_recv=dma((7, depth * slot_dev)),
        wz_send=dma((3, depth * slot_dev)),
        wz_recv=dma((depth * slot_dev,)),
        b_send=dma((3, slot_dev)),
        b_recv=dma((3, slot_dev)),
        bz_send=dma((3, depth * slot_dev)),
        bz_recv=dma((depth * slot_dev,)),
        bs_send=dma((depth * slot_dev,)),
        bs_recv=dma((depth * slot_dev,)),
        h_send=dma((2, peers)),
        h_recv=dma((2, peers)),
        l_send=dma((peers,)),
        l_recv=dma((peers,)),
        r_send=dma((3 * NBLOCK,)),
        r_recv=dma((3 * NBLOCK,)),
        z_send=dma((2, depth, slot_dev)),
        z_recv=dma((2, depth, slot_dev)),
        f_send=dma((slot_dev,)),
        f_recv=dma((slot_dev,)),
        g_send=dma((7, slot_dev)),
        g_recv=dma((7, slot_dev)),
        p_send=dma((7, 3 * slot_dev)),
        p_recv=dma((7, 3 * slot_dev)),
        v_send=dma((6,)),
        v_recv=dma((6,)),
        n_send=dma((peers + depth - 1,)),
        n_recv=dma((peers + depth - 1,)),
    )
    names = (*ins, *outs, *scratch)
    results = pl.pallas_call(
        functools.partial(step_kernel, names),
        out_shape=tuple(pltpu.VMEM(out.shape, out.dtype) for out in outs.values()),
        in_specs=[spec for _, spec in ins.values()],
        out_specs=(vmem,) * len(outs),
        scratch_shapes=list(scratch.values()),
        compiler_params=pltpu.CompilerParams(
            vmem_limit_bytes=52 << 20, collective_id=0, has_side_effects=True
        ),
        name="step",
    )(
        *(
            pltpu.with_memory_space_constraint(value, pltpu.HBM) if spec is hbm else value
            for value, spec in ins.values()
        )
    )
    final = [*outs.values()][:-1]
    return pl.pallas_call(
        store_kernel,
        out_shape=(*final, shape((1,), f32)),
        in_specs=[vmem] * len(outs),
        out_specs=(*([hbm] * len(final)), smem),
        scratch_shapes=[dma((len(final),))],
        compiler_params=pltpu.CompilerParams(vmem_limit_bytes=40 << 20),
        name="results",
    )(*results)


def local(
    node_state,
    edge_state,
    node_cotangent,
    edge_cotangent,
    send_rows,
    edge_sender,
    edge_receiver,
    rollout_length,
    slot_block,
    step_count,
    weight_slots,
    moment_first,
    moment_second,
    basis_left,
    basis_right,
    vector_params,
    vector_first,
    vector_second,
):
    width = node_state.shape[-1]
    roll, nodes = node_state.shape[1:3]
    clip_limit = math.sqrt(NBLOCK * width * width + 8 * width)
    slot_dev = weight_slots.shape[0]
    slot_total = slot_block.shape[0]
    halo_rows = send_rows.shape[1]
    peers = lax.axis_size("node")
    per_peer = halo_rows // peers
    if (lax.axis_size("dp"), peers) == (4, 8):
        return whole_step(
            node_state,
            edge_state,
            node_cotangent,
            edge_cotangent,
            send_rows,
            edge_sender,
            edge_receiver,
            rollout_length,
            slot_block,
            step_count,
            weight_slots,
            moment_first,
            moment_second,
            basis_left,
            basis_right,
            vector_params,
            vector_first,
            vector_second,
        )
    copies = lax.all_gather(weight_slots.astype(bf16), "node", axis=1, tiled=True)
    slots = lax.all_gather(copies, "dp", axis=0, tiled=True)
    back_onehot = (send_rows[0][:, None] == jnp.arange(nodes, dtype=jnp.int32)[None, :]).astype(bf16)
    outgoing = jnp.einsum("hk,tkd->htd", back_onehot, node_state[0], preferred_element_type=f32)
    outgoing = outgoing.astype(bf16).reshape(peers, per_peer, roll, width).transpose(0, 2, 1, 3)
    outgoing = outgoing.reshape(peers * roll * per_peer, width)
    halo = lax.all_to_all(outgoing, "node", split_axis=0, concat_axis=0, tiled=True)

    node_output, edge_output, node_base, edge_gradient, grads, grad_vectors, halo_back = layer(
        rollout_length,
        slot_block,
        node_state,
        edge_state,
        node_cotangent,
        edge_cotangent,
        edge_sender,
        edge_receiver,
        halo,
        slots,
        vector_params,
        per_peer,
    )
    returned = lax.all_to_all(halo_back, "node", split_axis=0, concat_axis=0, tiled=True)
    returned = returned.reshape(peers, roll, per_peer, width).transpose(0, 2, 1, 3)
    d_back = jnp.einsum(
        "hk,htd->tkd",
        back_onehot,
        returned.reshape(halo_rows, roll, width),
        preferred_element_type=f32,
    )
    node_gradient = node_base.reshape(roll, nodes, width) + d_back
    node_gradient = node_gradient.astype(bf16).reshape(node_state.shape)

    block_of_slot = slot_block[None, :] == jnp.arange(NBLOCK, dtype=jnp.int32)[:, None]
    first = lax.axis_index("dp") * slot_dev
    summed, grad_vectors = lax.psum((grads, grad_vectors), ("dp", "node"))
    own_square = jnp.sum(summed * summed)
    mine = lax.dynamic_slice_in_dim(block_of_slot.astype(f32), first, slot_dev, 1)
    owned_grads = jnp.einsum("bs,bij->sij", mine, summed, precision=highest)
    square_sum = own_square + jnp.sum(grad_vectors * grad_vectors)
    grad_norm = jnp.sqrt(square_sum)
    clip_scale = jnp.minimum(1.0, clip_limit / grad_norm)
    owned_grads = owned_grads * clip_scale
    grad_vectors = grad_vectors * clip_scale
    own_steps = lax.dynamic_slice_in_dim(step_count, first, slot_dev, 0)
    slot_steps = own_steps.astype(f32)[:, None, None]
    fix_one = 1.0 - jnp.power(f32(beta_first), slot_steps)
    fix_two = 1.0 - jnp.power(f32(beta_second), slot_steps)
    rotated = jnp.einsum("sij,sik->sjk", basis_left, owned_grads, precision=highest, preferred_element_type=f32)
    rotated = jnp.einsum("sjk,skl->sjl", rotated, basis_right, precision=highest, preferred_element_type=f32)
    moment_one = beta_first * moment_first + (1.0 - beta_first) * rotated
    moment_two = beta_second * moment_second + (1.0 - beta_second) * rotated * rotated
    direction = adam_direction(moment_one, moment_two, fix_one, fix_two)
    turned = jnp.einsum("sjl,sml->sjm", direction, basis_right, precision=highest, preferred_element_type=f32)
    reverted = jnp.einsum("sij,sjm->ism", basis_left, turned, precision=highest, preferred_element_type=f32)
    reverted = lax.psum_scatter(reverted.astype(bf16), "node", scatter_dimension=0, tiled=True).astype(f32)
    reverted = jnp.transpose(reverted, (1, 0, 2))
    new_weights = weight_slots - rate_matrix * (reverted + weight_decay * weight_slots)
    vec_step = step_count[slot_total].astype(f32)
    vfix_one = 1.0 - jnp.power(f32(beta_first), vec_step)
    vfix_two = 1.0 - jnp.power(f32(beta_second), vec_step)
    vec_one = beta_first * vector_first + (1.0 - beta_first) * grad_vectors
    vec_two = beta_second * vector_second + (1.0 - beta_second) * grad_vectors * grad_vectors
    vec_new = vector_params - rate_vector * adam_direction(vec_one, vec_two, vfix_one, vfix_two)
    vector_state = jnp.stack([vec_new, vec_one, vec_two])
    return (
        node_output,
        edge_output,
        node_gradient,
        edge_gradient,
        moment_one,
        moment_two,
        new_weights,
        new_weights.astype(bf16),
        vector_state,
        grad_norm.reshape(1),
    )


def solution(mesh):
    in_specs = (
        P("dp", None, "node", None),
        P("dp", None, "node", None),
        P("dp", None, "node", None),
        P("dp", None, "node", None),
        P("node", None),
        P("node"),
        P("node"),
        P("dp"),
        P(),
        P(),
        P("dp", "node", None),
        P("dp", "node", None),
        P("dp", "node", None),
        P("dp", None, "node"),
        P("dp", None, None),
        P(),
        P(),
        P(),
    )
    out_specs = (
        P("dp", None, "node", None),
        P("dp", None, "node", None),
        P("dp", None, "node", None),
        P("dp", None, "node", None),
        P("dp", "node", None),
        P("dp", "node", None),
        P("dp", "node", None),
        P("dp", "node", None),
        P(),
        P(),
    )
    return jax.shard_map(local, mesh=mesh, in_specs=in_specs, out_specs=out_specs, check_vma=False)
```
